128 devices in a mesh: gs: 16 (over z, y), img: 8 (over x, core).
Axes of the slice: x: 4, y: 4, z: 4, core: 2. Of those that a mesh axis runs over, the one named last changes fastest.
Arguments:
- gaussians: float32 [59, 655360], P(None, ('gs', 'img')), may hold values from -6 to 4096, as said below
- send_slots: int32 [128, 10240], P(('gs', 'img')), may hold values from 0 to 5119, as said below
- tile_lists: int32 [64, 256, 512], P('img', 'gs'), may hold values from -1 to 10239, as said below
- truth: float32 [3, 1024, 4096], P(None, 'img', 'gs'), may hold values from 0 to 1
Outputs:
- rendered: float32 [3, 1024, 4096], P(None, 'img', 'gs')
- pixel_loss: float32 [1024, 4096], P('img', 'gs')
The draws below stay inside these ranges and needn't reach their ends.
Inputs may be any that keep to these rules, and one draw needn't show every extreme that they name: `gaussians`: rows 0 and 1 are pixel positions, row 2 a depth of 10 to 60, rows 3 to 5 log scales, rows 6 to 9 a quaternion whose first component is at least 0.5, row 10 an opacity logit, rows 11 to 58 colour harmonics, 16 for each channel. `send_slots`: row s lists, for each destination device in order, 80 indices of source s's own Gaussians. `tile_lists`: live entries (0 or more) name distinct slots of the owning device's received Gaussians and come first, ordered by increasing depth (row 2) of the Gaussians they name; the rest are -1.
All inputs are finite; a program needn't handle non-finite values.
Results may differ from the reference program's by a relative error of at most 0.0003.
Values sent between devices are 32-bit elements; how exact they have to be, the bound alone decides.
A program may use at most 64 MiB of HBM per device.

```python
import math
import jax
import jax.numpy as jnp
from jax import lax

TILE = 16
LIST = 512
TC = 16
TR = 8
HOME = 40
G_DEV = 5120
CAP = 80
SLOTS = 10240
HEIGHT = 1024
WIDTH = 4096
N_GS = 16
N_IMG = 8
DEVICES = 128


def home_perms(key):
    subkeys = jax.random.split(jax.random.fold_in(key, 7), DEVICES)

    def shuffle(subkey):
        return jax.random.permutation(subkey, G_DEV)
    return jax.vmap(shuffle)(subkeys).astype(jnp.int32)


def column_fields(key):
    permuted = home_perms(key)
    home_ids = (jnp.argsort(permuted, axis=1) // HOME).reshape(DEVICES * G_DEV).astype(jnp.int32)
    amount = DEVICES * G_DEV
    subkeys = jax.random.split(jax.random.fold_in(key, 5), 4)
    place_x = home_ids // N_IMG * (TILE * TC) + jax.random.randint(subkeys[0], (amount,), 0, TILE * TC)
    place_y = home_ids % N_IMG * (TILE * TR) + jax.random.randint(subkeys[1], (amount,), 0, TILE * TR)
    size_class = jax.random.randint(subkeys[2], (amount,), 0, 5)
    depth_rank = jax.random.permutation(subkeys[3], amount).astype(jnp.int32)
    return (place_x.astype(jnp.int32), place_y.astype(jnp.int32), size_class.astype(jnp.int32), depth_rank)


def draw_send_slots(key, part):
    permuted = home_perms(key)
    targets = jnp.arange(DEVICES, dtype=jnp.int32)
    left_ids = (targets // N_IMG - 1) % N_GS * N_IMG + targets % N_IMG
    home_ids = jnp.stack([targets, left_ids], axis=1)
    picked = (home_ids[:, :, None] * HOME + jnp.arange(HOME, dtype=jnp.int32)[None, None, :]).reshape(DEVICES * CAP)
    return permuted[:, picked]


def draw_gaussians(key, part):
    place_x, place_y, size_class, depth_rank = column_fields(key)
    amount = DEVICES * G_DEV
    subkeys = jax.random.split(jax.random.fold_in(key, 3), 9)
    mean_x = place_x.astype(jnp.float32) + jax.random.uniform(subkeys[0], (amount,))
    mean_y = place_y.astype(jnp.float32) + jax.random.uniform(subkeys[1], (amount,))
    mean_z = 10.0 + 50.0 * (depth_rank.astype(jnp.float32) + jax.random.uniform(subkeys[2], (amount,))) / float(amount)
    top = math.log(8.0) + size_class.astype(jnp.float32) * math.log(2.0)
    log_scales = top[None, :] - jax.random.uniform(subkeys[3], (3, amount), minval=0.0, maxval=math.log(2.0))
    quat_w = jax.random.uniform(subkeys[4], (1, amount), minval=0.5, maxval=1.0)
    quat_rest = jax.random.uniform(subkeys[5], (3, amount), minval=-1.0, maxval=1.0)
    logits = jax.random.uniform(subkeys[6], (1, amount), minval=-6.0, maxval=-2.0)
    lowest = 0.5 * jax.random.truncated_normal(subkeys[7], -3.0, 3.0, (3, 1, amount))
    higher = 0.2 * jax.random.truncated_normal(subkeys[8], -3.0, 3.0, (3, 15, amount))
    harmonics = jnp.concatenate([lowest, higher], axis=1).reshape(48, amount)
    return jnp.concatenate([mean_x[None], mean_y[None], mean_z[None], log_scales, quat_w, quat_rest, logits, harmonics], axis=0)


def draw_tile_lists(key, part):
    place_x, place_y, size_class, depth_rank = column_fields(key)
    reach_table = jnp.array([26, 50, 98, 194, 386], dtype=jnp.int32)
    reach = reach_table[size_class]
    send = draw_send_slots(key, part)
    routed = send.reshape(DEVICES, DEVICES, CAP) + (jnp.arange(DEVICES, dtype=jnp.int32) * G_DEV)[:, None, None]
    received = jnp.transpose(routed, (1, 0, 2)).reshape(DEVICES, SLOTS)
    subkeys = jax.random.split(jax.random.fold_in(key, 11), 2)
    tile_rows = TR * N_IMG
    tile_cols = TC * N_GS
    dense = jax.random.randint(subkeys[0], (tile_rows, tile_cols), 0, 8) == 0
    wanted = jnp.where(dense, LIST, jax.random.randint(subkeys[1], (tile_rows, tile_cols), 32, 129)).astype(jnp.int32)
    cols = jnp.arange(tile_cols, dtype=jnp.int32)
    slot_pos = jnp.arange(SLOTS, dtype=jnp.int32)
    position = jnp.arange(LIST, dtype=jnp.int32)

    def one_row(inputs):
        row_number, wanted_row = inputs
        owners = cols // TC * N_IMG + row_number // TR
        columns = received[owners]
        gauss_x = place_x[columns]
        gauss_y = place_y[columns]
        gauss_reach = reach[columns]
        left_x = (cols * TILE)[:, None]
        top_y = row_number * TILE
        gap_x = jnp.maximum(jnp.maximum(left_x - gauss_x, gauss_x - (left_x + TILE)), 0)
        gap_y = jnp.maximum(jnp.maximum(top_y - gauss_y, gauss_y - (top_y + TILE)), 0)
        candidate = (gap_x <= gauss_reach) & (gap_y <= gauss_reach)
        order_key = jnp.where(candidate, depth_rank[columns], DEVICES * G_DEV + slot_pos[None, :])
        order = jnp.argsort(order_key, axis=1, stable=True).astype(jnp.int32)
        if SLOTS >= LIST:
            order = order[:, :LIST]
        else:
            order = jnp.pad(order, ((0, 0), (0, LIST - SLOTS)))
        live_count = jnp.minimum(jnp.sum(candidate.astype(jnp.int32), axis=1), wanted_row)
        return jnp.where(position[None, :] < live_count[:, None], order, -1).astype(jnp.int32)
    return lax.map(one_row, (jnp.arange(tile_rows, dtype=jnp.int32), wanted))


def steps_of(key, shape, pieces, smallest, high):
    loudness = 1.0
    for dim, shards_of in pieces:
        steps = jax.random.uniform(jax.random.fold_in(jax.random.fold_in(key, 6), dim), (shards_of,), jnp.float32, smallest / len(pieces), high / len(pieces))
        loudness = loudness * jnp.repeat(jnp.exp(steps), shape[dim] // shards_of).reshape((-1,) + (1,) * (len(shape) - 1 - dim))
    return loudness


def setup_inputs(seed: int = 0) -> dict:
    key_of = jax.random.split(jax.random.key(seed), 5)
    return {
        "gaussians": draw_gaussians(jax.random.fold_in(key_of[4], 71), 0),
        "send_slots": draw_send_slots(jax.random.fold_in(key_of[4], 71), 0),
        "tile_lists": draw_tile_lists(jax.random.fold_in(key_of[4], 71), 0),
        "truth": jnp.clip(1.0 * jax.random.uniform(key_of[3], (3, HEIGHT, WIDTH), jnp.float32) ** steps_of(key_of[3], (3, HEIGHT, WIDTH), ((1, 8), (2, 16)), -0.2, 0.2), 0.0, 1.0),
    }


coef_zero = 0.28209479177387814
coef_one = 0.4886025119029199
coef_two = [1.0925484305920792, -1.0925484305920792, 0.31539156525252005, -1.0925484305920792, 0.5462742152960396]
coef_three = [-0.5900435899266435, 2.890611442640554, -0.4570457994644658, 0.3731763325901154, -0.4570457994644658, 1.445305721320277, -0.5900435899266435]
camera_z = -3000.0
ssim_share = 0.2
stable_one = 0.0001
stable_two = 0.0009

def project(gauss):
    mean_x, mean_y, mean_z = (gauss[0], gauss[1], gauss[2])
    squared = jnp.exp(2.0 * gauss[3:6])
    rotation = gauss[6:10] / jnp.sqrt(lax.optimization_barrier(jnp.sum(gauss[6:10] * gauss[6:10], axis=0)))
    quat_w, quat_x, quat_y, quat_z = (rotation[0], rotation[1], rotation[2], rotation[3])
    first_a = 1.0 - 2.0 * (quat_y * quat_y + quat_z * quat_z)
    first_b = 2.0 * (quat_x * quat_y - quat_w * quat_z)
    first_c = 2.0 * (quat_x * quat_z + quat_w * quat_y)
    second_a = 2.0 * (quat_x * quat_y + quat_w * quat_z)
    second_b = 1.0 - 2.0 * (quat_x * quat_x + quat_z * quat_z)
    second_c = 2.0 * (quat_y * quat_z - quat_w * quat_x)
    cov_xx = first_a * first_a * squared[0] + first_b * first_b * squared[1] + first_c * first_c * squared[2] + 0.3
    cov_xy = first_a * second_a * squared[0] + first_b * second_b * squared[1] + first_c * second_c * squared[2]
    cov_yy = second_a * second_a * squared[0] + second_b * second_b * squared[1] + second_c * second_c * squared[2] + 0.3
    determinant = cov_xx * cov_yy - cov_xy * cov_xy
    opacity = jax.nn.sigmoid(gauss[10])
    delta_z = mean_z - camera_z
    length = jnp.sqrt(mean_x * mean_x + mean_y * mean_y + delta_z * delta_z)
    dir_x, dir_y, dir_z = (mean_x / length, mean_y / length, delta_z / length)
    sq_x, sq_y, sq_z = (dir_x * dir_x, dir_y * dir_y, dir_z * dir_z)
    prod_xy, prod_yz, prod_xz = (dir_x * dir_y, dir_y * dir_z, dir_x * dir_z)
    harmonic_basis = jnp.stack([coef_zero * jnp.ones_like(dir_x), -coef_one * dir_y, coef_one * dir_z, -coef_one * dir_x, coef_two[0] * prod_xy, coef_two[1] * prod_yz, coef_two[2] * (2.0 * sq_z - sq_x - sq_y), coef_two[3] * prod_xz, coef_two[4] * (sq_x - sq_y), coef_three[0] * dir_y * (3.0 * sq_x - sq_y), coef_three[1] * prod_xy * dir_z, coef_three[2] * dir_y * (4.0 * sq_z - sq_x - sq_y), coef_three[3] * dir_z * (2.0 * sq_z - 3.0 * sq_x - 3.0 * sq_y), coef_three[4] * dir_x * (4.0 * sq_z - sq_x - sq_y), coef_three[5] * dir_z * (sq_x - sq_y), coef_three[6] * dir_x * (sq_x - 3.0 * sq_y)])
    harmonics = gauss[11:59].reshape(3, 16, gauss.shape[1])
    colour = jnp.maximum(lax.optimization_barrier(jnp.sum(harmonics * harmonic_basis[None], axis=1)) + 0.5, 0.0)
    return jnp.stack([mean_x, mean_y, cov_yy / determinant, -cov_xy / determinant, cov_xx / determinant, opacity, colour[0], colour[1], colour[2]])

def splat_alpha(params, live_mask, pix_x, pix_y):
    delta_x = pix_x[:, :, None] - params[0][:, None, :]
    delta_y = pix_y[:, :, None] - params[1][:, None, :]
    power = -0.5 * (params[2][:, None, :] * delta_x * delta_x + params[4][:, None, :] * delta_y * delta_y)
    power = power - params[3][:, None, :] * delta_x * delta_y
    return jnp.where(live_mask[:, None, :], params[5][:, None, :] * jnp.exp(power), 0.0)

def window():
    offsets = jnp.arange(11, dtype=jnp.float32) - 5.0
    weights = jnp.exp(-offsets * offsets / 4.5)
    return weights / jnp.sum(weights)

def loss_from(filtered, rendered, truth):
    mean_r, mean_t = (filtered[0:3], filtered[3:6])
    variance_r = filtered[6:9] - mean_r * mean_r
    variance_t = filtered[9:12] - mean_t * mean_t
    covariance = filtered[12:15] - mean_r * mean_t
    similarity = (2.0 * mean_r * mean_t + stable_one) * (2.0 * covariance + stable_two) / ((mean_r * mean_r + mean_t * mean_t + stable_one) * (variance_r + variance_t + stable_two))
    return (1.0 - ssim_share) * lax.optimization_barrier(jnp.mean(jnp.abs(rendered - truth), axis=0)) + ssim_share * (1.0 - lax.optimization_barrier(jnp.mean(similarity, axis=0)))

def reference(gaussians, send_slots, tile_lists, truth):
    splats = project(gaussians)
    sources = jnp.arange(DEVICES, dtype=jnp.int32)
    routed = send_slots.reshape(DEVICES, DEVICES, CAP) + (sources * G_DEV)[:, None, None]
    slot_ids = jnp.transpose(routed, (1, 0, 2)).reshape(DEVICES, DEVICES * CAP)
    tile_rows, tile_cols = (tile_lists.shape[0], tile_lists.shape[1])
    row_index = jnp.arange(tile_rows, dtype=jnp.int32)
    col_index = jnp.arange(tile_cols, dtype=jnp.int32)
    owners = (col_index // TC)[None, :] * N_IMG + (row_index // TR)[:, None]
    pixels = jnp.arange(TILE * TILE, dtype=jnp.int32)

    def render_row(inputs):
        lists_row, owner_row, row_number = inputs
        live_mask = lists_row >= 0
        chosen = slot_ids[owner_row[:, None], jnp.maximum(lists_row, 0)]
        params = splats[:, chosen]
        pix_x = (col_index[:, None] * TILE + pixels[None, :] % TILE).astype(jnp.float32) + 0.5
        pix_y = jnp.broadcast_to((row_number * TILE + pixels // TILE).astype(jnp.float32) + 0.5, pix_x.shape)
        alphas = splat_alpha(params, live_mask, pix_x, pix_y)
        log_keep = jnp.log1p(-alphas)
        before = jnp.cumsum(log_keep, axis=2) - log_keep
        weight = jnp.exp(before) * alphas
        return jnp.einsum('qpk,cqk->cqp', weight, params[6:9], precision=lax.Precision.HIGHEST)
    colours = lax.map(render_row, (tile_lists, owners, row_index))
    rendered = colours.reshape(tile_rows, 3, tile_cols, TILE, TILE).transpose(1, 0, 3, 2, 4)
    rendered = rendered.reshape(3, tile_rows * TILE, tile_cols * TILE)
    quantities = jnp.concatenate([rendered, truth, rendered * rendered, truth * truth, rendered * truth])
    padded = jnp.pad(quantities, ((0, 0), (5, 5), (5, 5)))
    img_height, img_width = (rendered.shape[1], rendered.shape[2])
    weights = window()
    row_filtered = jnp.zeros((15, img_height, img_width + 10), jnp.float32)
    for offset in range(11):
        row_filtered = row_filtered + weights[offset] * padded[:, offset:offset + img_height, :]
    filtered = jnp.zeros((15, img_height, img_width), jnp.float32)
    for offset in range(11):
        filtered = filtered + weights[offset] * row_filtered[:, :, offset:offset + img_width]
    return (rendered, loss_from(filtered, rendered, truth))
```

```python
import functools
import math

import jax
import jax.numpy as jnp
import numpy as np
from jax import lax
from jax.experimental import pallas as pl
from jax.experimental.pallas import tpu as pltpu
from jax.sharding import PartitionSpec as P

TILE = 16
LANES = 128
CAP = 80
SPLAT = 9
GROUP = 8
STEP = LANES // GROUP
LOG2E = 1.0 / math.log(2.0)
VMEM = pltpu.VMEM


coef_zero = 0.28209479177387814
coef_one = 0.4886025119029199
coef_two = [
    1.0925484305920792,
    -1.0925484305920792,
    0.31539156525252005,
    -1.0925484305920792,
    0.5462742152960396,
]
coef_three = [
    -0.5900435899266435,
    2.890611442640554,
    -0.4570457994644658,
    0.3731763325901154,
    -0.4570457994644658,
    1.445305721320277,
    -0.5900435899266435,
]
camera_z = -3000.0
ssim_share = 0.2
stable_one = 0.0001
stable_two = 0.0009


def extended(value, sides, width):
    for axis, dim in sides:
        size, length = (lax.axis_size(axis), value.shape[dim])
        up = [(i, (i + 1) % size) for i in range(size - 1)]
        down = [(j, i) for i, j in up]
        last = lax.slice_in_dim(value, length - width, length, axis=dim)
        first = lax.slice_in_dim(value, 0, width, axis=dim)
        before = lax.ppermute(last, axis, up)
        after = lax.ppermute(first, axis, down)
        value = jnp.concatenate([before, value, after], axis=dim)
    return value


def window():
    offsets = jnp.arange(11, dtype=jnp.float32) - 5.0
    weights = jnp.exp(-offsets * offsets / 4.5)
    return weights / jnp.sum(weights)


def band_matrix(outputs, inputs_len, sign):
    difference = sign * (
        jnp.arange(inputs_len, dtype=jnp.int32)[None, :]
        - jnp.arange(outputs, dtype=jnp.int32)[:, None]
    )
    offsets = jnp.arange(11, dtype=jnp.int32)
    return jnp.sum(
        jnp.where(difference[:, :, None] == offsets[None, None, :], window()[None, None, :], 0.0),
        axis=2,
    )


def loss_from(filtered, rendered, truth):
    mean_r, mean_t = (filtered[0:3], filtered[3:6])
    variance_r = filtered[6:9] - mean_r * mean_r
    variance_t = filtered[9:12] - mean_t * mean_t
    covariance = filtered[12:15] - mean_r * mean_t
    similarity = (
        (2.0 * mean_r * mean_t + stable_one)
        * (2.0 * covariance + stable_two)
        / (
            (mean_r * mean_r + mean_t * mean_t + stable_one)
            * (variance_r + variance_t + stable_two)
        )
    )
    return (1.0 - ssim_share) * jnp.mean(jnp.abs(rendered - truth), axis=0) + ssim_share * (
        1.0 - jnp.mean(similarity, axis=0)
    )


def project_chunk(gauss):
    row = lambda i: gauss[i : i + 1]
    mean_x, mean_y, mean_z = (row(0), row(1), row(2))
    squared = jnp.exp(2.0 * gauss[3:6])
    sq_0, sq_1, sq_2 = (squared[0:1], squared[1:2], squared[2:3])
    inv = 1.0 / jnp.sqrt(row(6) * row(6) + row(7) * row(7) + row(8) * row(8) + row(9) * row(9))
    quat_w, quat_x, quat_y, quat_z = (row(6) * inv, row(7) * inv, row(8) * inv, row(9) * inv)
    first_a = 1.0 - 2.0 * (quat_y * quat_y + quat_z * quat_z)
    first_b = 2.0 * (quat_x * quat_y - quat_w * quat_z)
    first_c = 2.0 * (quat_x * quat_z + quat_w * quat_y)
    second_a = 2.0 * (quat_x * quat_y + quat_w * quat_z)
    second_b = 1.0 - 2.0 * (quat_x * quat_x + quat_z * quat_z)
    second_c = 2.0 * (quat_y * quat_z - quat_w * quat_x)
    cov_xx = first_a * first_a * sq_0 + first_b * first_b * sq_1 + first_c * first_c * sq_2 + 0.3
    cov_xy = first_a * second_a * sq_0 + first_b * second_b * sq_1 + first_c * second_c * sq_2
    cov_yy = second_a * second_a * sq_0 + second_b * second_b * sq_1 + second_c * second_c * sq_2 + 0.3
    determinant = cov_xx * cov_yy - cov_xy * cov_xy
    opacity = 1.0 / (1.0 + jnp.exp(-row(10)))
    delta_z = mean_z - camera_z
    length = jnp.sqrt(mean_x * mean_x + mean_y * mean_y + delta_z * delta_z)
    dir_x, dir_y, dir_z = (mean_x / length, mean_y / length, delta_z / length)
    sq_x, sq_y, sq_z = (dir_x * dir_x, dir_y * dir_y, dir_z * dir_z)
    prod_xy, prod_yz, prod_xz = (dir_x * dir_y, dir_y * dir_z, dir_x * dir_z)
    basis = jnp.concatenate(
        [
            coef_zero * jnp.ones_like(dir_x),
            -coef_one * dir_y,
            coef_one * dir_z,
            -coef_one * dir_x,
            coef_two[0] * prod_xy,
            coef_two[1] * prod_yz,
            coef_two[2] * (2.0 * sq_z - sq_x - sq_y),
            coef_two[3] * prod_xz,
            coef_two[4] * (sq_x - sq_y),
            coef_three[0] * dir_y * (3.0 * sq_x - sq_y),
            coef_three[1] * prod_xy * dir_z,
            coef_three[2] * dir_y * (4.0 * sq_z - sq_x - sq_y),
            coef_three[3] * dir_z * (2.0 * sq_z - 3.0 * sq_x - 3.0 * sq_y),
            coef_three[4] * dir_x * (4.0 * sq_z - sq_x - sq_y),
            coef_three[5] * dir_z * (sq_x - sq_y),
            coef_three[6] * dir_x * (sq_x - 3.0 * sq_y),
        ],
        axis=0,
    )
    colour = []
    for channel in range(3):
        weights = gauss[11 + 16 * channel : 27 + 16 * channel]
        colour.append(jnp.maximum(jnp.sum(weights * basis, axis=0, keepdims=True) + 0.5, 0.0))
    return [
        mean_x,
        mean_y,
        cov_yy / determinant,
        -cov_xy / determinant,
        cov_xx / determinant,
        opacity,
    ] + colour


def lookup(tables, code, blocks, unroll):
    row = lax.shift_right_arithmetic(code, 7)
    lane = jnp.bitwise_and(code, LANES - 1)

    def one(block, found):
        hit = row == block
        out = []
        for p in range(SPLAT):
            line = jnp.broadcast_to(tables[p, pl.ds(block, 1), :], code.shape)
            taken = jnp.take_along_axis(line, lane, axis=1, mode="promise_in_bounds")
            out.append(jnp.where(hit, taken, found[p]))
        return tuple(out)

    zero = jnp.zeros(code.shape, jnp.float32)
    return lax.fori_loop(0, blocks, one, (zero,) * SPLAT, unroll=unroll)


def outgoing_kernel(gauss_ref, code_ref, out_ref, table):
    blocks = gauss_ref.shape[1] // LANES
    for block in range(blocks):
        rows = project_chunk(gauss_ref[:, block * LANES : (block + 1) * LANES])
        for p in range(SPLAT):
            table[p, block : block + 1, :] = rows[p]

    def dest(i, carry):
        where = pl.ds(pl.multiple_of(i * 8, 8), 8)
        found = lookup(table, code_ref[where, :], blocks, 8)
        for p in range(SPLAT):
            out_ref[p, where, :] = found[p]
        return carry

    lax.fori_loop(0, code_ref.shape[0] // 8, dest, 0)


def outgoing_splats(gaussians, codes):
    devices = codes.shape[0]
    return pl.pallas_call(
        outgoing_kernel,
        out_shape=jax.ShapeDtypeStruct((SPLAT, devices, LANES), jnp.float32),
        in_specs=[pl.BlockSpec(memory_space=VMEM)] * 2,
        out_specs=pl.BlockSpec(memory_space=VMEM),
        scratch_shapes=[VMEM((SPLAT, gaussians.shape[1] // LANES, LANES), jnp.float32)],
        compiler_params=pltpu.CompilerParams(vmem_limit_bytes=32 << 20),
        name="outgoing_splats",
    )(gaussians, codes)


def monomials():
    pixel = np.arange(TILE * TILE)
    x = (pixel % TILE) - 7.5
    y = (pixel // TILE) - 7.5
    rows = np.stack([x * x, y * y, x * y, x, y, np.ones_like(x)])
    return np.concatenate([rows, rows, rows, np.zeros((14, TILE * TILE))]).astype(np.float32)


COEFS = 32


def blend_kernel(groups, counts, starts, order, arrived, codes, centre_x, centre_y, mono, out_ref,
                 table, packed, packed_x, packed_y, coefs, power_a, power_b):
    rows_per_group = codes.shape[1]
    for p in range(SPLAT):
        table[p] = jnp.transpose(arrived[p])[0:CAP]
    for g in range(groups):
        here = pl.ds(starts[g], rows_per_group)
        packed[here, :] = codes[g]
        packed_x[here, :] = jnp.broadcast_to(centre_x[g : g + 1, :], (rows_per_group, LANES))
        packed_y[here, :] = jnp.broadcast_to(centre_y[g : g + 1, :], (rows_per_group, LANES))
    total = starts[groups]
    packed[pl.ds(total, 8), :] = jnp.full((8, LANES), -1, jnp.int32)
    packed_x[pl.ds(total, 8), :] = jnp.zeros((8, LANES), jnp.float32)
    packed_y[pl.ds(total, 8), :] = jnp.zeros((8, LANES), jnp.float32)

    def prepare(i, carry):
        where = pl.ds(pl.multiple_of(i * 8, 8), 8)
        code = packed[where, :]
        m_x, m_y, a, b, c, o, red, green, blue = lookup(table, code, CAP, 8)
        live = code >= 0
        u, v = (m_x - packed_x[where, :], m_y - packed_y[where, :])
        level = LOG2E * (-0.5 * (a * u * u + c * v * v) - b * u * v)
        values = [
            (-0.5 * LOG2E) * a,
            (-0.5 * LOG2E) * c,
            -LOG2E * b,
            LOG2E * (a * u + b * v),
            LOG2E * (c * v + b * u),
            jnp.where(live, level + jnp.log2(o), -1e30),
        ]
        base = i * (8 * COEFS)
        for j, value in enumerate(values):
            for part in range(3):
                rounded = value.astype(jnp.bfloat16).astype(jnp.float32)
                value = value - rounded
                coefs[pl.ds(base + part * 6 + j, 8, stride=COEFS), :] = rounded
        zero = jnp.zeros_like(red)
        for j in range(18, 24):
            coefs[pl.ds(base + j, 8, stride=COEFS), :] = zero
        for j, value in enumerate([red, green, blue, zero, zero, zero, zero, zero]):
            coefs[pl.ds(base + 24 + j, 8, stride=COEFS), :] = value
        return carry

    lax.fori_loop(0, (total + 7) // 8, prepare, 0)

    sub = lax.broadcasted_iota(jnp.int32, (GROUP, LANES), 0)

    def exponents(row):
        left = coefs[pl.ds(pl.multiple_of(row * COEFS, 8), COEFS), :].astype(jnp.bfloat16)
        return lax.dot_general(left, mono[...], (((0,), (0,)), ((), ())), preferred_element_type=jnp.float32)

    def blend(row, power, state):
        left, colour = state[0:2], state[2:8]
        left, colour = list(left), list(colour)
        lines = [
            jnp.broadcast_to(coefs[pl.ds(row * COEFS + 24 + ch, 1), :], (GROUP, LANES)) for ch in range(3)
        ]
        for k in range(STEP):
            tints = [
                jnp.take_along_axis(line, sub + GROUP * k, axis=1, mode="promise_in_bounds") for line in lines
            ]
            for half in range(2):
                alpha = jnp.exp2(power[k * GROUP : (k + 1) * GROUP, half * LANES : (half + 1) * LANES])
                weight = left[half] * alpha
                left[half] = left[half] - weight
                for ch in range(3):
                    colour[ch * 2 + half] = colour[ch * 2 + half] + weight * tints[ch]
        return tuple(left) + tuple(colour)

    ones = jnp.ones((GROUP, LANES), jnp.float32)
    nothing = jnp.zeros((GROUP, LANES), jnp.float32)

    def one_group(g, carry):
        start = starts[g]
        pairs = (counts[g] + 1) // 2

        def two_rows(i, state):
            row = start + 2 * i
            power_b[...] = exponents(row + 1)
            state = blend(row, power_a, state)
            power_a[...] = exponents(row + 2)
            return blend(row + 1, power_b, state)

        power_a[...] = exponents(start)
        state = lax.fori_loop(0, pairs, two_rows, (ones, ones) + (nothing,) * 6)
        for t in range(GROUP):
            tile = order[g * GROUP + t]
            for ch in range(3):
                for half in range(2):
                    place = (ch * 2 + half) * (groups * GROUP) + tile
                    out_ref[pl.ds(place, 1), :] = state[2 + ch * 2 + half][t : t + 1]
        return carry

    lax.fori_loop(0, groups, one_group, 0)


def blend_tiles(counts, starts, order, arrived, codes, centre_x, centre_y):
    groups, rows_per_group = codes.shape[0], codes.shape[1]
    most = groups * rows_per_group + 16
    smem = pl.BlockSpec(memory_space=pltpu.SMEM)
    vmem = pl.BlockSpec(memory_space=VMEM)
    return pl.pallas_call(
        functools.partial(blend_kernel, groups),
        out_shape=jax.ShapeDtypeStruct((6 * groups * GROUP, LANES), jnp.float32),
        in_specs=[smem] * 3 + [vmem] * 5,
        out_specs=vmem,
        scratch_shapes=[
            VMEM((SPLAT, CAP, LANES), jnp.float32),
            VMEM((most, LANES), jnp.int32),
            VMEM((most, LANES), jnp.float32),
            VMEM((most, LANES), jnp.float32),
            VMEM((most * COEFS, LANES), jnp.float32),
            VMEM((LANES, TILE * TILE), jnp.float32),
            VMEM((LANES, TILE * TILE), jnp.float32),
        ],
        compiler_params=pltpu.CompilerParams(vmem_limit_bytes=48 << 20),
        name="blend_tiles",
    )(counts, starts, order, arrived, codes, centre_x, centre_y, jnp.asarray(monomials()).astype(jnp.bfloat16))


def arrange(tile_lists):
    rows_here, cols_here, list_len = tile_lists.shape
    tiles = rows_here * cols_here
    lists = tile_lists.reshape(tiles, list_len)
    live = jnp.sum((lists >= 0).astype(jnp.int32), axis=1)
    number = jnp.arange(tiles, dtype=jnp.int32)
    ahead = (live[None, :] > live[:, None]) | ((live[None, :] == live[:, None]) & (number[None, :] < number[:, None]))
    rank = jnp.sum(ahead.astype(jnp.int32), axis=1)
    hot = rank[None, :] == number[:, None]
    order = jnp.sum(jnp.where(hot, number[None, :], 0), axis=1)
    sorted_live = jnp.sum(jnp.where(hot, live[None, :], 0), axis=1)
    groups = tiles // GROUP
    counts = (jnp.max(sorted_live.reshape(groups, GROUP), axis=1) + STEP - 1) // STEP
    counts = (counts + 1) // 2 * 2
    ends = jnp.sum(jnp.where(jnp.arange(groups)[None, :] <= jnp.arange(groups)[:, None], counts[None, :], 0), axis=1)
    starts = jnp.concatenate([jnp.zeros((1,), jnp.int32), ends.astype(jnp.int32)])
    code = jnp.where(lists >= 0, lists % CAP * LANES + lists // CAP, -1)[order]
    code = code.reshape(groups, GROUP, list_len).transpose(0, 2, 1).reshape(groups, list_len // STEP, LANES)
    tile_row = lax.axis_index("img") * rows_here + order // cols_here
    tile_col = lax.axis_index("gs") * cols_here + order % cols_here
    spread = lambda v: jnp.tile((v * TILE + TILE // 2).astype(jnp.float32).reshape(groups, GROUP), (1, STEP))
    return counts, starts, order, code, spread(tile_col), spread(tile_row)


def on_device(gaussians, send_slots, tile_lists, truth):
    rows_here, cols_here, list_len = tile_lists.shape
    devices = send_slots.shape[1] // CAP
    codes = jnp.pad(send_slots.reshape(devices, CAP), ((0, 0), (0, LANES - CAP)))
    outgoing = outgoing_splats(gaussians, codes)
    arrived = lax.all_to_all(outgoing, ("gs", "img"), split_axis=1, concat_axis=1, tiled=True)
    counts, starts, order, code, centre_x, centre_y = arrange(tile_lists)
    colours = blend_tiles(counts, starts, order, arrived, code, centre_x, centre_y)
    rendered = colours.reshape(3, 2, rows_here, cols_here, TILE // 2, TILE).transpose(0, 2, 1, 4, 3, 5)
    rendered = rendered.reshape(3, rows_here * TILE, cols_here * TILE)
    stacked = jnp.concatenate([rendered, truth])
    padded = extended(stacked, (("gs", 2), ("img", 1)), 5)
    rim_r, rim_t = (padded[0:3], padded[3:6])
    quantities = jnp.concatenate([rim_r, rim_t, rim_r * rim_r, rim_t * rim_t, rim_r * rim_t])
    img_height, img_width = (rendered.shape[1], rendered.shape[2])
    band_rows = band_matrix(img_height, img_height + 10, 1)
    band_cols = band_matrix(img_width, img_width + 10, 1).T
    filtered = jnp.einsum("ij,cjw->ciw", band_rows, quantities, precision=lax.Precision.HIGHEST)
    filtered = jnp.einsum("ciw,wv->civ", filtered, band_cols, precision=lax.Precision.HIGHEST)
    return (rendered, loss_from(filtered, rendered, truth))


def solution(mesh):
    return jax.shard_map(
        on_device,
        mesh=mesh,
        in_specs=(
            P(None, ("gs", "img")),
            P(("gs", "img"), None),
            P("img", "gs", None),
            P(None, "img", "gs"),
        ),
        out_specs=(P(None, "img", "gs"), P("img", "gs")),
        check_vma=False,
    )
```

```python
import functools
import math

import jax
import jax.numpy as jnp
import numpy as np
from jax import lax
from jax.experimental import pallas as pl
from jax.experimental.pallas import tpu as pltpu
from jax.sharding import PartitionSpec as P

TILE = 16
LANES = 128
CAP = 80
SPLAT = 9
LOG2E = 1.0 / math.log(2.0)
VMEM = pltpu.VMEM


coef_zero = 0.28209479177387814
coef_one = 0.4886025119029199
coef_two = [
    1.0925484305920792,
    -1.0925484305920792,
    0.31539156525252005,
    -1.0925484305920792,
    0.5462742152960396,
]
coef_three = [
    -0.5900435899266435,
    2.890611442640554,
    -0.4570457994644658,
    0.3731763325901154,
    -0.4570457994644658,
    1.445305721320277,
    -0.5900435899266435,
]
camera_z = -3000.0
ssim_share = 0.2
stable_one = 0.0001
stable_two = 0.0009


def extended(value, sides, width):
    for axis, dim in sides:
        size, length = (lax.axis_size(axis), value.shape[dim])
        up = [(i, (i + 1) % size) for i in range(size - 1)]
        down = [(j, i) for i, j in up]
        last = lax.slice_in_dim(value, length - width, length, axis=dim)
        first = lax.slice_in_dim(value, 0, width, axis=dim)
        before = lax.ppermute(last, axis, up)
        after = lax.ppermute(first, axis, down)
        value = jnp.concatenate([before, value, after], axis=dim)
    return value


def window():
    offsets = jnp.arange(11, dtype=jnp.float32) - 5.0
    weights = jnp.exp(-offsets * offsets / 4.5)
    return weights / jnp.sum(weights)


def band_matrix(outputs, inputs_len, sign):
    difference = sign * (
        jnp.arange(inputs_len, dtype=jnp.int32)[None, :]
        - jnp.arange(outputs, dtype=jnp.int32)[:, None]
    )
    offsets = jnp.arange(11, dtype=jnp.int32)
    return jnp.sum(
        jnp.where(difference[:, :, None] == offsets[None, None, :], window()[None, None, :], 0.0),
        axis=2,
    )


def loss_from(filtered, rendered, truth):
    mean_r, mean_t = (filtered[0:3], filtered[3:6])
    variance_r = filtered[6:9] - mean_r * mean_r
    variance_t = filtered[9:12] - mean_t * mean_t
    covariance = filtered[12:15] - mean_r * mean_t
    similarity = (
        (2.0 * mean_r * mean_t + stable_one)
        * (2.0 * covariance + stable_two)
        / (
            (mean_r * mean_r + mean_t * mean_t + stable_one)
            * (variance_r + variance_t + stable_two)
        )
    )
    return (1.0 - ssim_share) * jnp.mean(jnp.abs(rendered - truth), axis=0) + ssim_share * (
        1.0 - jnp.mean(similarity, axis=0)
    )


def project_chunk(gauss):
    row = lambda i: gauss[i : i + 1]
    mean_x, mean_y, mean_z = (row(0), row(1), row(2))
    squared = jnp.exp(2.0 * gauss[3:6])
    sq_0, sq_1, sq_2 = (squared[0:1], squared[1:2], squared[2:3])
    inv = 1.0 / jnp.sqrt(row(6) * row(6) + row(7) * row(7) + row(8) * row(8) + row(9) * row(9))
    quat_w, quat_x, quat_y, quat_z = (row(6) * inv, row(7) * inv, row(8) * inv, row(9) * inv)
    first_a = 1.0 - 2.0 * (quat_y * quat_y + quat_z * quat_z)
    first_b = 2.0 * (quat_x * quat_y - quat_w * quat_z)
    first_c = 2.0 * (quat_x * quat_z + quat_w * quat_y)
    second_a = 2.0 * (quat_x * quat_y + quat_w * quat_z)
    second_b = 1.0 - 2.0 * (quat_x * quat_x + quat_z * quat_z)
    second_c = 2.0 * (quat_y * quat_z - quat_w * quat_x)
    cov_xx = first_a * first_a * sq_0 + first_b * first_b * sq_1 + first_c * first_c * sq_2 + 0.3
    cov_xy = first_a * second_a * sq_0 + first_b * second_b * sq_1 + first_c * second_c * sq_2
    cov_yy = second_a * second_a * sq_0 + second_b * second_b * sq_1 + second_c * second_c * sq_2 + 0.3
    determinant = cov_xx * cov_yy - cov_xy * cov_xy
    opacity = 1.0 / (1.0 + jnp.exp(-row(10)))
    delta_z = mean_z - camera_z
    length = jnp.sqrt(mean_x * mean_x + mean_y * mean_y + delta_z * delta_z)
    dir_x, dir_y, dir_z = (mean_x / length, mean_y / length, delta_z / length)
    sq_x, sq_y, sq_z = (dir_x * dir_x, dir_y * dir_y, dir_z * dir_z)
    prod_xy, prod_yz, prod_xz = (dir_x * dir_y, dir_y * dir_z, dir_x * dir_z)
    basis = jnp.concatenate(
        [
            coef_zero * jnp.ones_like(dir_x),
            -coef_one * dir_y,
            coef_one * dir_z,
            -coef_one * dir_x,
            coef_two[0] * prod_xy,
            coef_two[1] * prod_yz,
            coef_two[2] * (2.0 * sq_z - sq_x - sq_y),
            coef_two[3] * prod_xz,
            coef_two[4] * (sq_x - sq_y),
            coef_three[0] * dir_y * (3.0 * sq_x - sq_y),
            coef_three[1] * prod_xy * dir_z,
            coef_three[2] * dir_y * (4.0 * sq_z - sq_x - sq_y),
            coef_three[3] * dir_z * (2.0 * sq_z - 3.0 * sq_x - 3.0 * sq_y),
            coef_three[4] * dir_x * (4.0 * sq_z - sq_x - sq_y),
            coef_three[5] * dir_z * (sq_x - sq_y),
            coef_three[6] * dir_x * (sq_x - 3.0 * sq_y),
        ],
        axis=0,
    )
    colour = []
    for channel in range(3):
        weights = gauss[11 + 16 * channel : 27 + 16 * channel]
        colour.append(jnp.maximum(jnp.sum(weights * basis, axis=0, keepdims=True) + 0.5, 0.0))
    return [
        mean_x,
        mean_y,
        cov_yy / determinant,
        -cov_xy / determinant,
        cov_xx / determinant,
        opacity,
    ] + colour


def lookup(tables, code, blocks, unroll):
    row = lax.shift_right_arithmetic(code, 7)
    lane = jnp.bitwise_and(code, LANES - 1)

    def one(block, found):
        hit = row == block
        out = []
        for p in range(SPLAT):
            line = jnp.broadcast_to(tables[p, pl.ds(block, 1), :], code.shape)
            taken = jnp.take_along_axis(line, lane, axis=1, mode="promise_in_bounds")
            out.append(jnp.where(hit, taken, found[p]))
        return tuple(out)

    zero = jnp.zeros(code.shape, jnp.float32)
    return lax.fori_loop(0, blocks, one, (zero,) * SPLAT, unroll=unroll)


def outgoing_kernel(gauss_ref, code_ref, out_ref, table):
    blocks = gauss_ref.shape[1] // LANES
    for block in range(blocks):
        rows = project_chunk(gauss_ref[:, block * LANES : (block + 1) * LANES])
        for p in range(SPLAT):
            table[p, block : block + 1, :] = rows[p]

    def dest(i, carry):
        where = pl.ds(pl.multiple_of(i * 8, 8), 8)
        found = lookup(table, code_ref[where, :], blocks, 8)
        for p in range(SPLAT):
            out_ref[p, where, :] = found[p]
        return carry

    lax.fori_loop(0, code_ref.shape[0] // 8, dest, 0)


def outgoing_splats(gaussians, codes):
    devices = codes.shape[0]
    return pl.pallas_call(
        outgoing_kernel,
        out_shape=jax.ShapeDtypeStruct((SPLAT, devices, LANES), jnp.float32),
        in_specs=[pl.BlockSpec(memory_space=VMEM)] * 2,
        out_specs=pl.BlockSpec(memory_space=VMEM),
        scratch_shapes=[VMEM((SPLAT, gaussians.shape[1] // LANES, LANES), jnp.float32)],
        compiler_params=pltpu.CompilerParams(vmem_limit_bytes=32 << 20),
        name="outgoing_splats",
    )(gaussians, codes)


SEG = 32
ROWS = 40
BLOCK = 8
COEFS = 32
PIXELS = TILE * TILE
CHUNK = 64


def monomials():
    pixel = np.arange(PIXELS)
    x = (pixel % TILE) - 7.5
    y = (pixel // TILE) - 7.5
    cols = np.stack([x * x, y * y, x * y, x, y, np.ones_like(x)], axis=1)
    return np.concatenate([cols, cols, cols, np.zeros((PIXELS, COEFS - 18))], axis=1).astype(np.float32)


def split(value, parts):
    out = []
    for _ in range(parts):
        rounded = value.astype(jnp.bfloat16)
        out.append(rounded)
        value = value - rounded.astype(jnp.float32)
    return out


def lane_pick(value, index, axis):
    return jnp.take_along_axis(value, index, axis=axis, mode="promise_in_bounds")


def blend_kernel(cols_here, first, base, arrived, lists, owner, mono, out_ref,
                 table_a, table_b, table, packed, codes, params, coefs, power_a, power_b, state, total_ref,
                 carry_ref, carry_owner):
    tiles = first.shape[0] - 1
    runs = lists.shape[0] // tiles
    groups = (first[tiles] + LANES - 1) // LANES
    per_group = SEG // BLOCK

    for p in range(SPLAT):
        flat = jnp.transpose(arrived[p])
        for half, ref in enumerate((table_a, table_b)):
            value = flat[half * ROWS : (half + 1) * ROWS]
            if p < 8:
                ref[pl.ds(p, ROWS, stride=8), :] = value
            else:
                ref[8 * ROWS : 9 * ROWS, :] = value
    for half, ref in enumerate((table_a, table_b)):
        for part, value in enumerate(split(ref[...], 3)):
            table[:, part * 256 + half * LANES : part * 256 + (half + 1) * LANES] = value

    packed[...] = jnp.full(packed.shape, -1, jnp.int32)
    for t in range(tiles):
        packed[pl.ds(first[t], runs), :] = lists[t * runs : (t + 1) * runs, :]

    def turn(g, carry):
        lanes = jnp.transpose(packed[pl.ds(pl.multiple_of(g * LANES, LANES), LANES), :])
        codes[pl.ds(pl.multiple_of(g * SEG, SEG), SEG), :] = lanes[0:SEG]
        return carry

    lax.fori_loop(0, groups, turn, 0)
    total_ref[...] = jnp.zeros_like(total_ref)
    carry_ref[...] = jnp.ones_like(carry_ref)
    carry_owner[...] = jnp.full(carry_owner.shape, -1, jnp.int32)

    column = lax.broadcasted_iota(jnp.int32, (256, 256), 0)
    table_row = lax.broadcasted_iota(jnp.int32, (ROWS, 256), 0)

    def lookup(block, j):
        slot = (block % 3) * 72
        where = block * BLOCK + 2 * j
        code = jnp.concatenate([codes[pl.ds(where, 1), :], codes[pl.ds(where + 1, 1), :]], axis=1)
        col = jnp.bitwise_and(code, 255)
        row = lax.shift_right_arithmetic(code, 8)
        hot = jnp.where(column == col, 1.0, 0.0).astype(jnp.bfloat16)
        found = jnp.dot(table[...], jnp.concatenate([hot, hot, hot], axis=0), preferred_element_type=jnp.float32)
        picked = jnp.zeros((8, 256), jnp.float32)
        rows8 = jnp.broadcast_to(row, (8, 256))
        for r in range(ROWS):
            picked = jnp.where(rows8 == r, found[r * 8 : (r + 1) * 8], picked)
        ninth = jnp.sum(jnp.where(table_row == row, found[8 * ROWS :], 0.0), axis=0, keepdims=True)
        return slot, picked, ninth

    def keep(j, slot, picked, ninth):
        for e in range(2):
            lanes = slice(e * LANES, (e + 1) * LANES)
            params[pl.ds(pl.multiple_of(slot + (2 * j + e) * 8, 8), 8), :] = picked[:, lanes]
            params[pl.ds(slot + 64 + 2 * j + e, 1), :] = ninth[:, lanes]

    def expand(block):
        slot = (block % 3) * 72
        m_x, m_y, a, b, c, o = [params[pl.ds(slot + p, BLOCK, stride=8), :] for p in range(6)]
        live = codes[pl.ds(pl.multiple_of(block * BLOCK, BLOCK), BLOCK), :] >= 0
        tile = owner[pl.ds(block // per_group, 1), :]
        tile_y = lax.shift_right_logical(tile, cols_here.bit_length() - 1)
        tile_x = jnp.bitwise_and(tile, cols_here - 1)
        u = m_x - (tile_x * TILE + base[0]).astype(jnp.float32)
        v = m_y - (tile_y * TILE + base[1]).astype(jnp.float32)
        level = LOG2E * (-0.5 * (a * u * u + c * v * v) - b * u * v)
        values = [
            (-0.5 * LOG2E) * a,
            (-0.5 * LOG2E) * c,
            -LOG2E * b,
            LOG2E * (a * u + b * v),
            LOG2E * (c * v + b * u),
            jnp.where(live, level + jnp.log2(o), -1e30),
        ]
        for i, value in enumerate(values):
            for part, rounded in enumerate(split(value, 3)):
                coefs[pl.ds(part * 6 + i, BLOCK, stride=COEFS), :] = rounded.astype(jnp.float32)

    def exponents(j):
        pair = [
            coefs[pl.ds((2 * j + e) * COEFS, COEFS), :].astype(jnp.bfloat16) for e in range(2)
        ]
        return jnp.dot(mono[...], jnp.concatenate(pair, axis=1), preferred_element_type=jnp.float32)

    def blend(block, j, power):
        slot = (block % 3) * 72
        at = lambda q, i: pl.ds(q * PIXELS + j * CHUNK + i * 8, 8)
        pieces = range(CHUNK // 8)
        left = [state[at(0, i), :] for i in pieces]
        colour = [[state[at(1 + ch, i), :] for i in pieces] for ch in range(3)]
        for k in range(BLOCK):
            rows = (slot + k * 8 + 6, slot + k * 8 + 7, slot + 64 + k)
            tints = [jnp.broadcast_to(params[pl.ds(r, 1), :], (8, LANES)) for r in rows]
            for i in pieces:
                alpha = jnp.exp2(power[k // 2, at(0, i), (k % 2) * LANES : (k % 2 + 1) * LANES])
                weight = left[i] * alpha
                left[i] = left[i] - weight
                for ch in range(3):
                    colour[ch][i] = colour[ch][i] + weight * tints[ch]
        for i in pieces:
            state[at(0, i), :] = left[i]
            for ch in range(3):
                state[at(1 + ch, i), :] = colour[ch][i]

    lane = lax.broadcasted_iota(jnp.int32, (8, LANES), 1)

    def flush(g):
        tile = jnp.broadcast_to(owner[pl.ds(g, 1), :], (8, LANES))
        left = state[0:PIXELS, :]
        same = []
        for d in (1, 2, 4, 8):
            same.append(((pltpu.roll(tile, d, 1) == tile) & (lane >= d))[0:1])
        for d, mask in zip((1, 2, 4, 8), same):
            left = left * jnp.where(mask, pltpu.roll(left, d, 1), 1.0)
        before = jnp.where(same[0], pltpu.roll(left, 1, 1), 1.0)
        goes_on = (tile == carry_owner[...])[0:1]
        behind = jnp.where(goes_on, carry_ref[...], 1.0)
        before = before * behind
        carry_ref[...] = jnp.broadcast_to((left * behind)[:, LANES - 1 :], (PIXELS, LANES))
        carry_owner[...] = jnp.broadcast_to(tile[:, LANES - 1 :], (8, LANES))
        member = lax.broadcasted_iota(jnp.int32, (tiles, LANES), 0) == tile[0:1]
        member = jnp.where(member, 1.0, 0.0).astype(jnp.bfloat16)
        member = jnp.concatenate([member, member], axis=1)
        for ch in range(3):
            part = before * state[(1 + ch) * PIXELS : (2 + ch) * PIXELS, :]
            pair = jnp.concatenate(split(part, 2), axis=1)
            total_ref[ch] += lax.dot_general(
                member, pair, (((1,), (1,)), ((), ())), preferred_element_type=jnp.float32
            )

    coefs[...] = jnp.zeros_like(coefs)
    steps = BLOCK // 2

    def look_ahead(block):
        for j, found in enumerate([lookup(block, j) for j in range(steps)]):
            keep(j, *found)
        expand(block)

    look_ahead(0)
    for j in range(steps):
        power_a[j] = exponents(j)
    look_ahead(1)

    def one_group(g, carry):
        state[0:PIXELS, :] = jnp.ones((PIXELS, LANES), jnp.float32)
        state[PIXELS:, :] = jnp.zeros((3 * PIXELS, LANES), jnp.float32)

        def two_blocks(i, carry):
            for which in range(2):
                block = g * per_group + 2 * i + which
                now, later = ((power_a, power_b), (power_b, power_a))[which]

                found = [lookup(block + 2, j) for j in range(steps)]
                for j in range(steps):
                    later[j] = exponents(j)
                for j in range(steps):
                    blend(block, j, now)
                for j in range(steps):
                    keep(j, *found[j])
                expand(block + 2)
            return carry

        lax.fori_loop(0, per_group // 2, two_blocks, 0)
        flush(g)
        return carry

    lax.fori_loop(0, groups, one_group, 0)

    piece = lax.broadcasted_iota(jnp.int32, (8, LANES), 1)
    inner, outer = piece % TILE, piece // TILE
    sub = lax.broadcasted_iota(jnp.int32, (8, LANES), 0)
    skew = (outer + 8 - sub) % 8 * TILE + inner
    down = (outer + 8 - sub) % 8
    back = (outer + sub) % 8 * TILE + inner
    for ch in range(3):
        for r in range(tiles // cols_here):
            for q in range(cols_here // 8):
                for h in range(2):
                    x = total_ref[ch, r * cols_here + q * 8 : r * cols_here + q * 8 + 8, h * LANES : (h + 1) * LANES]
                    x = lane_pick(lane_pick(lane_pick(x, skew, 1), down, 0), back, 1)
                    out_ref[ch, r * TILE + h * 8 : r * TILE + h * 8 + 8, q * LANES : (q + 1) * LANES] = x


def blend_tiles(first, base, arrived, lists, owner, cols_here):
    tiles = first.shape[0] - 1
    most = lists.shape[0] // LANES
    smem = pl.BlockSpec(memory_space=pltpu.SMEM)
    vmem = pl.BlockSpec(memory_space=VMEM)
    f32 = jnp.float32
    return pl.pallas_call(
        functools.partial(blend_kernel, cols_here),
        out_shape=jax.ShapeDtypeStruct((3, tiles // cols_here * TILE, cols_here * TILE), f32),
        in_specs=[smem] * 2 + [vmem] * 4,
        out_specs=vmem,
        scratch_shapes=[
            VMEM((9 * ROWS, LANES), f32),
            VMEM((9 * ROWS, LANES), f32),
            VMEM((9 * ROWS, 768), jnp.bfloat16),
            VMEM((lists.shape[0] + LANES, LANES), jnp.int32),
            VMEM(((most + 1) * SEG, LANES), jnp.int32),
            VMEM((3 * 72, LANES), f32),
            VMEM((BLOCK * COEFS, LANES), f32),
            VMEM((BLOCK // 2, PIXELS, 256), f32),
            VMEM((BLOCK // 2, PIXELS, 256), f32),
            VMEM((4 * PIXELS, LANES), f32),
            VMEM((3, tiles, PIXELS), f32),
            VMEM((PIXELS, LANES), f32),
            VMEM((8, LANES), jnp.int32),
        ],
        compiler_params=pltpu.CompilerParams(vmem_limit_bytes=48 << 20),
        name="blend_tiles",
    )(first, base, arrived, lists, owner, jnp.asarray(monomials()).astype(jnp.bfloat16))


def arrange(tile_lists):
    rows_here, cols_here, list_len = tile_lists.shape
    tiles = rows_here * cols_here
    lists = tile_lists.reshape(tiles, list_len)
    runs = list_len // SEG
    live = (jnp.sum((lists >= 0).astype(jnp.int32), axis=1) + SEG - 1) // SEG
    number = jnp.arange(tiles, dtype=jnp.int32)
    ends = jnp.sum(jnp.where(number[None, :] <= number[:, None], live[None, :], 0), axis=1).astype(jnp.int32)
    first = jnp.concatenate([jnp.zeros((1,), jnp.int32), ends])
    most = tiles * runs
    segment = jnp.arange(most + LANES, dtype=jnp.int32)
    owner = jnp.sum((ends[None, :] <= segment[:, None]).astype(jnp.int32), axis=1).reshape(-1, LANES)
    slot, source = lists % CAP, lists // CAP
    code = jnp.where(lists >= 0, slot % ROWS * 256 + slot // ROWS * LANES + source, -1)
    code = jnp.pad(code.reshape(most, SEG), ((0, 0), (0, LANES - SEG)), constant_values=-1)
    half = TILE // 2
    base = jnp.stack(
        [lax.axis_index("gs") * (cols_here * TILE) + half, lax.axis_index("img") * (rows_here * TILE) + half]
    ).astype(jnp.int32)
    return first, base, code, owner


def on_device(gaussians, send_slots, tile_lists, truth):
    rows_here, cols_here, list_len = tile_lists.shape
    devices = send_slots.shape[1] // CAP
    codes = jnp.pad(send_slots.reshape(devices, CAP), ((0, 0), (0, LANES - CAP)))
    outgoing = outgoing_splats(gaussians, codes)
    arrived = lax.all_to_all(outgoing, ("gs", "img"), split_axis=1, concat_axis=1, tiled=True)
    first, base, code, owner = arrange(tile_lists)
    rendered = blend_tiles(first, base, arrived, code, owner, cols_here)
    stacked = jnp.concatenate([rendered, truth])
    padded = extended(stacked, (("gs", 2), ("img", 1)), 5)
    rim_r, rim_t = (padded[0:3], padded[3:6])
    quantities = jnp.concatenate([rim_r, rim_t, rim_r * rim_r, rim_t * rim_t, rim_r * rim_t])
    img_height, img_width = (rendered.shape[1], rendered.shape[2])
    band_rows = band_matrix(img_height, img_height + 10, 1)
    band_cols = band_matrix(img_width, img_width + 10, 1).T
    filtered = jnp.einsum("ij,cjw->ciw", band_rows, quantities, precision=lax.Precision.HIGHEST)
    filtered = jnp.einsum("ciw,wv->civ", filtered, band_cols, precision=lax.Precision.HIGHEST)
    return (rendered, loss_from(filtered, rendered, truth))


def solution(mesh):
    return jax.shard_map(
        on_device,
        mesh=mesh,
        in_specs=(
            P(None, ("gs", "img")),
            P(("gs", "img"), None),
            P("img", "gs", None),
            P(None, "img", "gs"),
        ),
        out_specs=(P(None, "img", "gs"), P("img", "gs")),
        check_vma=False,
    )
```

```python
import functools
import math

import jax
import jax.numpy as jnp
import numpy as np
from jax import lax
from jax.experimental import pallas as pl
from jax.experimental.pallas import tpu as pltpu
from jax.sharding import PartitionSpec as P

TILE = 16
LANES = 128
CAP = 80
SPLAT = 9
LOG2E = 1.0 / math.log(2.0)
VMEM = pltpu.VMEM


coef_zero = 0.28209479177387814
coef_one = 0.4886025119029199
coef_two = [
    1.0925484305920792,
    -1.0925484305920792,
    0.31539156525252005,
    -1.0925484305920792,
    0.5462742152960396,
]
coef_three = [
    -0.5900435899266435,
    2.890611442640554,
    -0.4570457994644658,
    0.3731763325901154,
    -0.4570457994644658,
    1.445305721320277,
    -0.5900435899266435,
]
camera_z = -3000.0
ssim_share = 0.2
stable_one = 0.0001
stable_two = 0.0009


def project_chunk(gauss):
    row = lambda i: gauss[i : i + 1]
    mean_x, mean_y, mean_z = (row(0), row(1), row(2))
    squared = jnp.exp(2.0 * gauss[3:6])
    sq_0, sq_1, sq_2 = (squared[0:1], squared[1:2], squared[2:3])
    inv = 1.0 / jnp.sqrt(row(6) * row(6) + row(7) * row(7) + row(8) * row(8) + row(9) * row(9))
    quat_w, quat_x, quat_y, quat_z = (row(6) * inv, row(7) * inv, row(8) * inv, row(9) * inv)
    first_a = 1.0 - 2.0 * (quat_y * quat_y + quat_z * quat_z)
    first_b = 2.0 * (quat_x * quat_y - quat_w * quat_z)
    first_c = 2.0 * (quat_x * quat_z + quat_w * quat_y)
    second_a = 2.0 * (quat_x * quat_y + quat_w * quat_z)
    second_b = 1.0 - 2.0 * (quat_x * quat_x + quat_z * quat_z)
    second_c = 2.0 * (quat_y * quat_z - quat_w * quat_x)
    cov_xx = first_a * first_a * sq_0 + first_b * first_b * sq_1 + first_c * first_c * sq_2 + 0.3
    cov_xy = first_a * second_a * sq_0 + first_b * second_b * sq_1 + first_c * second_c * sq_2
    cov_yy = second_a * second_a * sq_0 + second_b * second_b * sq_1 + second_c * second_c * sq_2 + 0.3
    determinant = cov_xx * cov_yy - cov_xy * cov_xy
    opacity = 1.0 / (1.0 + jnp.exp(-row(10)))
    delta_z = mean_z - camera_z
    length = jnp.sqrt(mean_x * mean_x + mean_y * mean_y + delta_z * delta_z)
    dir_x, dir_y, dir_z = (mean_x / length, mean_y / length, delta_z / length)
    sq_x, sq_y, sq_z = (dir_x * dir_x, dir_y * dir_y, dir_z * dir_z)
    prod_xy, prod_yz, prod_xz = (dir_x * dir_y, dir_y * dir_z, dir_x * dir_z)
    basis = jnp.concatenate(
        [
            coef_zero * jnp.ones_like(dir_x),
            -coef_one * dir_y,
            coef_one * dir_z,
            -coef_one * dir_x,
            coef_two[0] * prod_xy,
            coef_two[1] * prod_yz,
            coef_two[2] * (2.0 * sq_z - sq_x - sq_y),
            coef_two[3] * prod_xz,
            coef_two[4] * (sq_x - sq_y),
            coef_three[0] * dir_y * (3.0 * sq_x - sq_y),
            coef_three[1] * prod_xy * dir_z,
            coef_three[2] * dir_y * (4.0 * sq_z - sq_x - sq_y),
            coef_three[3] * dir_z * (2.0 * sq_z - 3.0 * sq_x - 3.0 * sq_y),
            coef_three[4] * dir_x * (4.0 * sq_z - sq_x - sq_y),
            coef_three[5] * dir_z * (sq_x - sq_y),
            coef_three[6] * dir_x * (sq_x - 3.0 * sq_y),
        ],
        axis=0,
    )
    colour = []
    for channel in range(3):
        weights = gauss[11 + 16 * channel : 27 + 16 * channel]
        colour.append(jnp.maximum(jnp.sum(weights * basis, axis=0, keepdims=True) + 0.5, 0.0))
    return [
        mean_x,
        mean_y,
        cov_yy / determinant,
        -cov_xy / determinant,
        cov_xx / determinant,
        opacity,
    ] + colour


def lookup(tables, code, blocks, unroll):
    row = lax.shift_right_arithmetic(code, 7)
    lane = jnp.bitwise_and(code, LANES - 1)

    def one(block, found):
        hit = row == block
        out = []
        for p in range(SPLAT):
            line = jnp.broadcast_to(tables[p, pl.ds(block, 1), :], code.shape)
            taken = jnp.take_along_axis(line, lane, axis=1, mode="promise_in_bounds")
            out.append(jnp.where(hit, taken, found[p]))
        return tuple(out)

    zero = jnp.zeros(code.shape, jnp.float32)
    return lax.fori_loop(0, blocks, one, (zero,) * SPLAT, unroll=unroll)


def outgoing_kernel(gauss_ref, code_ref, out_ref, table):
    blocks = gauss_ref.shape[1] // LANES
    for block in range(blocks):
        rows = project_chunk(gauss_ref[:, block * LANES : (block + 1) * LANES])
        for p in range(SPLAT):
            table[p, block : block + 1, :] = rows[p]

    def dest(i, carry):
        where = pl.ds(pl.multiple_of(i * 8, 8), 8)
        found = lookup(table, code_ref[where, :], blocks, 8)
        for p in range(SPLAT):
            out_ref[p, where, :] = found[p]
        return carry

    lax.fori_loop(0, code_ref.shape[0] // 8, dest, 0)


def outgoing_splats(gaussians, codes):
    devices = codes.shape[0]
    return pl.pallas_call(
        outgoing_kernel,
        out_shape=jax.ShapeDtypeStruct((SPLAT, devices, LANES), jnp.float32),
        in_specs=[pl.BlockSpec(memory_space=VMEM)] * 2,
        out_specs=pl.BlockSpec(memory_space=VMEM),
        scratch_shapes=[VMEM((SPLAT, gaussians.shape[1] // LANES, LANES), jnp.float32)],
        compiler_params=pltpu.CompilerParams(vmem_limit_bytes=32 << 20),
        name="outgoing_splats",
    )(gaussians, codes)


SEG = 32
ROWS = 40
BLOCK = 8
COEFS = 32
PIXELS = TILE * TILE
CHUNK = 64


def monomials():
    pixel = np.arange(PIXELS)
    x = (pixel % TILE) - 7.5
    y = (pixel // TILE) - 7.5
    cols = np.stack([x * x, y * y, x * y, x, y, np.ones_like(x)], axis=1)
    return np.concatenate([cols, cols, cols, np.zeros((PIXELS, COEFS - 18))], axis=1).astype(np.float32)


def split(value, parts):
    out = []
    for _ in range(parts):
        rounded = value.astype(jnp.bfloat16)
        out.append(rounded)
        value = value - rounded.astype(jnp.float32)
    return out


def lane_pick(value, index, axis):
    return jnp.take_along_axis(value, index, axis=axis, mode="promise_in_bounds")


def blend_kernel(cols_here, first, base, arrived, lists, owner, mono, out_ref,
                 table_a, table_b, table, packed, codes, params, coefs, power_a, power_b, state, total_ref,
                 carry_ref, carry_owner):
    tiles = first.shape[0] - 1
    runs = lists.shape[0] // tiles
    groups = (first[tiles] + LANES - 1) // LANES
    per_group = SEG // BLOCK

    for p in range(SPLAT):
        flat = jnp.transpose(arrived[p])
        for half, ref in enumerate((table_a, table_b)):
            value = flat[half * ROWS : (half + 1) * ROWS]
            if p < 8:
                ref[pl.ds(p, ROWS, stride=8), :] = value
            else:
                ref[8 * ROWS : 9 * ROWS, :] = value
    for half, ref in enumerate((table_a, table_b)):
        for part, value in enumerate(split(ref[...], 3)):
            table[:, part * 256 + half * LANES : part * 256 + (half + 1) * LANES] = value

    packed[...] = jnp.full(packed.shape, -1, jnp.int32)
    for t in range(tiles):
        packed[pl.ds(first[t], runs), :] = lists[t * runs : (t + 1) * runs, :]

    def turn(g, carry):
        lanes = jnp.transpose(packed[pl.ds(pl.multiple_of(g * LANES, LANES), LANES), :])
        codes[pl.ds(pl.multiple_of(g * SEG, SEG), SEG), :] = lanes[0:SEG]
        return carry

    lax.fori_loop(0, groups, turn, 0)
    total_ref[...] = jnp.zeros_like(total_ref)
    carry_ref[...] = jnp.ones_like(carry_ref)
    carry_owner[...] = jnp.full(carry_owner.shape, -1, jnp.int32)

    column = lax.broadcasted_iota(jnp.int32, (256, 256), 0)
    table_row = lax.broadcasted_iota(jnp.int32, (ROWS, 256), 0)

    def lookup(block, j):
        slot = (block % 3) * 72
        where = block * BLOCK + 2 * j
        code = jnp.concatenate([codes[pl.ds(where, 1), :], codes[pl.ds(where + 1, 1), :]], axis=1)
        col = jnp.bitwise_and(code, 255)
        row = lax.shift_right_arithmetic(code, 8)
        hot = jnp.where(column == col, 1.0, 0.0).astype(jnp.bfloat16)
        found = jnp.dot(table[...], jnp.concatenate([hot, hot, hot], axis=0), preferred_element_type=jnp.float32)
        picked = jnp.zeros((8, 256), jnp.float32)
        rows8 = jnp.broadcast_to(row, (8, 256))
        for r in range(ROWS):
            picked = jnp.where(rows8 == r, found[r * 8 : (r + 1) * 8], picked)
        ninth = jnp.sum(jnp.where(table_row == row, found[8 * ROWS :], 0.0), axis=0, keepdims=True)
        return slot, picked, ninth

    def keep(j, slot, picked, ninth):
        for e in range(2):
            lanes = slice(e * LANES, (e + 1) * LANES)
            params[pl.ds(pl.multiple_of(slot + (2 * j + e) * 8, 8), 8), :] = picked[:, lanes]
            params[pl.ds(slot + 64 + 2 * j + e, 1), :] = ninth[:, lanes]

    def expand(block):
        slot = (block % 3) * 72
        m_x, m_y, a, b, c, o = [params[pl.ds(slot + p, BLOCK, stride=8), :] for p in range(6)]
        live = codes[pl.ds(pl.multiple_of(block * BLOCK, BLOCK), BLOCK), :] >= 0
        tile = owner[pl.ds(block // per_group, 1), :]
        tile_y = lax.shift_right_logical(tile, cols_here.bit_length() - 1)
        tile_x = jnp.bitwise_and(tile, cols_here - 1)
        u = m_x - (tile_x * TILE + base[0]).astype(jnp.float32)
        v = m_y - (tile_y * TILE + base[1]).astype(jnp.float32)
        level = LOG2E * (-0.5 * (a * u * u + c * v * v) - b * u * v)
        values = [
            (-0.5 * LOG2E) * a,
            (-0.5 * LOG2E) * c,
            -LOG2E * b,
            LOG2E * (a * u + b * v),
            LOG2E * (c * v + b * u),
            jnp.where(live, level + jnp.log2(o), -1e30),
        ]
        for i, value in enumerate(values):
            for part, rounded in enumerate(split(value, 3)):
                coefs[pl.ds(part * 6 + i, BLOCK, stride=COEFS), :] = rounded.astype(jnp.float32)

    def exponents(j):
        pair = [
            coefs[pl.ds((2 * j + e) * COEFS, COEFS), :].astype(jnp.bfloat16) for e in range(2)
        ]
        return jnp.dot(mono[...], jnp.concatenate(pair, axis=1), preferred_element_type=jnp.float32)

    def blend(block, j, power):
        slot = (block % 3) * 72
        at = lambda q, i: pl.ds(q * PIXELS + j * CHUNK + i * 8, 8)
        pieces = range(CHUNK // 8)
        left = [state[at(0, i), :] for i in pieces]
        colour = [[state[at(1 + ch, i), :] for i in pieces] for ch in range(3)]
        for k in range(BLOCK):
            rows = (slot + k * 8 + 6, slot + k * 8 + 7, slot + 64 + k)
            tints = [jnp.broadcast_to(params[pl.ds(r, 1), :], (8, LANES)) for r in rows]
            for i in pieces:
                alpha = jnp.exp2(power[k // 2, at(0, i), (k % 2) * LANES : (k % 2 + 1) * LANES])
                weight = left[i] * alpha
                left[i] = left[i] - weight
                for ch in range(3):
                    colour[ch][i] = colour[ch][i] + weight * tints[ch]
        for i in pieces:
            state[at(0, i), :] = left[i]
            for ch in range(3):
                state[at(1 + ch, i), :] = colour[ch][i]

    lane = lax.broadcasted_iota(jnp.int32, (8, LANES), 1)

    def flush(g):
        tile = jnp.broadcast_to(owner[pl.ds(g, 1), :], (8, LANES))
        left = state[0:PIXELS, :]
        same = []
        for d in (1, 2, 4, 8):
            same.append(((pltpu.roll(tile, d, 1) == tile) & (lane >= d))[0:1])
        for d, mask in zip((1, 2, 4, 8), same):
            left = left * jnp.where(mask, pltpu.roll(left, d, 1), 1.0)
        before = jnp.where(same[0], pltpu.roll(left, 1, 1), 1.0)
        goes_on = (tile == carry_owner[...])[0:1]
        behind = jnp.where(goes_on, carry_ref[...], 1.0)
        before = before * behind
        carry_ref[...] = jnp.broadcast_to((left * behind)[:, LANES - 1 :], (PIXELS, LANES))
        carry_owner[...] = jnp.broadcast_to(tile[:, LANES - 1 :], (8, LANES))
        member = lax.broadcasted_iota(jnp.int32, (tiles, LANES), 0) == tile[0:1]
        member = jnp.where(member, 1.0, 0.0).astype(jnp.bfloat16)
        member = jnp.concatenate([member, member], axis=1)
        for ch in range(3):
            part = before * state[(1 + ch) * PIXELS : (2 + ch) * PIXELS, :]
            pair = jnp.concatenate(split(part, 2), axis=1)
            total_ref[ch] += lax.dot_general(
                member, pair, (((1,), (1,)), ((), ())), preferred_element_type=jnp.float32
            )

    coefs[...] = jnp.zeros_like(coefs)
    steps = BLOCK // 2

    def look_ahead(block):
        for j, found in enumerate([lookup(block, j) for j in range(steps)]):
            keep(j, *found)
        expand(block)

    look_ahead(0)
    for j in range(steps):
        power_a[j] = exponents(j)
    look_ahead(1)

    def one_group(g, carry):
        state[0:PIXELS, :] = jnp.ones((PIXELS, LANES), jnp.float32)
        state[PIXELS:, :] = jnp.zeros((3 * PIXELS, LANES), jnp.float32)

        def two_blocks(i, carry):
            for which in range(2):
                block = g * per_group + 2 * i + which
                now, later = ((power_a, power_b), (power_b, power_a))[which]

                found = [lookup(block + 2, j) for j in range(steps)]
                for j in range(steps):
                    later[j] = exponents(j)
                for j in range(steps):
                    blend(block, j, now)
                for j in range(steps):
                    keep(j, *found[j])
                expand(block + 2)
            return carry

        lax.fori_loop(0, per_group // 2, two_blocks, 0)
        flush(g)
        return carry

    lax.fori_loop(0, groups, one_group, 0)

    piece = lax.broadcasted_iota(jnp.int32, (8, LANES), 1)
    inner, outer = piece % TILE, piece // TILE
    sub = lax.broadcasted_iota(jnp.int32, (8, LANES), 0)
    skew = (outer + 8 - sub) % 8 * TILE + inner
    down = (outer + 8 - sub) % 8
    back = (outer + sub) % 8 * TILE + inner
    for ch in range(3):
        for r in range(tiles // cols_here):
            for q in range(cols_here // 8):
                for h in range(2):
                    x = total_ref[ch, r * cols_here + q * 8 : r * cols_here + q * 8 + 8, h * LANES : (h + 1) * LANES]
                    x = lane_pick(lane_pick(lane_pick(x, skew, 1), down, 0), back, 1)
                    out_ref[ch, r * TILE + h * 8 : r * TILE + h * 8 + 8, q * LANES : (q + 1) * LANES] = x


def blend_tiles(first, base, arrived, lists, owner, cols_here):
    tiles = first.shape[0] - 1
    most = lists.shape[0] // LANES
    smem = pl.BlockSpec(memory_space=pltpu.SMEM)
    vmem = pl.BlockSpec(memory_space=VMEM)
    f32 = jnp.float32
    return pl.pallas_call(
        functools.partial(blend_kernel, cols_here),
        out_shape=jax.ShapeDtypeStruct((3, tiles // cols_here * TILE, cols_here * TILE), f32),
        in_specs=[smem] * 2 + [vmem] * 4,
        out_specs=vmem,
        scratch_shapes=[
            VMEM((9 * ROWS, LANES), f32),
            VMEM((9 * ROWS, LANES), f32),
            VMEM((9 * ROWS, 768), jnp.bfloat16),
            VMEM((lists.shape[0] + LANES, LANES), jnp.int32),
            VMEM(((most + 1) * SEG, LANES), jnp.int32),
            VMEM((3 * 72, LANES), f32),
            VMEM((BLOCK * COEFS, LANES), f32),
            VMEM((BLOCK // 2, PIXELS, 256), f32),
            VMEM((BLOCK // 2, PIXELS, 256), f32),
            VMEM((4 * PIXELS, LANES), f32),
            VMEM((3, tiles, PIXELS), f32),
            VMEM((PIXELS, LANES), f32),
            VMEM((8, LANES), jnp.int32),
        ],
        compiler_params=pltpu.CompilerParams(vmem_limit_bytes=48 << 20),
        name="blend_tiles",
    )(first, base, arrived, lists, owner, jnp.asarray(monomials()).astype(jnp.bfloat16))


def arrange(tile_lists):
    rows_here, cols_here, list_len = tile_lists.shape
    tiles = rows_here * cols_here
    lists = tile_lists.reshape(tiles, list_len)
    runs = list_len // SEG
    live = (jnp.sum((lists >= 0).astype(jnp.int32), axis=1) + SEG - 1) // SEG
    number = jnp.arange(tiles, dtype=jnp.int32)
    ends = jnp.sum(jnp.where(number[None, :] <= number[:, None], live[None, :], 0), axis=1).astype(jnp.int32)
    first = jnp.concatenate([jnp.zeros((1,), jnp.int32), ends])
    most = tiles * runs
    segment = jnp.arange(most + LANES, dtype=jnp.int32)
    owner = jnp.sum((ends[None, :] <= segment[:, None]).astype(jnp.int32), axis=1).reshape(-1, LANES)
    slot, source = lists % CAP, lists // CAP
    code = jnp.where(lists >= 0, slot % ROWS * 256 + slot // ROWS * LANES + source, -1)
    code = jnp.pad(code.reshape(most, SEG), ((0, 0), (0, LANES - SEG)), constant_values=-1)
    half = TILE // 2
    base = jnp.stack(
        [lax.axis_index("gs") * (cols_here * TILE) + half, lax.axis_index("img") * (rows_here * TILE) + half]
    ).astype(jnp.int32)
    return first, base, code, owner


EDGE = 8
TAPS = 5


def halo_kernel(rendered, truth, row_out, col_out, row_buf, col_buf, row_sem, col_sem, row_done, col_done):
    n_gs, n_img = lax.axis_size("gs"), lax.axis_size("img")
    g, i = lax.axis_index("gs"), lax.axis_index("img")
    place = lambda dg, di: {"gs": lax.rem(g + n_gs + dg, n_gs), "img": lax.rem(i + n_img + di, n_img)}
    around = [(dg, di) for dg in (-1, 0, 1) for di in (-1, 0, 1) if (dg, di) != (0, 0)]
    barrier = pltpu.get_barrier_semaphore()
    for dg, di in around:
        pl.semaphore_signal(barrier, inc=1, device_id=place(dg, di), device_id_type=pl.DeviceIdType.MESH)

    height, width = rendered.shape[1:]
    for c in range(6):
        source = (rendered, truth)[c // 3]
        image = source[c % 3]
        for side in range(2):
            edge = image[0:EDGE] if side == 0 else image[height - EDGE :]
            for half in range(2):
                row_buf[side, c, half] = edge[:, half * LANES : (half + 1) * LANES]
            columns = image[:, 0:LANES] if side == 0 else image[:, width - LANES :]
            turned = jnp.transpose(columns)
            col_buf[side, c] = turned[0:EDGE] if side == 0 else turned[LANES - EDGE :]

    pl.semaphore_wait(barrier, len(around))
    copies = []
    for side in range(2):
        step = -1 if side == 0 else 1
        copies.append(
            pltpu.make_async_remote_copy(
                src_ref=row_buf.at[side],
                dst_ref=row_out.at[side],
                send_sem=row_sem.at[side],
                recv_sem=row_done.at[side],
                device_id=place(0, step),
                device_id_type=pl.DeviceIdType.MESH,
            )
        )
        for di in (-1, 0, 1):
            copies.append(
                pltpu.make_async_remote_copy(
                    src_ref=col_buf.at[side],
                    dst_ref=col_out.at[side * 3 + di + 1],
                    send_sem=col_sem.at[side * 3 + di + 1],
                    recv_sem=col_done.at[side * 3 + di + 1],
                    device_id=place(step, di),
                    device_id_type=pl.DeviceIdType.MESH,
                )
            )
    for copy in copies:
        copy.start()
    for copy in copies:
        copy.wait()


def exchange_halos(rendered, truth):
    vmem = pl.BlockSpec(memory_space=VMEM)
    rows = (2, 6, 2, EDGE, LANES)
    f32 = jnp.float32
    return pl.pallas_call(
        halo_kernel,
        out_shape=(jax.ShapeDtypeStruct(rows, f32), jax.ShapeDtypeStruct((6, 6, EDGE, LANES), f32)),
        in_specs=[vmem] * 2,
        out_specs=(vmem, vmem),
        scratch_shapes=[
            VMEM(rows, f32),
            VMEM((2, 6, EDGE, LANES), f32),
            pltpu.SemaphoreType.DMA((2,)),
            pltpu.SemaphoreType.DMA((6,)),
            pltpu.SemaphoreType.DMA((2,)),
            pltpu.SemaphoreType.DMA((6,)),
        ],
        compiler_params=pltpu.CompilerParams(collective_id=1, has_side_effects=True, vmem_limit_bytes=16 << 20),
        name="exchange_halos",
    )(rendered, truth)


def window():
    offsets = np.arange(11, dtype=np.float32) - 5.0
    weights = np.exp(-offsets * offsets / np.float32(4.5))
    return [float(w) for w in weights / np.sum(weights)]


def loss_kernel(has, rendered, truth, rows, cols, out_ref, maps):
    height = rendered.shape[1]
    tall = height + 2 * EDGE
    start = lambda q, part: (q * 3 + part) * tall
    left, right, above, below = [has[n] > 0 for n in range(4)]
    keep = lambda flag, value: jnp.where(flag, value, 0.0)
    lane = lax.broadcasted_iota(jnp.int32, (EDGE, LANES), 1)
    gap = jnp.zeros((LANES - 2 * EDGE, LANES), jnp.float32)
    for c in range(6):
        image = (rendered, truth)[c // 3]
        for half in range(2):
            base = start(c, half)
            maps[base : base + EDGE, :] = keep(above, rows[1, c, half])
            maps[base + EDGE : base + EDGE + height, :] = image[c % 3, :, half * LANES : (half + 1) * LANES]
            maps[base + EDGE + height : base + tall, :] = keep(below, rows[0, c, half])
        base = start(c, 2)
        after = keep(right, cols[1, c])
        before = keep(left, cols[4, c])
        maps[base + EDGE : base + EDGE + height, :] = jnp.transpose(jnp.concatenate([after, gap, before], axis=0))
        mixed = []
        for flag, side in ((right, 0), (left, 3)):
            upper = keep(flag & above, cols[side + 2, c])
            lower = keep(flag & below, cols[side + 0, c])
            mixed.append(jnp.where(lane < LANES // 2, lower, upper))
        turned = jnp.transpose(jnp.concatenate([mixed[0], gap, mixed[1]], axis=0))
        maps[base : base + EDGE, :] = turned[LANES - EDGE :]
        maps[base + EDGE + height : base + tall, :] = turned[0:EDGE]

    def products(n, carry):
        for ch in range(3):
            for part in range(3):
                at = lambda q: pl.ds(pl.multiple_of(start(q + ch, part) + n * 8, 8), 8)
                r, t = maps[at(0), :], maps[at(3), :]
                maps[at(6), :] = r * r + t * t
                maps[at(9), :] = r * t
        return carry

    lax.fori_loop(0, tall // 8, products, 0)
    weights = window()

    def filtered(q, n):
        parts = []
        for part in range(3):
            row = lambda d: maps[pl.ds(start(q, part) + EDGE + n * 8 + d, 8), :]
            total = weights[TAPS] * row(0)
            for d in range(1, TAPS + 1):
                total = total + weights[TAPS + d] * (row(d) + row(-d))
            parts.append(total)
        first, second, outside = parts
        sums = [weights[TAPS] * first, weights[TAPS] * second]
        for d in range(1, TAPS + 1):
            ahead = [pltpu.roll(x, LANES - d, 1) for x in (first, second, outside)]
            back = [pltpu.roll(x, d, 1) for x in (outside, first, second)]
            inside_ahead, inside_back = lane < LANES - d, lane >= d
            for half in range(2):
                pair = jnp.where(inside_ahead, ahead[half], ahead[half + 1])
                pair = pair + jnp.where(inside_back, back[half + 1], back[half])
                sums[half] = sums[half] + weights[TAPS + d] * pair
        return sums

    def one_block(n, carry):
        difference = [0.0, 0.0]
        alike = [0.0, 0.0]
        where = pl.ds(pl.multiple_of(n * 8, 8), 8)
        for ch in range(3):
            means_r, means_t, squares, products_rt = [filtered(q + ch, n) for q in (0, 3, 6, 9)]
            for half in range(2):
                mean_r, mean_t = means_r[half], means_t[half]
                both = mean_r * mean_t
                squared = mean_r * mean_r + mean_t * mean_t
                above_line = (2.0 * both + stable_one) * (2.0 * (products_rt[half] - both) + stable_two)
                below_line = (squared + stable_one) * (squares[half] - squared + stable_two)
                alike[half] = alike[half] + above_line / below_line
                at = pl.ds(pl.multiple_of(start(ch, half) + EDGE + n * 8, 8), 8)
                at_t = pl.ds(pl.multiple_of(start(ch + 3, half) + EDGE + n * 8, 8), 8)
                difference[half] = difference[half] + jnp.abs(maps[at, :] - maps[at_t, :])
        for half in range(2):
            out_ref[where, half * LANES : (half + 1) * LANES] = (1.0 - ssim_share) * (
                difference[half] * (1.0 / 3.0)
            ) + ssim_share * (1.0 - alike[half] * (1.0 / 3.0))
        return carry

    lax.fori_loop(0, height // 8, one_block, 0)


def pixel_loss(has, rendered, truth, rows, cols):
    vmem = pl.BlockSpec(memory_space=VMEM)
    height, width = rendered.shape[1:]
    return pl.pallas_call(
        loss_kernel,
        out_shape=jax.ShapeDtypeStruct((height, width), jnp.float32),
        in_specs=[pl.BlockSpec(memory_space=pltpu.SMEM)] + [vmem] * 4,
        out_specs=vmem,
        scratch_shapes=[VMEM((12 * 3 * (height + 2 * EDGE), LANES), jnp.float32)],
        compiler_params=pltpu.CompilerParams(vmem_limit_bytes=32 << 20),
        name="pixel_loss",
    )(has, rendered, truth, rows, cols)


def on_device(gaussians, send_slots, tile_lists, truth):
    rows_here, cols_here, list_len = tile_lists.shape
    devices = send_slots.shape[1] // CAP
    codes = jnp.pad(send_slots.reshape(devices, CAP), ((0, 0), (0, LANES - CAP)))
    outgoing = outgoing_splats(gaussians, codes)
    arrived = lax.all_to_all(outgoing, ("gs", "img"), split_axis=1, concat_axis=1, tiled=True)
    first, base, code, owner = arrange(tile_lists)
    rendered = blend_tiles(first, base, arrived, code, owner, cols_here)
    rows, cols = exchange_halos(rendered, truth)
    g, i = lax.axis_index("gs"), lax.axis_index("img")
    has = jnp.stack([g > 0, g < lax.axis_size("gs") - 1, i > 0, i < lax.axis_size("img") - 1]).astype(jnp.int32)
    return (rendered, pixel_loss(has, rendered, truth, rows, cols))


def solution(mesh):
    return jax.shard_map(
        on_device,
        mesh=mesh,
        in_specs=(
            P(None, ("gs", "img")),
            P(("gs", "img"), None),
            P("img", "gs", None),
            P(None, "img", "gs"),
        ),
        out_specs=(P(None, "img", "gs"), P("img", "gs")),
        check_vma=False,
    )
```

```python
import functools
import math

import jax
import jax.numpy as jnp
import numpy as np
from jax import lax
from jax.experimental import pallas as pl
from jax.experimental.pallas import tpu as pltpu
from jax.sharding import PartitionSpec as P

TILE = 16
LANES = 128
CAP = 80
SPLAT = 9
LOG2E = 1.0 / math.log(2.0)
VMEM = pltpu.VMEM


coef_zero = 0.28209479177387814
coef_one = 0.4886025119029199
coef_two = [
    1.0925484305920792,
    -1.0925484305920792,
    0.31539156525252005,
    -1.0925484305920792,
    0.5462742152960396,
]
coef_three = [
    -0.5900435899266435,
    2.890611442640554,
    -0.4570457994644658,
    0.3731763325901154,
    -0.4570457994644658,
    1.445305721320277,
    -0.5900435899266435,
]
camera_z = -3000.0
ssim_share = 0.2
stable_one = 0.0001
stable_two = 0.0009


def project_chunk(gauss):
    row = lambda i: gauss[i : i + 1]
    mean_x, mean_y, mean_z = (row(0), row(1), row(2))
    squared = jnp.exp(2.0 * gauss[3:6])
    sq_0, sq_1, sq_2 = (squared[0:1], squared[1:2], squared[2:3])
    inv = 1.0 / jnp.sqrt(row(6) * row(6) + row(7) * row(7) + row(8) * row(8) + row(9) * row(9))
    quat_w, quat_x, quat_y, quat_z = (row(6) * inv, row(7) * inv, row(8) * inv, row(9) * inv)
    first_a = 1.0 - 2.0 * (quat_y * quat_y + quat_z * quat_z)
    first_b = 2.0 * (quat_x * quat_y - quat_w * quat_z)
    first_c = 2.0 * (quat_x * quat_z + quat_w * quat_y)
    second_a = 2.0 * (quat_x * quat_y + quat_w * quat_z)
    second_b = 1.0 - 2.0 * (quat_x * quat_x + quat_z * quat_z)
    second_c = 2.0 * (quat_y * quat_z - quat_w * quat_x)
    cov_xx = first_a * first_a * sq_0 + first_b * first_b * sq_1 + first_c * first_c * sq_2 + 0.3
    cov_xy = first_a * second_a * sq_0 + first_b * second_b * sq_1 + first_c * second_c * sq_2
    cov_yy = second_a * second_a * sq_0 + second_b * second_b * sq_1 + second_c * second_c * sq_2 + 0.3
    determinant = cov_xx * cov_yy - cov_xy * cov_xy
    opacity = 1.0 / (1.0 + jnp.exp(-row(10)))
    delta_z = mean_z - camera_z
    length = jnp.sqrt(mean_x * mean_x + mean_y * mean_y + delta_z * delta_z)
    dir_x, dir_y, dir_z = (mean_x / length, mean_y / length, delta_z / length)
    sq_x, sq_y, sq_z = (dir_x * dir_x, dir_y * dir_y, dir_z * dir_z)
    prod_xy, prod_yz, prod_xz = (dir_x * dir_y, dir_y * dir_z, dir_x * dir_z)
    basis = jnp.concatenate(
        [
            coef_zero * jnp.ones_like(dir_x),
            -coef_one * dir_y,
            coef_one * dir_z,
            -coef_one * dir_x,
            coef_two[0] * prod_xy,
            coef_two[1] * prod_yz,
            coef_two[2] * (2.0 * sq_z - sq_x - sq_y),
            coef_two[3] * prod_xz,
            coef_two[4] * (sq_x - sq_y),
            coef_three[0] * dir_y * (3.0 * sq_x - sq_y),
            coef_three[1] * prod_xy * dir_z,
            coef_three[2] * dir_y * (4.0 * sq_z - sq_x - sq_y),
            coef_three[3] * dir_z * (2.0 * sq_z - 3.0 * sq_x - 3.0 * sq_y),
            coef_three[4] * dir_x * (4.0 * sq_z - sq_x - sq_y),
            coef_three[5] * dir_z * (sq_x - sq_y),
            coef_three[6] * dir_x * (sq_x - 3.0 * sq_y),
        ],
        axis=0,
    )
    colour = []
    for channel in range(3):
        weights = gauss[11 + 16 * channel : 27 + 16 * channel]
        colour.append(jnp.maximum(jnp.sum(weights * basis, axis=0, keepdims=True) + 0.5, 0.0))
    return [
        mean_x,
        mean_y,
        cov_yy / determinant,
        -cov_xy / determinant,
        cov_xx / determinant,
        opacity,
    ] + colour


def split(value, parts):
    out = []
    for _ in range(parts):
        rounded = value.astype(jnp.bfloat16)
        out.append(rounded)
        value = value - rounded.astype(jnp.float32)
    return out


def fill_table(table, halves):
    for half, ref in enumerate(halves):
        for part, value in enumerate(split(ref[...], 3)):
            table[:, part * 256 + half * LANES : part * 256 + (half + 1) * LANES] = value


def lookup(table, code):
    rows = table.shape[0] // SPLAT
    column = lax.broadcasted_iota(jnp.int32, (256, 256), 0)
    col = jnp.bitwise_and(code, 255)
    row = lax.shift_right_arithmetic(code, 8)
    hot = jnp.where(column == col, 1.0, 0.0).astype(jnp.bfloat16)
    found = jnp.dot(table[...], jnp.concatenate([hot, hot, hot], axis=0), preferred_element_type=jnp.float32)
    picked = jnp.zeros((8, 256), jnp.float32)
    rows8 = jnp.broadcast_to(row, (8, 256))
    for r in range(rows):
        picked = jnp.where(rows8 == r, found[r * 8 : (r + 1) * 8], picked)
    table_row = lax.broadcasted_iota(jnp.int32, (rows, 256), 0)
    ninth = jnp.sum(jnp.where(table_row == row, found[8 * rows :], 0.0), axis=0, keepdims=True)
    return picked, ninth


def outgoing_kernel(gauss_ref, code_ref, out_ref, table_a, table_b, table, eight, ninth):
    blocks = gauss_ref.shape[1] // LANES
    rows = blocks // 2
    for block in range(blocks):
        splat = project_chunk(gauss_ref[:, block * LANES : (block + 1) * LANES])
        ref = (table_a, table_b)[block // rows]
        r = block % rows
        ref[r * 8 : r * 8 + 8, :] = jnp.concatenate(splat[:8], axis=0)
        ref[8 * rows + r : 8 * rows + r + 1, :] = splat[8]
    fill_table(table, (table_a, table_b))

    def eight_slots(i, carry):
        where = pl.multiple_of(i * 8, 8)
        codes = code_ref[pl.ds(where, 8), :]
        found = [
            lookup(table, jnp.concatenate([codes[2 * j : 2 * j + 1], codes[2 * j + 1 : 2 * j + 2]], axis=1))
            for j in range(4)
        ]
        for j, (first, last) in enumerate(found):
            for e in range(2):
                lanes = slice(e * LANES, (e + 1) * LANES)
                eight[pl.ds(where * 8 + (2 * j + e) * 8, 8), :] = first[:, lanes]
                ninth[pl.ds(where + 2 * j + e, 1), :] = last[:, lanes]
        return carry

    eight[CAP * 8 :, :] = jnp.zeros((eight.shape[0] - CAP * 8, LANES), jnp.float32)
    ninth[CAP:, :] = jnp.zeros((LANES - CAP, LANES), jnp.float32)
    lax.fori_loop(0, CAP // 8, eight_slots, 0)
    for p in range(SPLAT):
        out_ref[p] = jnp.transpose(eight[pl.ds(p, LANES, stride=8), :] if p < 8 else ninth[...])


def outgoing_splats(gaussians, codes):
    devices = codes.shape[1]
    rows = gaussians.shape[1] // (2 * LANES)
    f32 = jnp.float32
    return pl.pallas_call(
        outgoing_kernel,
        out_shape=jax.ShapeDtypeStruct((SPLAT, devices, LANES), f32),
        in_specs=[pl.BlockSpec(memory_space=VMEM)] * 2,
        out_specs=pl.BlockSpec(memory_space=VMEM),
        scratch_shapes=[
            VMEM((SPLAT * rows, LANES), f32),
            VMEM((SPLAT * rows, LANES), f32),
            VMEM((SPLAT * rows, 768), jnp.bfloat16),
            VMEM((8 * LANES, LANES), f32),
            VMEM((LANES, LANES), f32),
        ],
        compiler_params=pltpu.CompilerParams(vmem_limit_bytes=32 << 20),
        name="outgoing_splats",
    )(gaussians, codes)


def deal_kernel(out_ref, in_ref, held, send_1, done_1, send_2, done_2, local_sem):
    n_gs, n_img = lax.axis_size("gs"), lax.axis_size("img")
    g, i = lax.axis_index("gs"), lax.axis_index("img")
    mesh_id = pl.DeviceIdType.MESH
    barrier = pltpu.get_barrier_semaphore()
    other_g = [lax.rem(g + d, n_gs) for d in range(1, n_gs)]
    other_i = [lax.rem(i + d, n_img) for d in range(1, n_img)]
    for to in other_g:
        pl.semaphore_signal(barrier, inc=1, device_id={"gs": to, "img": i}, device_id_type=mesh_id)
    for to in other_i:
        pl.semaphore_signal(barrier, inc=1, device_id={"gs": g, "img": to}, device_id_type=mesh_id)
    pl.semaphore_wait(barrier, n_gs + n_img - 2)
    first = [
        pltpu.make_async_remote_copy(
            src_ref=out_ref.at[:, to],
            dst_ref=held.at[:, g],
            send_sem=send_1.at[d],
            recv_sem=done_1.at[d],
            device_id={"gs": to, "img": i},
            device_id_type=mesh_id,
        )
        for d, to in enumerate(other_g)
    ]
    for copy in first:
        copy.start()
    own = pltpu.make_async_copy(out_ref.at[:, g], held.at[:, g], local_sem.at[0])
    own.start()
    own.wait()
    for copy in first:
        copy.wait_recv()
    second = [
        pltpu.make_async_remote_copy(
            src_ref=held.at[:, :, to],
            dst_ref=in_ref.at[:, :, i],
            send_sem=send_2.at[d],
            recv_sem=done_2.at[d],
            device_id={"gs": g, "img": to},
            device_id_type=mesh_id,
        )
        for d, to in enumerate(other_i)
    ]
    for copy in second:
        copy.start()
    own = pltpu.make_async_copy(held.at[:, :, i], in_ref.at[:, :, i], local_sem.at[1])
    own.start()
    own.wait()
    for copy in first:
        copy.wait_send()
    for copy in second:
        copy.wait()


def deal(outgoing):
    n_gs, n_img = lax.axis_size("gs"), lax.axis_size("img")
    shape = (SPLAT, n_gs, n_img, LANES)
    vmem = pl.BlockSpec(memory_space=VMEM)
    dma = pltpu.SemaphoreType.DMA
    arrived = pl.pallas_call(
        deal_kernel,
        out_shape=jax.ShapeDtypeStruct(shape, jnp.float32),
        in_specs=[vmem],
        out_specs=vmem,
        scratch_shapes=[
            VMEM(shape, jnp.float32), dma((n_gs - 1,)), dma((n_gs - 1,)), dma((n_img - 1,)), dma((n_img - 1,)), dma((2,))
        ],
        compiler_params=pltpu.CompilerParams(collective_id=2, has_side_effects=True, vmem_limit_bytes=16 << 20),
        name="deal_splats",
    )(outgoing.reshape(shape))
    return arrived.reshape(outgoing.shape)


SEG = 32
ROWS = 40
BLOCK = 8
COEFS = 32
PIXELS = TILE * TILE
CHUNK = 64


def monomials():
    pixel = np.arange(PIXELS)
    x = (pixel % TILE) - 7.5
    y = (pixel // TILE) - 7.5
    cols = np.stack([x * x, y * y, x * y, x, y, np.ones_like(x)], axis=1)
    return np.concatenate([cols, cols, cols, np.zeros((PIXELS, COEFS - 18))], axis=1).astype(np.float32)


def lane_pick(value, index, axis):
    return jnp.take_along_axis(value, index, axis=axis, mode="promise_in_bounds")


def blend_kernel(cols_here, first, base, arrived, lists, owner, mono, out_ref,
                 table_a, table_b, table, packed, codes, params, coefs, power_a, power_b, state, total_ref,
                 carry_ref, carry_owner):
    tiles = first.shape[0] - 1
    runs = lists.shape[0] // tiles
    groups = (first[tiles] + LANES - 1) // LANES
    per_group = SEG // BLOCK

    for p in range(SPLAT):
        flat = jnp.transpose(arrived[p])
        for half, ref in enumerate((table_a, table_b)):
            value = flat[half * ROWS : (half + 1) * ROWS]
            if p < 8:
                ref[pl.ds(p, ROWS, stride=8), :] = value
            else:
                ref[8 * ROWS : 9 * ROWS, :] = value
    fill_table(table, (table_a, table_b))

    packed[...] = jnp.full(packed.shape, -1, jnp.int32)
    for t in range(tiles):
        packed[pl.ds(first[t], runs), :] = lists[t * runs : (t + 1) * runs, :]

    def turn(g, carry):
        lanes = jnp.transpose(packed[pl.ds(pl.multiple_of(g * LANES, LANES), LANES), :])
        codes[pl.ds(pl.multiple_of(g * SEG, SEG), SEG), :] = lanes[0:SEG]
        return carry

    lax.fori_loop(0, groups, turn, 0)
    total_ref[...] = jnp.zeros_like(total_ref)
    carry_ref[...] = jnp.ones_like(carry_ref)
    carry_owner[...] = jnp.full(carry_owner.shape, -1, jnp.int32)

    def look(block, j):
        where = block * BLOCK + 2 * j
        code = jnp.concatenate([codes[pl.ds(where, 1), :], codes[pl.ds(where + 1, 1), :]], axis=1)
        return ((block % 3) * 72,) + lookup(table, code)

    def keep(j, slot, picked, ninth):
        for e in range(2):
            lanes = slice(e * LANES, (e + 1) * LANES)
            params[pl.ds(pl.multiple_of(slot + (2 * j + e) * 8, 8), 8), :] = picked[:, lanes]
            params[pl.ds(slot + 64 + 2 * j + e, 1), :] = ninth[:, lanes]

    def expand(block):
        slot = (block % 3) * 72
        m_x, m_y, a, b, c, o = [params[pl.ds(slot + p, BLOCK, stride=8), :] for p in range(6)]
        live = codes[pl.ds(pl.multiple_of(block * BLOCK, BLOCK), BLOCK), :] >= 0
        tile = owner[pl.ds(block // per_group, 1), :]
        tile_y = lax.shift_right_logical(tile, cols_here.bit_length() - 1)
        tile_x = jnp.bitwise_and(tile, cols_here - 1)
        u = m_x - (tile_x * TILE + base[0]).astype(jnp.float32)
        v = m_y - (tile_y * TILE + base[1]).astype(jnp.float32)
        level = LOG2E * (-0.5 * (a * u * u + c * v * v) - b * u * v)
        values = [
            (-0.5 * LOG2E) * a,
            (-0.5 * LOG2E) * c,
            -LOG2E * b,
            LOG2E * (a * u + b * v),
            LOG2E * (c * v + b * u),
            jnp.where(live, level + jnp.log2(o), -1e30),
        ]
        for i, value in enumerate(values):
            for part, rounded in enumerate(split(value, 3)):
                coefs[pl.ds(part * 6 + i, BLOCK, stride=COEFS), :] = rounded.astype(jnp.float32)

    def exponents(j):
        pair = [
            coefs[pl.ds((2 * j + e) * COEFS, COEFS), :].astype(jnp.bfloat16) for e in range(2)
        ]
        return jnp.dot(mono[...], jnp.concatenate(pair, axis=1), preferred_element_type=jnp.float32)

    def blend(block, j, power):
        slot = (block % 3) * 72
        at = lambda q, i: pl.ds(q * PIXELS + j * CHUNK + i * 8, 8)
        pieces = range(CHUNK // 8)
        left = [state[at(0, i), :] for i in pieces]
        colour = [[state[at(1 + ch, i), :] for i in pieces] for ch in range(3)]
        for k in range(BLOCK):
            rows = (slot + k * 8 + 6, slot + k * 8 + 7, slot + 64 + k)
            tints = [jnp.broadcast_to(params[pl.ds(r, 1), :], (8, LANES)) for r in rows]
            for i in pieces:
                alpha = jnp.exp2(power[k // 2, at(0, i), (k % 2) * LANES : (k % 2 + 1) * LANES])
                weight = left[i] * alpha
                left[i] = left[i] - weight
                for ch in range(3):
                    colour[ch][i] = colour[ch][i] + weight * tints[ch]
        for i in pieces:
            state[at(0, i), :] = left[i]
            for ch in range(3):
                state[at(1 + ch, i), :] = colour[ch][i]

    lane = lax.broadcasted_iota(jnp.int32, (8, LANES), 1)

    def flush(g):
        tile = jnp.broadcast_to(owner[pl.ds(g, 1), :], (8, LANES))
        left = state[0:PIXELS, :]
        same = []
        for d in (1, 2, 4, 8):
            same.append(((pltpu.roll(tile, d, 1) == tile) & (lane >= d))[0:1])
        for d, mask in zip((1, 2, 4, 8), same):
            left = left * jnp.where(mask, pltpu.roll(left, d, 1), 1.0)
        before = jnp.where(same[0], pltpu.roll(left, 1, 1), 1.0)
        goes_on = (tile == carry_owner[...])[0:1]
        behind = jnp.where(goes_on, carry_ref[...], 1.0)
        before = before * behind
        carry_ref[...] = jnp.broadcast_to((left * behind)[:, LANES - 1 :], (PIXELS, LANES))
        carry_owner[...] = jnp.broadcast_to(tile[:, LANES - 1 :], (8, LANES))
        member = lax.broadcasted_iota(jnp.int32, (tiles, LANES), 0) == tile[0:1]
        member = jnp.where(member, 1.0, 0.0).astype(jnp.bfloat16)
        member = jnp.concatenate([member, member], axis=1)
        for ch in range(3):
            part = before * state[(1 + ch) * PIXELS : (2 + ch) * PIXELS, :]
            pair = jnp.concatenate(split(part, 2), axis=1)
            total_ref[ch] += lax.dot_general(
                member, pair, (((1,), (1,)), ((), ())), preferred_element_type=jnp.float32
            )

    coefs[...] = jnp.zeros_like(coefs)
    steps = BLOCK // 2

    def look_ahead(block):
        for j, found in enumerate([look(block, j) for j in range(steps)]):
            keep(j, *found)
        expand(block)

    look_ahead(0)
    for j in range(steps):
        power_a[j] = exponents(j)
    look_ahead(1)

    def one_group(g, carry):
        state[0:PIXELS, :] = jnp.ones((PIXELS, LANES), jnp.float32)
        state[PIXELS:, :] = jnp.zeros((3 * PIXELS, LANES), jnp.float32)

        def two_blocks(i, carry):
            for which in range(2):
                block = g * per_group + 2 * i + which
                now, later = ((power_a, power_b), (power_b, power_a))[which]

                found = [look(block + 2, j) for j in range(steps)]
                for j in range(steps):
                    later[j] = exponents(j)
                for j in range(steps):
                    blend(block, j, now)
                for j in range(steps):
                    keep(j, *found[j])
                expand(block + 2)
            return carry

        lax.fori_loop(0, per_group // 2, two_blocks, 0)
        flush(g)
        return carry

    lax.fori_loop(0, groups, one_group, 0)

    piece = lax.broadcasted_iota(jnp.int32, (8, LANES), 1)
    inner, outer = piece % TILE, piece // TILE
    sub = lax.broadcasted_iota(jnp.int32, (8, LANES), 0)
    skew = (outer + 8 - sub) % 8 * TILE + inner
    down = (outer + 8 - sub) % 8
    back = (outer + sub) % 8 * TILE + inner
    for ch in range(3):
        for r in range(tiles // cols_here):
            for q in range(cols_here // 8):
                for h in range(2):
                    x = total_ref[ch, r * cols_here + q * 8 : r * cols_here + q * 8 + 8, h * LANES : (h + 1) * LANES]
                    x = lane_pick(lane_pick(lane_pick(x, skew, 1), down, 0), back, 1)
                    out_ref[ch, r * TILE + h * 8 : r * TILE + h * 8 + 8, q * LANES : (q + 1) * LANES] = x


def blend_tiles(first, base, arrived, lists, owner, cols_here):
    tiles = first.shape[0] - 1
    most = lists.shape[0] // LANES
    smem = pl.BlockSpec(memory_space=pltpu.SMEM)
    vmem = pl.BlockSpec(memory_space=VMEM)
    f32 = jnp.float32
    return pl.pallas_call(
        functools.partial(blend_kernel, cols_here),
        out_shape=jax.ShapeDtypeStruct((3, tiles // cols_here * TILE, cols_here * TILE), f32),
        in_specs=[smem] * 2 + [vmem] * 4,
        out_specs=vmem,
        scratch_shapes=[
            VMEM((9 * ROWS, LANES), f32),
            VMEM((9 * ROWS, LANES), f32),
            VMEM((9 * ROWS, 768), jnp.bfloat16),
            VMEM((lists.shape[0] + LANES, LANES), jnp.int32),
            VMEM(((most + 1) * SEG, LANES), jnp.int32),
            VMEM((3 * 72, LANES), f32),
            VMEM((BLOCK * COEFS, LANES), f32),
            VMEM((BLOCK // 2, PIXELS, 256), f32),
            VMEM((BLOCK // 2, PIXELS, 256), f32),
            VMEM((4 * PIXELS, LANES), f32),
            VMEM((3, tiles, PIXELS), f32),
            VMEM((PIXELS, LANES), f32),
            VMEM((8, LANES), jnp.int32),
        ],
        compiler_params=pltpu.CompilerParams(vmem_limit_bytes=48 << 20),
        name="blend_tiles",
    )(first, base, arrived, lists, owner, jnp.asarray(monomials()).astype(jnp.bfloat16))


def arrange(tile_lists):
    rows_here, cols_here, list_len = tile_lists.shape
    tiles = rows_here * cols_here
    lists = tile_lists.reshape(tiles, list_len)
    runs = list_len // SEG
    live = (jnp.sum((lists >= 0).astype(jnp.int32), axis=1) + SEG - 1) // SEG
    number = jnp.arange(tiles, dtype=jnp.int32)
    ends = jnp.sum(jnp.where(number[None, :] <= number[:, None], live[None, :], 0), axis=1).astype(jnp.int32)
    first = jnp.concatenate([jnp.zeros((1,), jnp.int32), ends])
    most = tiles * runs
    segment = jnp.arange(most + LANES, dtype=jnp.int32)
    owner = jnp.sum((ends[None, :] <= segment[:, None]).astype(jnp.int32), axis=1).reshape(-1, LANES)
    slot, source = lists % CAP, lists // CAP
    code = jnp.where(lists >= 0, slot % ROWS * 256 + slot // ROWS * LANES + source, -1)
    code = jnp.pad(code.reshape(most, SEG), ((0, 0), (0, LANES - SEG)), constant_values=-1)
    half = TILE // 2
    base = jnp.stack(
        [lax.axis_index("gs") * (cols_here * TILE) + half, lax.axis_index("img") * (rows_here * TILE) + half]
    ).astype(jnp.int32)
    return first, base, code, owner


EDGE = 8
TAPS = 5


def halo_kernel(rendered, truth, row_out, col_out, row_buf, col_buf, row_sem, col_sem, row_done, col_done):
    n_gs, n_img = lax.axis_size("gs"), lax.axis_size("img")
    g, i = lax.axis_index("gs"), lax.axis_index("img")
    place = lambda dg, di: {"gs": lax.rem(g + n_gs + dg, n_gs), "img": lax.rem(i + n_img + di, n_img)}
    around = [(dg, di) for dg in (-1, 0, 1) for di in (-1, 0, 1) if (dg, di) != (0, 0)]
    barrier = pltpu.get_barrier_semaphore()
    for dg, di in around:
        pl.semaphore_signal(barrier, inc=1, device_id=place(dg, di), device_id_type=pl.DeviceIdType.MESH)

    height, width = rendered.shape[1:]
    for c in range(6):
        source = (rendered, truth)[c // 3]
        image = source[c % 3]
        for side in range(2):
            edge = image[0:EDGE] if side == 0 else image[height - EDGE :]
            for half in range(2):
                row_buf[side, c, half] = edge[:, half * LANES : (half + 1) * LANES]
            columns = image[:, 0:LANES] if side == 0 else image[:, width - LANES :]
            turned = jnp.transpose(columns)
            col_buf[side, c] = turned[0:EDGE] if side == 0 else turned[LANES - EDGE :]

    pl.semaphore_wait(barrier, len(around))
    copies = []
    for side in range(2):
        step = -1 if side == 0 else 1
        copies.append(
            pltpu.make_async_remote_copy(
                src_ref=row_buf.at[side],
                dst_ref=row_out.at[side],
                send_sem=row_sem.at[side],
                recv_sem=row_done.at[side],
                device_id=place(0, step),
                device_id_type=pl.DeviceIdType.MESH,
            )
        )
        for di in (-1, 0, 1):
            copies.append(
                pltpu.make_async_remote_copy(
                    src_ref=col_buf.at[side],
                    dst_ref=col_out.at[side * 3 + di + 1],
                    send_sem=col_sem.at[side * 3 + di + 1],
                    recv_sem=col_done.at[side * 3 + di + 1],
                    device_id=place(step, di),
                    device_id_type=pl.DeviceIdType.MESH,
                )
            )
    for copy in copies:
        copy.start()
    for copy in copies:
        copy.wait()


def exchange_halos(rendered, truth):
    vmem = pl.BlockSpec(memory_space=VMEM)
    rows = (2, 6, 2, EDGE, LANES)
    f32 = jnp.float32
    return pl.pallas_call(
        halo_kernel,
        out_shape=(jax.ShapeDtypeStruct(rows, f32), jax.ShapeDtypeStruct((6, 6, EDGE, LANES), f32)),
        in_specs=[vmem] * 2,
        out_specs=(vmem, vmem),
        scratch_shapes=[
            VMEM(rows, f32),
            VMEM((2, 6, EDGE, LANES), f32),
            pltpu.SemaphoreType.DMA((2,)),
            pltpu.SemaphoreType.DMA((6,)),
            pltpu.SemaphoreType.DMA((2,)),
            pltpu.SemaphoreType.DMA((6,)),
        ],
        compiler_params=pltpu.CompilerParams(collective_id=1, has_side_effects=True, vmem_limit_bytes=16 << 20),
        name="exchange_halos",
    )(rendered, truth)


def window():
    offsets = np.arange(11, dtype=np.float32) - 5.0
    weights = np.exp(-offsets * offsets / np.float32(4.5))
    return [float(w) for w in weights / np.sum(weights)]


def loss_kernel(has, rendered, truth, rows, cols, out_ref, maps):
    height = rendered.shape[1]
    tall = height + 2 * EDGE
    start = lambda q, part: (q * 3 + part) * tall
    left, right, above, below = [has[n] > 0 for n in range(4)]
    keep = lambda flag, value: jnp.where(flag, value, 0.0)
    lane = lax.broadcasted_iota(jnp.int32, (EDGE, LANES), 1)
    gap = jnp.zeros((LANES - 2 * EDGE, LANES), jnp.float32)
    for c in range(6):
        image = (rendered, truth)[c // 3]
        for half in range(2):
            base = start(c, half)
            maps[base : base + EDGE, :] = keep(above, rows[1, c, half])
            maps[base + EDGE : base + EDGE + height, :] = image[c % 3, :, half * LANES : (half + 1) * LANES]
            maps[base + EDGE + height : base + tall, :] = keep(below, rows[0, c, half])
        base = start(c, 2)
        after = keep(right, cols[1, c])
        before = keep(left, cols[4, c])
        maps[base + EDGE : base + EDGE + height, :] = jnp.transpose(jnp.concatenate([after, gap, before], axis=0))
        mixed = []
        for flag, side in ((right, 0), (left, 3)):
            upper = keep(flag & above, cols[side + 2, c])
            lower = keep(flag & below, cols[side + 0, c])
            mixed.append(jnp.where(lane < LANES // 2, lower, upper))
        turned = jnp.transpose(jnp.concatenate([mixed[0], gap, mixed[1]], axis=0))
        maps[base : base + EDGE, :] = turned[LANES - EDGE :]
        maps[base + EDGE + height : base + tall, :] = turned[0:EDGE]

    def products(n, carry):
        for ch in range(3):
            for part in range(3):
                at = lambda q: pl.ds(pl.multiple_of(start(q + ch, part) + n * 8, 8), 8)
                r, t = maps[at(0), :], maps[at(3), :]
                maps[at(6), :] = r * r + t * t
                maps[at(9), :] = r * t
        return carry

    lax.fori_loop(0, tall // 8, products, 0)
    weights = window()

    def filtered(q, n):
        parts = []
        for part in range(3):
            row = lambda d: maps[pl.ds(start(q, part) + EDGE + n * 8 + d, 8), :]
            total = weights[TAPS] * row(0)
            for d in range(1, TAPS + 1):
                total = total + weights[TAPS + d] * (row(d) + row(-d))
            parts.append(total)
        first, second, outside = parts
        sums = [weights[TAPS] * first, weights[TAPS] * second]
        for d in range(1, TAPS + 1):
            ahead = [pltpu.roll(x, LANES - d, 1) for x in (first, second, outside)]
            back = [pltpu.roll(x, d, 1) for x in (outside, first, second)]
            inside_ahead, inside_back = lane < LANES - d, lane >= d
            for half in range(2):
                pair = jnp.where(inside_ahead, ahead[half], ahead[half + 1])
                pair = pair + jnp.where(inside_back, back[half + 1], back[half])
                sums[half] = sums[half] + weights[TAPS + d] * pair
        return sums

    def one_block(n, carry):
        difference = [0.0, 0.0]
        alike = [0.0, 0.0]
        where = pl.ds(pl.multiple_of(n * 8, 8), 8)
        for ch in range(3):
            means_r, means_t, squares, products_rt = [filtered(q + ch, n) for q in (0, 3, 6, 9)]
            for half in range(2):
                mean_r, mean_t = means_r[half], means_t[half]
                both = mean_r * mean_t
                squared = mean_r * mean_r + mean_t * mean_t
                above_line = (2.0 * both + stable_one) * (2.0 * (products_rt[half] - both) + stable_two)
                below_line = (squared + stable_one) * (squares[half] - squared + stable_two)
                alike[half] = alike[half] + above_line / below_line
                at = pl.ds(pl.multiple_of(start(ch, half) + EDGE + n * 8, 8), 8)
                at_t = pl.ds(pl.multiple_of(start(ch + 3, half) + EDGE + n * 8, 8), 8)
                difference[half] = difference[half] + jnp.abs(maps[at, :] - maps[at_t, :])
        for half in range(2):
            out_ref[where, half * LANES : (half + 1) * LANES] = (1.0 - ssim_share) * (
                difference[half] * (1.0 / 3.0)
            ) + ssim_share * (1.0 - alike[half] * (1.0 / 3.0))
        return carry

    lax.fori_loop(0, height // 8, one_block, 0)


def pixel_loss(has, rendered, truth, rows, cols):
    vmem = pl.BlockSpec(memory_space=VMEM)
    height, width = rendered.shape[1:]
    return pl.pallas_call(
        loss_kernel,
        out_shape=jax.ShapeDtypeStruct((height, width), jnp.float32),
        in_specs=[pl.BlockSpec(memory_space=pltpu.SMEM)] + [vmem] * 4,
        out_specs=vmem,
        scratch_shapes=[VMEM((12 * 3 * (height + 2 * EDGE), LANES), jnp.float32)],
        compiler_params=pltpu.CompilerParams(vmem_limit_bytes=32 << 20),
        name="pixel_loss",
    )(has, rendered, truth, rows, cols)


def on_device(gaussians, send_slots, tile_lists, truth):
    rows_here, cols_here, list_len = tile_lists.shape
    devices = send_slots.shape[1] // CAP
    half = gaussians.shape[1] // 2
    picks = send_slots.reshape(devices, CAP).T
    codes = picks % half // LANES * 256 + picks // half * LANES + picks % LANES
    arrived = deal(outgoing_splats(gaussians, codes))
    first, base, code, owner = arrange(tile_lists)
    rendered = blend_tiles(first, base, arrived, code, owner, cols_here)
    rows, cols = exchange_halos(rendered, truth)
    g, i = lax.axis_index("gs"), lax.axis_index("img")
    has = jnp.stack([g > 0, g < lax.axis_size("gs") - 1, i > 0, i < lax.axis_size("img") - 1]).astype(jnp.int32)
    return (rendered, pixel_loss(has, rendered, truth, rows, cols))


def solution(mesh):
    return jax.shard_map(
        on_device,
        mesh=mesh,
        in_specs=(
            P(None, ("gs", "img")),
            P(("gs", "img"), None),
            P("img", "gs", None),
            P(None, "img", "gs"),
        ),
        out_specs=(P(None, "img", "gs"), P("img", "gs")),
        check_vma=False,
    )
```

```python
import functools
import math

import jax
import jax.numpy as jnp
import numpy as np
from jax import lax
from jax.experimental import pallas as pl
from jax.experimental.pallas import tpu as pltpu
from jax.sharding import PartitionSpec as P

TILE = 16
LANES = 128
CAP = 80
SPLAT = 9
ROWS = CAP // 2
LOG2E = 1.0 / math.log(2.0)
VMEM = pltpu.VMEM


coef_zero = 0.28209479177387814
coef_one = 0.4886025119029199
coef_two = [
    1.0925484305920792,
    -1.0925484305920792,
    0.31539156525252005,
    -1.0925484305920792,
    0.5462742152960396,
]
coef_three = [
    -0.5900435899266435,
    2.890611442640554,
    -0.4570457994644658,
    0.3731763325901154,
    -0.4570457994644658,
    1.445305721320277,
    -0.5900435899266435,
]
camera_z = -3000.0
ssim_share = 0.2
stable_one = 0.0001
stable_two = 0.0009


def project_chunk(gauss):
    row = lambda i: gauss[i : i + 1]
    mean_x, mean_y, mean_z = (row(0), row(1), row(2))
    squared = jnp.exp(2.0 * gauss[3:6])
    sq_0, sq_1, sq_2 = (squared[0:1], squared[1:2], squared[2:3])
    inv = 1.0 / jnp.sqrt(row(6) * row(6) + row(7) * row(7) + row(8) * row(8) + row(9) * row(9))
    quat_w, quat_x, quat_y, quat_z = (row(6) * inv, row(7) * inv, row(8) * inv, row(9) * inv)
    first_a = 1.0 - 2.0 * (quat_y * quat_y + quat_z * quat_z)
    first_b = 2.0 * (quat_x * quat_y - quat_w * quat_z)
    first_c = 2.0 * (quat_x * quat_z + quat_w * quat_y)
    second_a = 2.0 * (quat_x * quat_y + quat_w * quat_z)
    second_b = 1.0 - 2.0 * (quat_x * quat_x + quat_z * quat_z)
    second_c = 2.0 * (quat_y * quat_z - quat_w * quat_x)
    cov_xx = first_a * first_a * sq_0 + first_b * first_b * sq_1 + first_c * first_c * sq_2 + 0.3
    cov_xy = first_a * second_a * sq_0 + first_b * second_b * sq_1 + first_c * second_c * sq_2
    cov_yy = second_a * second_a * sq_0 + second_b * second_b * sq_1 + second_c * second_c * sq_2 + 0.3
    determinant = cov_xx * cov_yy - cov_xy * cov_xy
    opacity = 1.0 / (1.0 + jnp.exp(-row(10)))
    delta_z = mean_z - camera_z
    length = jnp.sqrt(mean_x * mean_x + mean_y * mean_y + delta_z * delta_z)
    dir_x, dir_y, dir_z = (mean_x / length, mean_y / length, delta_z / length)
    sq_x, sq_y, sq_z = (dir_x * dir_x, dir_y * dir_y, dir_z * dir_z)
    prod_xy, prod_yz, prod_xz = (dir_x * dir_y, dir_y * dir_z, dir_x * dir_z)
    basis = jnp.concatenate(
        [
            coef_zero * jnp.ones_like(dir_x),
            -coef_one * dir_y,
            coef_one * dir_z,
            -coef_one * dir_x,
            coef_two[0] * prod_xy,
            coef_two[1] * prod_yz,
            coef_two[2] * (2.0 * sq_z - sq_x - sq_y),
            coef_two[3] * prod_xz,
            coef_two[4] * (sq_x - sq_y),
            coef_three[0] * dir_y * (3.0 * sq_x - sq_y),
            coef_three[1] * prod_xy * dir_z,
            coef_three[2] * dir_y * (4.0 * sq_z - sq_x - sq_y),
            coef_three[3] * dir_z * (2.0 * sq_z - 3.0 * sq_x - 3.0 * sq_y),
            coef_three[4] * dir_x * (4.0 * sq_z - sq_x - sq_y),
            coef_three[5] * dir_z * (sq_x - sq_y),
            coef_three[6] * dir_x * (sq_x - 3.0 * sq_y),
        ],
        axis=0,
    )
    colour = []
    for channel in range(3):
        weights = gauss[11 + 16 * channel : 27 + 16 * channel]
        colour.append(jnp.maximum(jnp.sum(weights * basis, axis=0, keepdims=True) + 0.5, 0.0))
    return [
        mean_x,
        mean_y,
        cov_yy / determinant,
        -cov_xy / determinant,
        cov_xx / determinant,
        opacity,
    ] + colour


def split(value, parts):
    out = []
    for _ in range(parts):
        rounded = value.astype(jnp.bfloat16)
        out.append(rounded)
        value = value - rounded.astype(jnp.float32)
    return out


def fill_table(table, halves):
    for half, ref in enumerate(halves):
        for part, value in enumerate(split(ref[...], 3)):
            table[:, part * 256 + half * LANES : part * 256 + (half + 1) * LANES] = value


def lookup(table, code):
    rows = table.shape[0] // SPLAT
    column = lax.broadcasted_iota(jnp.int32, (256, 256), 0)
    col = jnp.bitwise_and(code, 255)
    row = lax.shift_right_arithmetic(code, 8)
    hot = jnp.where(column == col, 1.0, 0.0).astype(jnp.bfloat16)
    found = jnp.dot(table[...], jnp.concatenate([hot, hot, hot], axis=0), preferred_element_type=jnp.float32)
    picked = jnp.zeros((8, 256), jnp.float32)
    rows8 = jnp.broadcast_to(row, (8, 256))
    for r in range(rows):
        picked = jnp.where(rows8 == r, found[r * 8 : (r + 1) * 8], picked)
    table_row = lax.broadcasted_iota(jnp.int32, (rows, 256), 0)
    ninth = jnp.sum(jnp.where(table_row == row, found[8 * rows :], 0.0), axis=0, keepdims=True)
    return picked, ninth


def outgoing_kernel(gauss_ref, code_ref, out_ref, table_a, table_b, table, eight):
    blocks = gauss_ref.shape[1] // LANES
    rows = blocks // 2
    for block in range(blocks):
        splat = project_chunk(gauss_ref[:, block * LANES : (block + 1) * LANES])
        ref = (table_a, table_b)[block // rows]
        r = block % rows
        ref[r * 8 : r * 8 + 8, :] = jnp.concatenate(splat[:8], axis=0)
        ref[8 * rows + r : 8 * rows + r + 1, :] = splat[8]
    fill_table(table, (table_a, table_b))

    def eight_slots(i, carry):
        where = pl.multiple_of(i * 8, 8)
        codes = code_ref[pl.ds(where, 8), :]
        found = [
            lookup(table, jnp.concatenate([codes[2 * j : 2 * j + 1], codes[2 * j + 1 : 2 * j + 2]], axis=1))
            for j in range(4)
        ]
        for j, (first, last) in enumerate(found):
            for e in range(2):
                lanes = slice(e * LANES, (e + 1) * LANES)
                eight[pl.ds(where * 8 + (2 * j + e) * 8, 8), :] = first[:, lanes]
                k = where + 2 * j + e
                eight[pl.ds((CAP + k % ROWS) * 8 + k // ROWS, 1), :] = last[:, lanes]
        return carry

    eight[CAP * 8 :, :] = jnp.zeros((eight.shape[0] - CAP * 8, LANES), jnp.float32)
    lax.fori_loop(0, CAP // 8, eight_slots, 0)
    for p in range(8):
        out_ref[pl.ds(p, LANES, stride=8), :] = jnp.transpose(eight[pl.ds(p, LANES, stride=8), :])


def outgoing_splats(gaussians, codes):
    devices = codes.shape[1]
    rows = gaussians.shape[1] // (2 * LANES)
    f32 = jnp.float32
    return pl.pallas_call(
        outgoing_kernel,
        out_shape=jax.ShapeDtypeStruct((devices * 8, LANES), f32),
        in_specs=[pl.BlockSpec(memory_space=VMEM)] * 2,
        out_specs=pl.BlockSpec(memory_space=VMEM),
        scratch_shapes=[
            VMEM((SPLAT * rows, LANES), f32),
            VMEM((SPLAT * rows, LANES), f32),
            VMEM((SPLAT * rows, 768), jnp.bfloat16),
            VMEM((8 * LANES, LANES), f32),
        ],
        compiler_params=pltpu.CompilerParams(vmem_limit_bytes=32 << 20),
        name="outgoing_splats",
    )(gaussians, codes)


def deal_kernel(out_ref, in_ref, send_sem, done_sem, local_sem):
    n_gs, n_img = lax.axis_size("gs"), lax.axis_size("img")
    devices = n_gs * n_img
    me = lax.axis_index("gs") * n_img + lax.axis_index("img")
    place = lambda d: {"gs": lax.div(d, n_img), "img": lax.rem(d, n_img)}
    barrier = pltpu.get_barrier_semaphore()

    def greet(d, carry):
        to = lax.rem(me + d, devices)
        pl.semaphore_signal(barrier, inc=1, device_id=place(to), device_id_type=pl.DeviceIdType.MESH)
        return carry

    def send(d, carry):
        to = lax.rem(me + d, devices)
        pltpu.make_async_remote_copy(
            src_ref=out_ref.at[to],
            dst_ref=in_ref.at[me],
            send_sem=send_sem,
            recv_sem=done_sem,
            device_id=place(to),
            device_id_type=pl.DeviceIdType.MESH,
        ).start()
        return carry

    lax.fori_loop(1, devices, greet, 0)
    own = pltpu.make_async_copy(out_ref.at[me], in_ref.at[me], local_sem)
    own.start()
    own.wait()
    pl.semaphore_wait(barrier, devices - 1)
    lax.fori_loop(1, devices, send, 0)
    others = pl.ds(0, devices - 1)
    pltpu.make_async_copy(out_ref.at[others], out_ref.at[others], send_sem).wait()
    pltpu.make_async_copy(in_ref.at[others], in_ref.at[others], done_sem).wait()


def deal(outgoing):
    devices = lax.axis_size("gs") * lax.axis_size("img")
    shape = (devices, 8, LANES)
    vmem = pl.BlockSpec(memory_space=VMEM)
    arrived = pl.pallas_call(
        deal_kernel,
        out_shape=jax.ShapeDtypeStruct(shape, jnp.float32),
        in_specs=[vmem],
        out_specs=vmem,
        scratch_shapes=[pltpu.SemaphoreType.DMA] * 3,
        compiler_params=pltpu.CompilerParams(collective_id=2, has_side_effects=True, vmem_limit_bytes=16 << 20),
        name="deal_splats",
    )(outgoing.reshape(shape))
    return arrived.reshape(outgoing.shape)


SEG = 32
BLOCK = 8
COEFS = 32
PIXELS = TILE * TILE
CHUNK = 64


def monomials():
    pixel = np.arange(PIXELS)
    x = (pixel % TILE) - 7.5
    y = (pixel // TILE) - 7.5
    cols = np.stack([x * x, y * y, x * y, x, y, np.ones_like(x)], axis=1)
    return np.concatenate([cols, cols, cols, np.zeros((PIXELS, COEFS - 18))], axis=1).astype(np.float32)


def lane_pick(value, index, axis):
    return jnp.take_along_axis(value, index, axis=axis, mode="promise_in_bounds")


def blend_kernel(cols_here, first, base, arrived, lists, owner, mono, out_ref,
                 table_a, table_b, table, packed, codes, params, coefs, power_a, power_b, state, total_ref,
                 carry_ref, carry_owner):
    tiles = first.shape[0] - 1
    runs = lists.shape[0] // tiles
    groups = (first[tiles] + LANES - 1) // LANES
    per_group = SEG // BLOCK

    for p in range(8):
        flat = jnp.transpose(arrived[pl.ds(p, LANES, stride=8), :])
        for half, ref in enumerate((table_a, table_b)):
            ref[pl.ds(p, ROWS, stride=8), :] = flat[half * ROWS : (half + 1) * ROWS]
            if p == half:
                ref[8 * ROWS :, :] = flat[CAP : CAP + ROWS]
    fill_table(table, (table_a, table_b))

    packed[...] = jnp.full(packed.shape, -1, jnp.int32)
    for t in range(tiles):
        packed[pl.ds(first[t], runs), :] = lists[t * runs : (t + 1) * runs, :]

    def turn(g, carry):
        lanes = jnp.transpose(packed[pl.ds(pl.multiple_of(g * LANES, LANES), LANES), :])
        codes[pl.ds(pl.multiple_of(g * SEG, SEG), SEG), :] = lanes[0:SEG]
        return carry

    lax.fori_loop(0, groups, turn, 0)
    total_ref[...] = jnp.zeros_like(total_ref)
    carry_ref[...] = jnp.ones_like(carry_ref)
    carry_owner[...] = jnp.full(carry_owner.shape, -1, jnp.int32)

    def look(block, j):
        where = block * BLOCK + 2 * j
        code = jnp.concatenate([codes[pl.ds(where, 1), :], codes[pl.ds(where + 1, 1), :]], axis=1)
        return ((block % 3) * 72,) + lookup(table, code)

    def keep(j, slot, picked, ninth):
        for e in range(2):
            lanes = slice(e * LANES, (e + 1) * LANES)
            params[pl.ds(pl.multiple_of(slot + (2 * j + e) * 8, 8), 8), :] = picked[:, lanes]
            params[pl.ds(slot + 64 + 2 * j + e, 1), :] = ninth[:, lanes]

    def expand(block):
        slot = (block % 3) * 72
        m_x, m_y, a, b, c, o = [params[pl.ds(slot + p, BLOCK, stride=8), :] for p in range(6)]
        live = codes[pl.ds(pl.multiple_of(block * BLOCK, BLOCK), BLOCK), :] >= 0
        tile = owner[pl.ds(block // per_group, 1), :]
        tile_y = lax.shift_right_logical(tile, cols_here.bit_length() - 1)
        tile_x = jnp.bitwise_and(tile, cols_here - 1)
        u = m_x - (tile_x * TILE + base[0]).astype(jnp.float32)
        v = m_y - (tile_y * TILE + base[1]).astype(jnp.float32)
        level = LOG2E * (-0.5 * (a * u * u + c * v * v) - b * u * v)
        values = [
            (-0.5 * LOG2E) * a,
            (-0.5 * LOG2E) * c,
            -LOG2E * b,
            LOG2E * (a * u + b * v),
            LOG2E * (c * v + b * u),
            jnp.where(live, level + jnp.log2(o), -1e30),
        ]
        for i, value in enumerate(values):
            for part, rounded in enumerate(split(value, 3)):
                coefs[pl.ds(part * 6 + i, BLOCK, stride=COEFS), :] = rounded.astype(jnp.float32)

    def exponents(j):
        pair = [
            coefs[pl.ds((2 * j + e) * COEFS, COEFS), :].astype(jnp.bfloat16) for e in range(2)
        ]
        return jnp.dot(mono[...], jnp.concatenate(pair, axis=1), preferred_element_type=jnp.float32)

    def blend(block, j, power):
        slot = (block % 3) * 72
        at = lambda q, i: pl.ds(q * PIXELS + j * CHUNK + i * 8, 8)
        pieces = range(CHUNK // 8)
        left = [state[at(0, i), :] for i in pieces]
        colour = [[state[at(1 + ch, i), :] for i in pieces] for ch in range(3)]
        for k in range(BLOCK):
            rows = (slot + k * 8 + 6, slot + k * 8 + 7, slot + 64 + k)
            tints = [jnp.broadcast_to(params[pl.ds(r, 1), :], (8, LANES)) for r in rows]
            for i in pieces:
                alpha = jnp.exp2(power[k // 2, at(0, i), (k % 2) * LANES : (k % 2 + 1) * LANES])
                weight = left[i] * alpha
                left[i] = left[i] - weight
                for ch in range(3):
                    colour[ch][i] = colour[ch][i] + weight * tints[ch]
        for i in pieces:
            state[at(0, i), :] = left[i]
            for ch in range(3):
                state[at(1 + ch, i), :] = colour[ch][i]

    lane = lax.broadcasted_iota(jnp.int32, (8, LANES), 1)

    def flush(g):
        tile = jnp.broadcast_to(owner[pl.ds(g, 1), :], (8, LANES))
        left = state[0:PIXELS, :]
        same = []
        for d in (1, 2, 4, 8):
            same.append(((pltpu.roll(tile, d, 1) == tile) & (lane >= d))[0:1])
        for d, mask in zip((1, 2, 4, 8), same):
            left = left * jnp.where(mask, pltpu.roll(left, d, 1), 1.0)
        before = jnp.where(same[0], pltpu.roll(left, 1, 1), 1.0)
        goes_on = (tile == carry_owner[...])[0:1]
        behind = jnp.where(goes_on, carry_ref[...], 1.0)
        before = before * behind
        carry_ref[...] = jnp.broadcast_to((left * behind)[:, LANES - 1 :], (PIXELS, LANES))
        carry_owner[...] = jnp.broadcast_to(tile[:, LANES - 1 :], (8, LANES))
        member = lax.broadcasted_iota(jnp.int32, (tiles, LANES), 0) == tile[0:1]
        member = jnp.where(member, 1.0, 0.0).astype(jnp.bfloat16)
        member = jnp.concatenate([member, member], axis=1)
        for ch in range(3):
            part = before * state[(1 + ch) * PIXELS : (2 + ch) * PIXELS, :]
            pair = jnp.concatenate(split(part, 2), axis=1)
            total_ref[ch] += lax.dot_general(
                member, pair, (((1,), (1,)), ((), ())), preferred_element_type=jnp.float32
            )

    coefs[...] = jnp.zeros_like(coefs)
    steps = BLOCK // 2

    def look_ahead(block):
        for j, found in enumerate([look(block, j) for j in range(steps)]):
            keep(j, *found)
        expand(block)

    look_ahead(0)
    for j in range(steps):
        power_a[j] = exponents(j)
    look_ahead(1)

    def one_group(g, carry):
        state[0:PIXELS, :] = jnp.ones((PIXELS, LANES), jnp.float32)
        state[PIXELS:, :] = jnp.zeros((3 * PIXELS, LANES), jnp.float32)

        def two_blocks(i, carry):
            for which in range(2):
                block = g * per_group + 2 * i + which
                now, later = ((power_a, power_b), (power_b, power_a))[which]

                found = [look(block + 2, j) for j in range(steps)]
                for j in range(steps):
                    later[j] = exponents(j)
                for j in range(steps):
                    blend(block, j, now)
                for j in range(steps):
                    keep(j, *found[j])
                expand(block + 2)
            return carry

        lax.fori_loop(0, per_group // 2, two_blocks, 0)
        flush(g)
        return carry

    lax.fori_loop(0, groups, one_group, 0)

    piece = lax.broadcasted_iota(jnp.int32, (8, LANES), 1)
    inner, outer = piece % TILE, piece // TILE
    sub = lax.broadcasted_iota(jnp.int32, (8, LANES), 0)
    skew = (outer + 8 - sub) % 8 * TILE + inner
    down = (outer + 8 - sub) % 8
    back = (outer + sub) % 8 * TILE + inner
    for ch in range(3):
        for r in range(tiles // cols_here):
            for q in range(cols_here // 8):
                for h in range(2):
                    x = total_ref[ch, r * cols_here + q * 8 : r * cols_here + q * 8 + 8, h * LANES : (h + 1) * LANES]
                    x = lane_pick(lane_pick(lane_pick(x, skew, 1), down, 0), back, 1)
                    out_ref[ch, r * TILE + h * 8 : r * TILE + h * 8 + 8, q * LANES : (q + 1) * LANES] = x


def blend_tiles(first, base, arrived, lists, owner, cols_here):
    tiles = first.shape[0] - 1
    most = lists.shape[0] // LANES
    smem = pl.BlockSpec(memory_space=pltpu.SMEM)
    vmem = pl.BlockSpec(memory_space=VMEM)
    f32 = jnp.float32
    return pl.pallas_call(
        functools.partial(blend_kernel, cols_here),
        out_shape=jax.ShapeDtypeStruct((3, tiles // cols_here * TILE, cols_here * TILE), f32),
        in_specs=[smem] * 2 + [vmem] * 4,
        out_specs=vmem,
        scratch_shapes=[
            VMEM((9 * ROWS, LANES), f32),
            VMEM((9 * ROWS, LANES), f32),
            VMEM((9 * ROWS, 768), jnp.bfloat16),
            VMEM((lists.shape[0] + LANES, LANES), jnp.int32),
            VMEM(((most + 1) * SEG, LANES), jnp.int32),
            VMEM((3 * 72, LANES), f32),
            VMEM((BLOCK * COEFS, LANES), f32),
            VMEM((BLOCK // 2, PIXELS, 256), f32),
            VMEM((BLOCK // 2, PIXELS, 256), f32),
            VMEM((4 * PIXELS, LANES), f32),
            VMEM((3, tiles, PIXELS), f32),
            VMEM((PIXELS, LANES), f32),
            VMEM((8, LANES), jnp.int32),
        ],
        compiler_params=pltpu.CompilerParams(vmem_limit_bytes=48 << 20),
        name="blend_tiles",
    )(first, base, arrived, lists, owner, jnp.asarray(monomials()).astype(jnp.bfloat16))


def arrange(tile_lists):
    rows_here, cols_here, list_len = tile_lists.shape
    tiles = rows_here * cols_here
    lists = tile_lists.reshape(tiles, list_len)
    runs = list_len // SEG
    live = (jnp.sum((lists >= 0).astype(jnp.int32), axis=1) + SEG - 1) // SEG
    number = jnp.arange(tiles, dtype=jnp.int32)
    ends = jnp.sum(jnp.where(number[None, :] <= number[:, None], live[None, :], 0), axis=1).astype(jnp.int32)
    first = jnp.concatenate([jnp.zeros((1,), jnp.int32), ends])
    most = tiles * runs
    segment = jnp.arange(most + LANES, dtype=jnp.int32)
    owner = jnp.sum((ends[None, :] <= segment[:, None]).astype(jnp.int32), axis=1).reshape(-1, LANES)
    slot, source = lists % CAP, lists // CAP
    code = jnp.where(lists >= 0, slot % ROWS * 256 + slot // ROWS * LANES + source, -1)
    code = jnp.pad(code.reshape(most, SEG), ((0, 0), (0, LANES - SEG)), constant_values=-1)
    half = TILE // 2
    base = jnp.stack(
        [lax.axis_index("gs") * (cols_here * TILE) + half, lax.axis_index("img") * (rows_here * TILE) + half]
    ).astype(jnp.int32)
    return first, base, code, owner


EDGE = 8
TAPS = 5


def halo_kernel(rendered, truth, row_out, col_out, row_buf, col_buf, row_sem, col_sem, row_done, col_done):
    n_gs, n_img = lax.axis_size("gs"), lax.axis_size("img")
    g, i = lax.axis_index("gs"), lax.axis_index("img")
    place = lambda dg, di: {"gs": lax.rem(g + n_gs + dg, n_gs), "img": lax.rem(i + n_img + di, n_img)}
    around = [(dg, di) for dg in (-1, 0, 1) for di in (-1, 0, 1) if (dg, di) != (0, 0)]
    barrier = pltpu.get_barrier_semaphore()
    for dg, di in around:
        pl.semaphore_signal(barrier, inc=1, device_id=place(dg, di), device_id_type=pl.DeviceIdType.MESH)

    height, width = rendered.shape[1:]
    for c in range(6):
        source = (rendered, truth)[c // 3]
        image = source[c % 3]
        for side in range(2):
            edge = image[0:EDGE] if side == 0 else image[height - EDGE :]
            for half in range(2):
                row_buf[side, c, half] = edge[:, half * LANES : (half + 1) * LANES]
            columns = image[:, 0:LANES] if side == 0 else image[:, width - LANES :]
            turned = jnp.transpose(columns)
            col_buf[side, c] = turned[0:EDGE] if side == 0 else turned[LANES - EDGE :]

    pl.semaphore_wait(barrier, len(around))
    copies = []
    for side in range(2):
        step = -1 if side == 0 else 1
        copies.append(
            pltpu.make_async_remote_copy(
                src_ref=row_buf.at[side],
                dst_ref=row_out.at[side],
                send_sem=row_sem.at[side],
                recv_sem=row_done.at[side],
                device_id=place(0, step),
                device_id_type=pl.DeviceIdType.MESH,
            )
        )
        for di in (-1, 0, 1):
            copies.append(
                pltpu.make_async_remote_copy(
                    src_ref=col_buf.at[side],
                    dst_ref=col_out.at[side * 3 + di + 1],
                    send_sem=col_sem.at[side * 3 + di + 1],
                    recv_sem=col_done.at[side * 3 + di + 1],
                    device_id=place(step, di),
                    device_id_type=pl.DeviceIdType.MESH,
                )
            )
    for copy in copies:
        copy.start()
    for copy in copies:
        copy.wait()


def exchange_halos(rendered, truth):
    vmem = pl.BlockSpec(memory_space=VMEM)
    rows = (2, 6, 2, EDGE, LANES)
    f32 = jnp.float32
    return pl.pallas_call(
        halo_kernel,
        out_shape=(jax.ShapeDtypeStruct(rows, f32), jax.ShapeDtypeStruct((6, 6, EDGE, LANES), f32)),
        in_specs=[vmem] * 2,
        out_specs=(vmem, vmem),
        scratch_shapes=[
            VMEM(rows, f32),
            VMEM((2, 6, EDGE, LANES), f32),
            pltpu.SemaphoreType.DMA((2,)),
            pltpu.SemaphoreType.DMA((6,)),
            pltpu.SemaphoreType.DMA((2,)),
            pltpu.SemaphoreType.DMA((6,)),
        ],
        compiler_params=pltpu.CompilerParams(collective_id=1, has_side_effects=True, vmem_limit_bytes=16 << 20),
        name="exchange_halos",
    )(rendered, truth)


def window():
    offsets = np.arange(11, dtype=np.float32) - 5.0
    weights = np.exp(-offsets * offsets / np.float32(4.5))
    return [float(w) for w in weights / np.sum(weights)]


def loss_kernel(has, rendered, truth, rows, cols, out_ref, maps):
    height = rendered.shape[1]
    tall = height + 2 * EDGE
    start = lambda q, part: (q * 3 + part) * tall
    left, right, above, below = [has[n] > 0 for n in range(4)]
    keep = lambda flag, value: jnp.where(flag, value, 0.0)
    lane = lax.broadcasted_iota(jnp.int32, (EDGE, LANES), 1)
    gap = jnp.zeros((LANES - 2 * EDGE, LANES), jnp.float32)
    for c in range(6):
        image = (rendered, truth)[c // 3]
        for half in range(2):
            base = start(c, half)
            maps[base : base + EDGE, :] = keep(above, rows[1, c, half])
            maps[base + EDGE : base + EDGE + height, :] = image[c % 3, :, half * LANES : (half + 1) * LANES]
            maps[base + EDGE + height : base + tall, :] = keep(below, rows[0, c, half])
        base = start(c, 2)
        after = keep(right, cols[1, c])
        before = keep(left, cols[4, c])
        maps[base + EDGE : base + EDGE + height, :] = jnp.transpose(jnp.concatenate([after, gap, before], axis=0))
        mixed = []
        for flag, side in ((right, 0), (left, 3)):
            upper = keep(flag & above, cols[side + 2, c])
            lower = keep(flag & below, cols[side + 0, c])
            mixed.append(jnp.where(lane < LANES // 2, lower, upper))
        turned = jnp.transpose(jnp.concatenate([mixed[0], gap, mixed[1]], axis=0))
        maps[base : base + EDGE, :] = turned[LANES - EDGE :]
        maps[base + EDGE + height : base + tall, :] = turned[0:EDGE]

    def products(n, carry):
        for ch in range(3):
            for part in range(3):
                at = lambda q: pl.ds(pl.multiple_of(start(q + ch, part) + n * 8, 8), 8)
                r, t = maps[at(0), :], maps[at(3), :]
                maps[at(6), :] = r * r + t * t
                maps[at(9), :] = r * t
        return carry

    lax.fori_loop(0, tall // 8, products, 0)
    weights = window()

    def filtered(q, n):
        parts = []
        for part in range(3):
            row = lambda d: maps[pl.ds(start(q, part) + EDGE + n * 8 + d, 8), :]
            total = weights[TAPS] * row(0)
            for d in range(1, TAPS + 1):
                total = total + weights[TAPS + d] * (row(d) + row(-d))
            parts.append(total)
        first, second, outside = parts
        sums = [weights[TAPS] * first, weights[TAPS] * second]
        for d in range(1, TAPS + 1):
            ahead = [pltpu.roll(x, LANES - d, 1) for x in (first, second, outside)]
            back = [pltpu.roll(x, d, 1) for x in (outside, first, second)]
            inside_ahead, inside_back = lane < LANES - d, lane >= d
            for half in range(2):
                pair = jnp.where(inside_ahead, ahead[half], ahead[half + 1])
                pair = pair + jnp.where(inside_back, back[half + 1], back[half])
                sums[half] = sums[half] + weights[TAPS + d] * pair
        return sums

    def one_block(n, carry):
        difference = [0.0, 0.0]
        alike = [0.0, 0.0]
        where = pl.ds(pl.multiple_of(n * 8, 8), 8)
        for ch in range(3):
            means_r, means_t, squares, products_rt = [filtered(q + ch, n) for q in (0, 3, 6, 9)]
            for half in range(2):
                mean_r, mean_t = means_r[half], means_t[half]
                both = mean_r * mean_t
                squared = mean_r * mean_r + mean_t * mean_t
                above_line = (2.0 * both + stable_one) * (2.0 * (products_rt[half] - both) + stable_two)
                below_line = (squared + stable_one) * (squares[half] - squared + stable_two)
                alike[half] = alike[half] + above_line / below_line
                at = pl.ds(pl.multiple_of(start(ch, half) + EDGE + n * 8, 8), 8)
                at_t = pl.ds(pl.multiple_of(start(ch + 3, half) + EDGE + n * 8, 8), 8)
                difference[half] = difference[half] + jnp.abs(maps[at, :] - maps[at_t, :])
        for half in range(2):
            out_ref[where, half * LANES : (half + 1) * LANES] = (1.0 - ssim_share) * (
                difference[half] * (1.0 / 3.0)
            ) + ssim_share * (1.0 - alike[half] * (1.0 / 3.0))
        return carry

    lax.fori_loop(0, height // 8, one_block, 0)


def pixel_loss(has, rendered, truth, rows, cols):
    vmem = pl.BlockSpec(memory_space=VMEM)
    height, width = rendered.shape[1:]
    return pl.pallas_call(
        loss_kernel,
        out_shape=jax.ShapeDtypeStruct((height, width), jnp.float32),
        in_specs=[pl.BlockSpec(memory_space=pltpu.SMEM)] + [vmem] * 4,
        out_specs=vmem,
        scratch_shapes=[VMEM((12 * 3 * (height + 2 * EDGE), LANES), jnp.float32)],
        compiler_params=pltpu.CompilerParams(vmem_limit_bytes=32 << 20),
        name="pixel_loss",
    )(has, rendered, truth, rows, cols)


def on_device(gaussians, send_slots, tile_lists, truth):
    rows_here, cols_here, list_len = tile_lists.shape
    devices = send_slots.shape[1] // CAP
    half = gaussians.shape[1] // 2
    picks = send_slots.reshape(devices, CAP).T
    codes = picks % half // LANES * 256 + picks // half * LANES + picks % LANES
    arrived = deal(outgoing_splats(gaussians, codes))
    first, base, code, owner = arrange(tile_lists)
    rendered = blend_tiles(first, base, arrived, code, owner, cols_here)
    rows, cols = exchange_halos(rendered, truth)
    g, i = lax.axis_index("gs"), lax.axis_index("img")
    has = jnp.stack([g > 0, g < lax.axis_size("gs") - 1, i > 0, i < lax.axis_size("img") - 1]).astype(jnp.int32)
    return (rendered, pixel_loss(has, rendered, truth, rows, cols))


def solution(mesh):
    return jax.shard_map(
        on_device,
        mesh=mesh,
        in_specs=(
            P(None, ("gs", "img")),
            P(("gs", "img"), None),
            P("img", "gs", None),
            P(None, "img", "gs"),
        ),
        out_specs=(P(None, "img", "gs"), P("img", "gs")),
        check_vma=False,
    )
```

```python
import functools
import math

import jax
import jax.numpy as jnp
import numpy as np
from jax import lax
from jax.experimental import pallas as pl
from jax.experimental.pallas import tpu as pltpu
from jax.sharding import PartitionSpec as P

TILE = 16
LANES = 128
CAP = 80
SPLAT = 9
ROWS = CAP // 2
LOG2E = 1.0 / math.log(2.0)
VMEM = pltpu.VMEM


coef_zero = 0.28209479177387814
coef_one = 0.4886025119029199
coef_two = [
    1.0925484305920792,
    -1.0925484305920792,
    0.31539156525252005,
    -1.0925484305920792,
    0.5462742152960396,
]
coef_three = [
    -0.5900435899266435,
    2.890611442640554,
    -0.4570457994644658,
    0.3731763325901154,
    -0.4570457994644658,
    1.445305721320277,
    -0.5900435899266435,
]
camera_z = -3000.0
ssim_share = 0.2
stable_one = 0.0001
stable_two = 0.0009


def project_chunk(gauss):
    row = lambda i: gauss[i : i + 1]
    mean_x, mean_y, mean_z = (row(0), row(1), row(2))
    squared = jnp.exp(2.0 * gauss[3:6])
    sq_0, sq_1, sq_2 = (squared[0:1], squared[1:2], squared[2:3])
    inv = 1.0 / jnp.sqrt(row(6) * row(6) + row(7) * row(7) + row(8) * row(8) + row(9) * row(9))
    quat_w, quat_x, quat_y, quat_z = (row(6) * inv, row(7) * inv, row(8) * inv, row(9) * inv)
    first_a = 1.0 - 2.0 * (quat_y * quat_y + quat_z * quat_z)
    first_b = 2.0 * (quat_x * quat_y - quat_w * quat_z)
    first_c = 2.0 * (quat_x * quat_z + quat_w * quat_y)
    second_a = 2.0 * (quat_x * quat_y + quat_w * quat_z)
    second_b = 1.0 - 2.0 * (quat_x * quat_x + quat_z * quat_z)
    second_c = 2.0 * (quat_y * quat_z - quat_w * quat_x)
    cov_xx = first_a * first_a * sq_0 + first_b * first_b * sq_1 + first_c * first_c * sq_2 + 0.3
    cov_xy = first_a * second_a * sq_0 + first_b * second_b * sq_1 + first_c * second_c * sq_2
    cov_yy = second_a * second_a * sq_0 + second_b * second_b * sq_1 + second_c * second_c * sq_2 + 0.3
    determinant = cov_xx * cov_yy - cov_xy * cov_xy
    opacity = 1.0 / (1.0 + jnp.exp(-row(10)))
    delta_z = mean_z - camera_z
    length = jnp.sqrt(mean_x * mean_x + mean_y * mean_y + delta_z * delta_z)
    dir_x, dir_y, dir_z = (mean_x / length, mean_y / length, delta_z / length)
    sq_x, sq_y, sq_z = (dir_x * dir_x, dir_y * dir_y, dir_z * dir_z)
    prod_xy, prod_yz, prod_xz = (dir_x * dir_y, dir_y * dir_z, dir_x * dir_z)
    basis = jnp.concatenate(
        [
            coef_zero * jnp.ones_like(dir_x),
            -coef_one * dir_y,
            coef_one * dir_z,
            -coef_one * dir_x,
            coef_two[0] * prod_xy,
            coef_two[1] * prod_yz,
            coef_two[2] * (2.0 * sq_z - sq_x - sq_y),
            coef_two[3] * prod_xz,
            coef_two[4] * (sq_x - sq_y),
            coef_three[0] * dir_y * (3.0 * sq_x - sq_y),
            coef_three[1] * prod_xy * dir_z,
            coef_three[2] * dir_y * (4.0 * sq_z - sq_x - sq_y),
            coef_three[3] * dir_z * (2.0 * sq_z - 3.0 * sq_x - 3.0 * sq_y),
            coef_three[4] * dir_x * (4.0 * sq_z - sq_x - sq_y),
            coef_three[5] * dir_z * (sq_x - sq_y),
            coef_three[6] * dir_x * (sq_x - 3.0 * sq_y),
        ],
        axis=0,
    )
    colour = []
    for channel in range(3):
        weights = gauss[11 + 16 * channel : 27 + 16 * channel]
        colour.append(jnp.maximum(jnp.sum(weights * basis, axis=0, keepdims=True) + 0.5, 0.0))
    return [
        mean_x,
        mean_y,
        cov_yy / determinant,
        -cov_xy / determinant,
        cov_xx / determinant,
        opacity,
    ] + colour


def split(value, parts):
    out = []
    for _ in range(parts):
        rounded = value.astype(jnp.bfloat16)
        out.append(rounded)
        value = value - rounded.astype(jnp.float32)
    return out


def fill_table(table, third, halves):
    rows = third.shape[0] // 2
    for half, ref in enumerate(halves):
        lanes = slice(half * LANES, (half + 1) * LANES)
        for part, value in enumerate(split(ref[...], 2)):
            table[:, part * 256 + half * LANES : part * 256 + (half + 1) * LANES] = value
        for p in range(2):
            third[p * rows : (p + 1) * rows, lanes] = split(ref[pl.ds(p, rows, stride=8), :], 3)[2]


def lookup(table, third, code):
    rows = table.shape[0] // SPLAT
    column = lax.broadcasted_iota(jnp.int32, (256, 256), 0)
    col = jnp.bitwise_and(code, 255)
    row = lax.shift_right_arithmetic(code, 8)
    hot = jnp.where(column == col, 1.0, 0.0).astype(jnp.bfloat16)
    found = jnp.dot(table[...], jnp.concatenate([hot, hot], axis=0), preferred_element_type=jnp.float32)
    finer = jnp.dot(third[...], hot, preferred_element_type=jnp.float32)
    picked = jnp.zeros((8, 256), jnp.float32)
    rows8 = jnp.broadcast_to(row, (8, 256))
    for r in range(rows):
        picked = jnp.where(rows8 == r, found[r * 8 : (r + 1) * 8], picked)
    table_row = lax.broadcasted_iota(jnp.int32, (rows, 256), 0)
    choose = lambda lines: jnp.sum(jnp.where(table_row == row, lines, 0.0), axis=0, keepdims=True)
    sub = lax.broadcasted_iota(jnp.int32, (8, 256), 0)
    for p in range(2):
        picked = picked + jnp.where(sub == p, choose(finer[p * rows : (p + 1) * rows]), 0.0)
    return picked, choose(found[8 * rows :])


def outgoing_kernel(gauss_ref, pick_ref, out_ref, table_a, table_b, table, third, eight):
    blocks = gauss_ref.shape[1] // LANES
    rows = blocks // 2
    for block in range(blocks):
        splat = project_chunk(gauss_ref[:, block * LANES : (block + 1) * LANES])
        ref = (table_a, table_b)[block // rows]
        r = block % rows
        ref[r * 8 : r * 8 + 8, :] = jnp.concatenate(splat[:8], axis=0)
        ref[8 * rows + r : 8 * rows + r + 1, :] = splat[8]
    fill_table(table, third, (table_a, table_b))

    def eight_slots(i, carry):
        where = pl.multiple_of(i * 8, 8)
        picks = pick_ref[pl.ds(where, 8), :]
        block = lax.shift_right_logical(picks, 7)
        codes = jnp.bitwise_and(picks, LANES - 1) + jnp.where(block < rows, block * 256, (block - rows) * 256 + LANES)
        found = [
            lookup(table, third, jnp.concatenate([codes[2 * j : 2 * j + 1], codes[2 * j + 1 : 2 * j + 2]], axis=1))
            for j in range(4)
        ]
        for j, (first, last) in enumerate(found):
            for e in range(2):
                lanes = slice(e * LANES, (e + 1) * LANES)
                eight[pl.ds(where * 8 + (2 * j + e) * 8, 8), :] = first[:, lanes]
                k = where + 2 * j + e
                eight[pl.ds((CAP + k % ROWS) * 8 + k // ROWS, 1), :] = last[:, lanes]
        return carry

    eight[CAP * 8 :, :] = jnp.zeros((eight.shape[0] - CAP * 8, LANES), jnp.float32)
    lax.fori_loop(0, CAP // 8, eight_slots, 0)
    for p in range(8):
        out_ref[pl.ds(p, LANES, stride=8), :] = jnp.transpose(eight[pl.ds(p, LANES, stride=8), :])


def deal_kernel(gauss_ref, pick_ref, in_ref, out_ref, send_sem, done_sem, local_sem, *scratch):
    n_gs, n_img = lax.axis_size("gs"), lax.axis_size("img")
    devices = n_gs * n_img
    me = lax.axis_index("gs") * n_img + lax.axis_index("img")
    place = lambda d: {"gs": lax.div(d, n_img), "img": lax.rem(d, n_img)}
    block = lambda d: pl.ds(pl.multiple_of(d * 8, 8), 8)
    barrier = pltpu.get_barrier_semaphore()

    def greet(d, carry):
        to = lax.rem(me + d, devices)
        pl.semaphore_signal(barrier, inc=1, device_id=place(to), device_id_type=pl.DeviceIdType.MESH)
        return carry

    def send(d, carry):
        to = lax.rem(me + d, devices)
        pltpu.make_async_remote_copy(
            src_ref=out_ref.at[block(to)],
            dst_ref=in_ref.at[block(me)],
            send_sem=send_sem,
            recv_sem=done_sem,
            device_id=place(to),
            device_id_type=pl.DeviceIdType.MESH,
        ).start()
        return carry

    lax.fori_loop(1, devices, greet, 0)
    outgoing_kernel(gauss_ref, pick_ref, out_ref, *scratch)
    own = pltpu.make_async_copy(out_ref.at[block(me)], in_ref.at[block(me)], local_sem)
    own.start()
    own.wait()
    pl.semaphore_wait(barrier, devices - 1)
    lax.fori_loop(1, devices, send, 0)
    others = pl.ds(0, (devices - 1) * 8)
    pltpu.make_async_copy(out_ref.at[others], out_ref.at[others], send_sem).wait()
    pltpu.make_async_copy(in_ref.at[others], in_ref.at[others], done_sem).wait()


def deal(gaussians, picks):
    devices = picks.shape[1]
    rows = gaussians.shape[1] // (2 * LANES)
    vmem = pl.BlockSpec(memory_space=VMEM)
    f32 = jnp.float32
    return pl.pallas_call(
        deal_kernel,
        out_shape=jax.ShapeDtypeStruct((devices * 8, LANES), f32),
        in_specs=[vmem] * 2,
        out_specs=vmem,
        scratch_shapes=[VMEM((devices * 8, LANES), f32)]
        + [pltpu.SemaphoreType.DMA] * 3
        + [
            VMEM((SPLAT * rows, LANES), f32),
            VMEM((SPLAT * rows, LANES), f32),
            VMEM((SPLAT * rows, 512), jnp.bfloat16),
            VMEM((2 * rows, 256), jnp.bfloat16),
            VMEM((8 * LANES, LANES), f32),
        ],
        compiler_params=pltpu.CompilerParams(collective_id=2, has_side_effects=True, vmem_limit_bytes=32 << 20),
        name="deal_splats",
    )(gaussians, picks)


SEG = 32
BLOCK = 8
COEFS = 32
PIXELS = TILE * TILE
CHUNK = 64


def monomials():
    pixel = np.arange(PIXELS)
    x = (pixel % TILE) - 7.5
    y = (pixel // TILE) - 7.5
    cols = np.stack([x * x, y * y, x * y, x, y, np.ones_like(x)], axis=1)
    return np.concatenate([cols, cols, cols, np.zeros((PIXELS, COEFS - 18))], axis=1).astype(np.float32)


def lane_pick(value, index, axis):
    return jnp.take_along_axis(value, index, axis=axis, mode="promise_in_bounds")


def blend_kernel(cols_here, first, base, arrived, lists, owner, mono, out_ref,
                 table_a, table_b, table, third, packed, codes, params, coefs, power_a, power_b, state, total_ref,
                 carry_ref, carry_owner):
    tiles = first.shape[0] - 1
    runs = lists.shape[0] // tiles
    groups = (first[tiles] + LANES - 1) // LANES
    per_group = SEG // BLOCK

    for p in range(8):
        flat = jnp.transpose(arrived[pl.ds(p, LANES, stride=8), :])
        for half, ref in enumerate((table_a, table_b)):
            ref[pl.ds(p, ROWS, stride=8), :] = flat[half * ROWS : (half + 1) * ROWS]
            if p == half:
                ref[8 * ROWS :, :] = flat[CAP : CAP + ROWS]
    fill_table(table, third, (table_a, table_b))

    packed[...] = jnp.full(packed.shape, -1, jnp.int32)
    for t in range(tiles):
        packed[pl.ds(first[t], runs), :] = lists[t * runs : (t + 1) * runs, :]

    def turn(g, carry):
        lanes = jnp.transpose(packed[pl.ds(pl.multiple_of(g * LANES, LANES), LANES), :])
        slot = lanes[0:SEG]
        source = ((slot.astype(jnp.float32) + 0.5) * (1.0 / CAP)).astype(jnp.int32)
        k = slot - source * CAP
        code = source + jnp.where(k < ROWS, k * 256, (k - ROWS) * 256 + LANES)
        codes[pl.ds(pl.multiple_of(g * SEG, SEG), SEG), :] = jnp.where(slot >= 0, code, -1)
        return carry

    lax.fori_loop(0, groups, turn, 0)
    total_ref[...] = jnp.zeros_like(total_ref)
    carry_ref[...] = jnp.ones_like(carry_ref)
    carry_owner[...] = jnp.full(carry_owner.shape, -1, jnp.int32)

    def look(block, j):
        where = block * BLOCK + 2 * j
        code = jnp.concatenate([codes[pl.ds(where, 1), :], codes[pl.ds(where + 1, 1), :]], axis=1)
        return ((block % 3) * 72,) + lookup(table, third, code)

    def keep(j, slot, picked, ninth):
        for e in range(2):
            lanes = slice(e * LANES, (e + 1) * LANES)
            params[pl.ds(pl.multiple_of(slot + (2 * j + e) * 8, 8), 8), :] = picked[:, lanes]
            params[pl.ds(slot + 64 + 2 * j + e, 1), :] = ninth[:, lanes]

    def expand(block):
        slot = (block % 3) * 72
        m_x, m_y, a, b, c, o = [params[pl.ds(slot + p, BLOCK, stride=8), :] for p in range(6)]
        live = codes[pl.ds(pl.multiple_of(block * BLOCK, BLOCK), BLOCK), :] >= 0
        tile = owner[pl.ds(block // per_group, 1), :]
        tile_y = lax.shift_right_logical(tile, cols_here.bit_length() - 1)
        tile_x = jnp.bitwise_and(tile, cols_here - 1)
        u = m_x - (tile_x * TILE + base[0]).astype(jnp.float32)
        v = m_y - (tile_y * TILE + base[1]).astype(jnp.float32)
        level = LOG2E * (-0.5 * (a * u * u + c * v * v) - b * u * v)
        values = [
            (-0.5 * LOG2E) * a,
            (-0.5 * LOG2E) * c,
            -LOG2E * b,
            LOG2E * (a * u + b * v),
            LOG2E * (c * v + b * u),
            jnp.where(live, level + jnp.log2(o), -1e30),
        ]
        for i, value in enumerate(values):
            for part, rounded in enumerate(split(value, 3)):
                coefs[pl.ds(part * 6 + i, BLOCK, stride=COEFS), :] = rounded.astype(jnp.float32)

    def exponents(j):
        pair = [
            coefs[pl.ds((2 * j + e) * COEFS, COEFS), :].astype(jnp.bfloat16) for e in range(2)
        ]
        return jnp.dot(mono[...], jnp.concatenate(pair, axis=1), preferred_element_type=jnp.float32)

    def blend(block, j, power):
        slot = (block % 3) * 72
        at = lambda q, i: pl.ds(q * PIXELS + j * CHUNK + i * 8, 8)
        pieces = range(CHUNK // 8)
        left = [state[at(0, i), :] for i in pieces]
        colour = [[state[at(1 + ch, i), :] for i in pieces] for ch in range(3)]
        for k in range(BLOCK):
            rows = (slot + k * 8 + 6, slot + k * 8 + 7, slot + 64 + k)
            tints = [jnp.broadcast_to(params[pl.ds(r, 1), :], (8, LANES)) for r in rows]
            for i in pieces:
                alpha = jnp.exp2(power[k // 2, at(0, i), (k % 2) * LANES : (k % 2 + 1) * LANES])
                weight = left[i] * alpha
                left[i] = left[i] - weight
                for ch in range(3):
                    colour[ch][i] = colour[ch][i] + weight * tints[ch]
        for i in pieces:
            state[at(0, i), :] = left[i]
            for ch in range(3):
                state[at(1 + ch, i), :] = colour[ch][i]

    lane = lax.broadcasted_iota(jnp.int32, (8, LANES), 1)

    def flush(g):
        tile = jnp.broadcast_to(owner[pl.ds(g, 1), :], (8, LANES))
        left = state[0:PIXELS, :]
        same = []
        for d in (1, 2, 4, 8):
            same.append(((pltpu.roll(tile, d, 1) == tile) & (lane >= d))[0:1])
        for d, mask in zip((1, 2, 4, 8), same):
            left = left * jnp.where(mask, pltpu.roll(left, d, 1), 1.0)
        before = jnp.where(same[0], pltpu.roll(left, 1, 1), 1.0)
        goes_on = (tile == carry_owner[...])[0:1]
        behind = jnp.where(goes_on, carry_ref[...], 1.0)
        before = before * behind
        carry_ref[...] = jnp.broadcast_to((left * behind)[:, LANES - 1 :], (PIXELS, LANES))
        carry_owner[...] = jnp.broadcast_to(tile[:, LANES - 1 :], (8, LANES))
        member = lax.broadcasted_iota(jnp.int32, (tiles, LANES), 0) == tile[0:1]
        member = jnp.where(member, 1.0, 0.0).astype(jnp.bfloat16)
        member = jnp.concatenate([member, member], axis=1)
        for ch in range(3):
            part = before * state[(1 + ch) * PIXELS : (2 + ch) * PIXELS, :]
            pair = jnp.concatenate(split(part, 2), axis=1)
            total_ref[ch] += lax.dot_general(
                member, pair, (((1,), (1,)), ((), ())), preferred_element_type=jnp.float32
            )

    coefs[...] = jnp.zeros_like(coefs)
    steps = BLOCK // 2

    def look_ahead(block):
        for j, found in enumerate([look(block, j) for j in range(steps)]):
            keep(j, *found)
        expand(block)

    look_ahead(0)
    for j in range(steps):
        power_a[j] = exponents(j)
    look_ahead(1)

    def one_group(g, carry):
        state[0:PIXELS, :] = jnp.ones((PIXELS, LANES), jnp.float32)
        state[PIXELS:, :] = jnp.zeros((3 * PIXELS, LANES), jnp.float32)

        def two_blocks(i, carry):
            for which in range(2):
                block = g * per_group + 2 * i + which
                now, later = ((power_a, power_b), (power_b, power_a))[which]

                found = [look(block + 2, j) for j in range(steps)]
                for j in range(steps):
                    later[j] = exponents(j)
                for j in range(steps):
                    blend(block, j, now)
                for j in range(steps):
                    keep(j, *found[j])
                expand(block + 2)
            return carry

        lax.fori_loop(0, per_group // 2, two_blocks, 0)
        flush(g)
        return carry

    lax.fori_loop(0, groups, one_group, 0)

    piece = lax.broadcasted_iota(jnp.int32, (8, LANES), 1)
    inner, outer = piece % TILE, piece // TILE
    sub = lax.broadcasted_iota(jnp.int32, (8, LANES), 0)
    skew = (outer + 8 - sub) % 8 * TILE + inner
    down = (outer + 8 - sub) % 8
    back = (outer + sub) % 8 * TILE + inner
    for ch in range(3):
        for r in range(tiles // cols_here):
            for q in range(cols_here // 8):
                for h in range(2):
                    x = total_ref[ch, r * cols_here + q * 8 : r * cols_here + q * 8 + 8, h * LANES : (h + 1) * LANES]
                    x = lane_pick(lane_pick(lane_pick(x, skew, 1), down, 0), back, 1)
                    out_ref[ch, r * TILE + h * 8 : r * TILE + h * 8 + 8, q * LANES : (q + 1) * LANES] = x


def blend_tiles(first, base, arrived, lists, owner, cols_here):
    tiles = first.shape[0] - 1
    most = lists.shape[0] // LANES
    smem = pl.BlockSpec(memory_space=pltpu.SMEM)
    vmem = pl.BlockSpec(memory_space=VMEM)
    f32 = jnp.float32
    return pl.pallas_call(
        functools.partial(blend_kernel, cols_here),
        out_shape=jax.ShapeDtypeStruct((3, tiles // cols_here * TILE, cols_here * TILE), f32),
        in_specs=[smem] * 2 + [vmem] * 4,
        out_specs=vmem,
        scratch_shapes=[
            VMEM((9 * ROWS, LANES), f32),
            VMEM((9 * ROWS, LANES), f32),
            VMEM((9 * ROWS, 512), jnp.bfloat16),
            VMEM((2 * ROWS, 256), jnp.bfloat16),
            VMEM((lists.shape[0] + LANES, LANES), jnp.int32),
            VMEM(((most + 1) * SEG, LANES), jnp.int32),
            VMEM((3 * 72, LANES), f32),
            VMEM((BLOCK * COEFS, LANES), f32),
            VMEM((BLOCK // 2, PIXELS, 256), f32),
            VMEM((BLOCK // 2, PIXELS, 256), f32),
            VMEM((4 * PIXELS, LANES), f32),
            VMEM((3, tiles, PIXELS), f32),
            VMEM((PIXELS, LANES), f32),
            VMEM((8, LANES), jnp.int32),
        ],
        compiler_params=pltpu.CompilerParams(vmem_limit_bytes=48 << 20),
        name="blend_tiles",
    )(first, base, arrived, lists, owner, jnp.asarray(monomials()).astype(jnp.bfloat16))


def arrange(tile_lists):
    rows_here, cols_here, list_len = tile_lists.shape
    tiles = rows_here * cols_here
    lists = tile_lists.reshape(tiles, list_len)
    runs = list_len // SEG
    live = (jnp.sum((lists >= 0).astype(jnp.int32), axis=1) + SEG - 1) // SEG
    number = jnp.arange(tiles, dtype=jnp.int32)
    ends = jnp.sum(jnp.where(number[None, :] <= number[:, None], live[None, :], 0), axis=1).astype(jnp.int32)
    first = jnp.concatenate([jnp.zeros((1,), jnp.int32), ends])
    most = tiles * runs
    segment = jnp.arange(most + LANES, dtype=jnp.int32)
    owner = jnp.sum((ends[None, :] <= segment[:, None]).astype(jnp.int32), axis=1).reshape(-1, LANES)
    code = jnp.pad(lists.reshape(most, SEG), ((0, 0), (0, LANES - SEG)), constant_values=-1)
    half = TILE // 2
    base = jnp.stack(
        [lax.axis_index("gs") * (cols_here * TILE) + half, lax.axis_index("img") * (rows_here * TILE) + half]
    ).astype(jnp.int32)
    return first, base, code, owner


EDGE = 8
TAPS = 5


def halo_kernel(rendered, truth, row_out, col_out, row_buf, col_buf, row_sem, col_sem, row_done, col_done):
    n_gs, n_img = lax.axis_size("gs"), lax.axis_size("img")
    g, i = lax.axis_index("gs"), lax.axis_index("img")
    place = lambda dg, di: {"gs": lax.rem(g + n_gs + dg, n_gs), "img": lax.rem(i + n_img + di, n_img)}
    around = [(dg, di) for dg in (-1, 0, 1) for di in (-1, 0, 1) if (dg, di) != (0, 0)]
    barrier = pltpu.get_barrier_semaphore()
    for dg, di in around:
        pl.semaphore_signal(barrier, inc=1, device_id=place(dg, di), device_id_type=pl.DeviceIdType.MESH)

    height, width = rendered.shape[1:]
    for c in range(6):
        source = (rendered, truth)[c // 3]
        image = source[c % 3]
        for side in range(2):
            edge = image[0:EDGE] if side == 0 else image[height - EDGE :]
            for half in range(2):
                row_buf[side, c, half] = edge[:, half * LANES : (half + 1) * LANES]
            columns = image[:, 0:LANES] if side == 0 else image[:, width - LANES :]
            turned = jnp.transpose(columns)
            col_buf[side, c] = turned[0:EDGE] if side == 0 else turned[LANES - EDGE :]

    pl.semaphore_wait(barrier, len(around))
    copies = []
    for side in range(2):
        step = -1 if side == 0 else 1
        copies.append(
            pltpu.make_async_remote_copy(
                src_ref=row_buf.at[side],
                dst_ref=row_out.at[side],
                send_sem=row_sem.at[side],
                recv_sem=row_done.at[side],
                device_id=place(0, step),
                device_id_type=pl.DeviceIdType.MESH,
            )
        )
        for di in (-1, 0, 1):
            copies.append(
                pltpu.make_async_remote_copy(
                    src_ref=col_buf.at[side],
                    dst_ref=col_out.at[side * 3 + di + 1],
                    send_sem=col_sem.at[side * 3 + di + 1],
                    recv_sem=col_done.at[side * 3 + di + 1],
                    device_id=place(step, di),
                    device_id_type=pl.DeviceIdType.MESH,
                )
            )
    for copy in copies:
        copy.start()
    for copy in copies:
        copy.wait()


def exchange_halos(rendered, truth):
    vmem = pl.BlockSpec(memory_space=VMEM)
    rows = (2, 6, 2, EDGE, LANES)
    f32 = jnp.float32
    return pl.pallas_call(
        halo_kernel,
        out_shape=(jax.ShapeDtypeStruct(rows, f32), jax.ShapeDtypeStruct((6, 6, EDGE, LANES), f32)),
        in_specs=[vmem] * 2,
        out_specs=(vmem, vmem),
        scratch_shapes=[
            VMEM(rows, f32),
            VMEM((2, 6, EDGE, LANES), f32),
            pltpu.SemaphoreType.DMA((2,)),
            pltpu.SemaphoreType.DMA((6,)),
            pltpu.SemaphoreType.DMA((2,)),
            pltpu.SemaphoreType.DMA((6,)),
        ],
        compiler_params=pltpu.CompilerParams(collective_id=1, has_side_effects=True, vmem_limit_bytes=16 << 20),
        name="exchange_halos",
    )(rendered, truth)


def window():
    offsets = np.arange(11, dtype=np.float32) - 5.0
    weights = np.exp(-offsets * offsets / np.float32(4.5))
    return [float(w) for w in weights / np.sum(weights)]


def loss_kernel(has, rendered, truth, rows, cols, out_ref, maps):
    height = rendered.shape[1]
    tall = height + 2 * EDGE
    start = lambda q, part: (q * 3 + part) * tall
    left, right, above, below = [has[n] > 0 for n in range(4)]
    keep = lambda flag, value: jnp.where(flag, value, 0.0)
    lane = lax.broadcasted_iota(jnp.int32, (EDGE, LANES), 1)
    gap = jnp.zeros((LANES - 2 * EDGE, LANES), jnp.float32)
    for c in range(6):
        image = (rendered, truth)[c // 3]
        for half in range(2):
            base = start(c, half)
            maps[base : base + EDGE, :] = keep(above, rows[1, c, half])
            maps[base + EDGE : base + EDGE + height, :] = image[c % 3, :, half * LANES : (half + 1) * LANES]
            maps[base + EDGE + height : base + tall, :] = keep(below, rows[0, c, half])
        base = start(c, 2)
        after = keep(right, cols[1, c])
        before = keep(left, cols[4, c])
        maps[base + EDGE : base + EDGE + height, :] = jnp.transpose(jnp.concatenate([after, gap, before], axis=0))
        mixed = []
        for flag, side in ((right, 0), (left, 3)):
            upper = keep(flag & above, cols[side + 2, c])
            lower = keep(flag & below, cols[side + 0, c])
            mixed.append(jnp.where(lane < LANES // 2, lower, upper))
        turned = jnp.transpose(jnp.concatenate([mixed[0], gap, mixed[1]], axis=0))
        maps[base : base + EDGE, :] = turned[LANES - EDGE :]
        maps[base + EDGE + height : base + tall, :] = turned[0:EDGE]

    def products(n, carry):
        for ch in range(3):
            for part in range(3):
                at = lambda q: pl.ds(pl.multiple_of(start(q + ch, part) + n * 8, 8), 8)
                r, t = maps[at(0), :], maps[at(3), :]
                maps[at(6), :] = r * r + t * t
                maps[at(9), :] = r * t
        return carry

    lax.fori_loop(0, tall // 8, products, 0)
    weights = window()

    def filtered(q, n):
        parts = []
        for part in range(3):
            row = lambda d: maps[pl.ds(start(q, part) + EDGE + n * 8 + d, 8), :]
            total = weights[TAPS] * row(0)
            for d in range(1, TAPS + 1):
                total = total + weights[TAPS + d] * (row(d) + row(-d))
            parts.append(total)
        first, second, outside = parts
        sums = [weights[TAPS] * first, weights[TAPS] * second]
        for d in range(1, TAPS + 1):
            from_ahead, from_back = lane >= d, lane < LANES - d
            for half, (before, here, after) in enumerate(((outside, first, second), (first, second, outside))):
                pair = pltpu.roll(jnp.where(from_ahead, here, after), LANES - d, 1)
                pair = pair + pltpu.roll(jnp.where(from_back, here, before), d, 1)
                sums[half] = sums[half] + weights[TAPS + d] * pair
        return sums

    def one_block(n, carry):
        difference = [0.0, 0.0]
        alike = [0.0, 0.0]
        where = pl.ds(pl.multiple_of(n * 8, 8), 8)
        for ch in range(3):
            means_r, means_t, squares, products_rt = [filtered(q + ch, n) for q in (0, 3, 6, 9)]
            for half in range(2):
                mean_r, mean_t = means_r[half], means_t[half]
                both = mean_r * mean_t
                squared = mean_r * mean_r + mean_t * mean_t
                above_line = (2.0 * both + stable_one) * (2.0 * (products_rt[half] - both) + stable_two)
                below_line = (squared + stable_one) * (squares[half] - squared + stable_two)
                alike[half] = alike[half] + above_line / below_line
                at = pl.ds(pl.multiple_of(start(ch, half) + EDGE + n * 8, 8), 8)
                at_t = pl.ds(pl.multiple_of(start(ch + 3, half) + EDGE + n * 8, 8), 8)
                difference[half] = difference[half] + jnp.abs(maps[at, :] - maps[at_t, :])
        for half in range(2):
            out_ref[where, half * LANES : (half + 1) * LANES] = (1.0 - ssim_share) * (
                difference[half] * (1.0 / 3.0)
            ) + ssim_share * (1.0 - alike[half] * (1.0 / 3.0))
        return carry

    lax.fori_loop(0, height // 8, one_block, 0)


def pixel_loss(has, rendered, truth, rows, cols):
    vmem = pl.BlockSpec(memory_space=VMEM)
    height, width = rendered.shape[1:]
    return pl.pallas_call(
        loss_kernel,
        out_shape=jax.ShapeDtypeStruct((height, width), jnp.float32),
        in_specs=[pl.BlockSpec(memory_space=pltpu.SMEM)] + [vmem] * 4,
        out_specs=vmem,
        scratch_shapes=[VMEM((12 * 3 * (height + 2 * EDGE), LANES), jnp.float32)],
        compiler_params=pltpu.CompilerParams(vmem_limit_bytes=32 << 20),
        name="pixel_loss",
    )(has, rendered, truth, rows, cols)


def on_device(gaussians, send_slots, tile_lists, truth):
    rows_here, cols_here, list_len = tile_lists.shape
    devices = send_slots.shape[1] // CAP
    arrived = deal(gaussians, send_slots.reshape(devices, CAP).T)
    first, base, code, owner = arrange(tile_lists)
    rendered = blend_tiles(first, base, arrived, code, owner, cols_here)
    rows, cols = exchange_halos(rendered, truth)
    g, i = lax.axis_index("gs"), lax.axis_index("img")
    has = jnp.stack([g > 0, g < lax.axis_size("gs") - 1, i > 0, i < lax.axis_size("img") - 1]).astype(jnp.int32)
    return (rendered, pixel_loss(has, rendered, truth, rows, cols))


def solution(mesh):
    return jax.shard_map(
        on_device,
        mesh=mesh,
        in_specs=(
            P(None, ("gs", "img")),
            P(("gs", "img"), None),
            P("img", "gs", None),
            P(None, "img", "gs"),
        ),
        out_specs=(P(None, "img", "gs"), P("img", "gs")),
        check_vma=False,
    )
```

```python
import functools
import math

import jax
import jax.numpy as jnp
import numpy as np
from jax import lax
from jax.experimental import pallas as pl
from jax.experimental.pallas import tpu as pltpu
from jax.sharding import PartitionSpec as P

TILE = 16
LANES = 128
CAP = 80
SPLAT = 9
ROWS = CAP // 2
LOG2E = 1.0 / math.log(2.0)
VMEM = pltpu.VMEM


coef_zero = 0.28209479177387814
coef_one = 0.4886025119029199
coef_two = [
    1.0925484305920792,
    -1.0925484305920792,
    0.31539156525252005,
    -1.0925484305920792,
    0.5462742152960396,
]
coef_three = [
    -0.5900435899266435,
    2.890611442640554,
    -0.4570457994644658,
    0.3731763325901154,
    -0.4570457994644658,
    1.445305721320277,
    -0.5900435899266435,
]
camera_z = -3000.0
ssim_share = 0.2
stable_one = 0.0001
stable_two = 0.0009


def project_chunk(gauss):
    row = lambda i: gauss[i : i + 1]
    mean_x, mean_y, mean_z = (row(0), row(1), row(2))
    squared = jnp.exp(2.0 * gauss[3:6])
    sq_0, sq_1, sq_2 = (squared[0:1], squared[1:2], squared[2:3])
    inv = 1.0 / jnp.sqrt(row(6) * row(6) + row(7) * row(7) + row(8) * row(8) + row(9) * row(9))
    quat_w, quat_x, quat_y, quat_z = (row(6) * inv, row(7) * inv, row(8) * inv, row(9) * inv)
    first_a = 1.0 - 2.0 * (quat_y * quat_y + quat_z * quat_z)
    first_b = 2.0 * (quat_x * quat_y - quat_w * quat_z)
    first_c = 2.0 * (quat_x * quat_z + quat_w * quat_y)
    second_a = 2.0 * (quat_x * quat_y + quat_w * quat_z)
    second_b = 1.0 - 2.0 * (quat_x * quat_x + quat_z * quat_z)
    second_c = 2.0 * (quat_y * quat_z - quat_w * quat_x)
    cov_xx = first_a * first_a * sq_0 + first_b * first_b * sq_1 + first_c * first_c * sq_2 + 0.3
    cov_xy = first_a * second_a * sq_0 + first_b * second_b * sq_1 + first_c * second_c * sq_2
    cov_yy = second_a * second_a * sq_0 + second_b * second_b * sq_1 + second_c * second_c * sq_2 + 0.3
    determinant = cov_xx * cov_yy - cov_xy * cov_xy
    opacity = 1.0 / (1.0 + jnp.exp(-row(10)))
    delta_z = mean_z - camera_z
    length = jnp.sqrt(mean_x * mean_x + mean_y * mean_y + delta_z * delta_z)
    dir_x, dir_y, dir_z = (mean_x / length, mean_y / length, delta_z / length)
    sq_x, sq_y, sq_z = (dir_x * dir_x, dir_y * dir_y, dir_z * dir_z)
    prod_xy, prod_yz, prod_xz = (dir_x * dir_y, dir_y * dir_z, dir_x * dir_z)
    basis = jnp.concatenate(
        [
            coef_zero * jnp.ones_like(dir_x),
            -coef_one * dir_y,
            coef_one * dir_z,
            -coef_one * dir_x,
            coef_two[0] * prod_xy,
            coef_two[1] * prod_yz,
            coef_two[2] * (2.0 * sq_z - sq_x - sq_y),
            coef_two[3] * prod_xz,
            coef_two[4] * (sq_x - sq_y),
            coef_three[0] * dir_y * (3.0 * sq_x - sq_y),
            coef_three[1] * prod_xy * dir_z,
            coef_three[2] * dir_y * (4.0 * sq_z - sq_x - sq_y),
            coef_three[3] * dir_z * (2.0 * sq_z - 3.0 * sq_x - 3.0 * sq_y),
            coef_three[4] * dir_x * (4.0 * sq_z - sq_x - sq_y),
            coef_three[5] * dir_z * (sq_x - sq_y),
            coef_three[6] * dir_x * (sq_x - 3.0 * sq_y),
        ],
        axis=0,
    )
    colour = []
    for channel in range(3):
        weights = gauss[11 + 16 * channel : 27 + 16 * channel]
        colour.append(jnp.maximum(jnp.sum(weights * basis, axis=0, keepdims=True) + 0.5, 0.0))
    return [
        mean_x,
        mean_y,
        cov_yy / determinant,
        -cov_xy / determinant,
        cov_xx / determinant,
        opacity,
    ] + colour


def split(value, parts):
    out = []
    for _ in range(parts):
        rounded = value.astype(jnp.bfloat16)
        out.append(rounded)
        value = value - rounded.astype(jnp.float32)
    return out


def fill_table(table, third, halves):
    rows = third.shape[0] // 2
    for half, ref in enumerate(halves):
        lanes = slice(half * LANES, (half + 1) * LANES)
        for part, value in enumerate(split(ref[...], 2)):
            table[:, part * 256 + half * LANES : part * 256 + (half + 1) * LANES] = value
        for p in range(2):
            third[p * rows : (p + 1) * rows, lanes] = split(ref[pl.ds(p, rows, stride=8), :], 3)[2]


def lookup(table, third, code):
    rows = table.shape[0] // SPLAT
    column = lax.broadcasted_iota(jnp.int32, (256, 256), 0).astype(jnp.float32).astype(jnp.bfloat16)
    col = jnp.bitwise_and(code, 255).astype(jnp.float32).astype(jnp.bfloat16)
    row = lax.shift_right_arithmetic(code, 8)
    hot = jnp.where(column == col, jnp.bfloat16(1), jnp.bfloat16(0))
    found = jnp.dot(table[...], jnp.concatenate([hot, hot], axis=0), preferred_element_type=jnp.float32)
    finer = jnp.dot(third[...], hot, preferred_element_type=jnp.float32)
    picked = jnp.zeros((8, 256), jnp.float32)
    rows8 = jnp.broadcast_to(row, (8, 256))
    for r in range(rows):
        picked = jnp.where(rows8 == r, found[r * 8 : (r + 1) * 8], picked)
    table_row = lax.broadcasted_iota(jnp.int32, (rows, 256), 0)
    choose = lambda lines: jnp.sum(jnp.where(table_row == row, lines, 0.0), axis=0, keepdims=True)
    sub = lax.broadcasted_iota(jnp.int32, (8, 256), 0)
    for p in range(2):
        picked = picked + jnp.where(sub == p, choose(finer[p * rows : (p + 1) * rows]), 0.0)
    return picked, choose(found[8 * rows :])


def outgoing_kernel(gauss_ref, pick_ref, out_ref, table_a, table_b, table, third, eight):
    blocks = gauss_ref.shape[1] // LANES
    rows = blocks // 2
    for block in range(blocks):
        splat = project_chunk(gauss_ref[:, block * LANES : (block + 1) * LANES])
        ref = (table_a, table_b)[block // rows]
        r = block % rows
        ref[r * 8 : r * 8 + 8, :] = jnp.concatenate(splat[:8], axis=0)
        ref[8 * rows + r : 8 * rows + r + 1, :] = splat[8]
    fill_table(table, third, (table_a, table_b))

    def eight_slots(i, carry):
        where = pl.multiple_of(i * 8, 8)
        picks = pick_ref[pl.ds(where, 8), :]
        block = lax.shift_right_logical(picks, 7)
        codes = jnp.bitwise_and(picks, LANES - 1) + jnp.where(block < rows, block * 256, (block - rows) * 256 + LANES)
        found = [
            lookup(table, third, jnp.concatenate([codes[2 * j : 2 * j + 1], codes[2 * j + 1 : 2 * j + 2]], axis=1))
            for j in range(4)
        ]
        for j, (first, last) in enumerate(found):
            for e in range(2):
                lanes = slice(e * LANES, (e + 1) * LANES)
                eight[pl.ds(where * 8 + (2 * j + e) * 8, 8), :] = first[:, lanes]
                k = where + 2 * j + e
                eight[pl.ds((CAP + k % ROWS) * 8 + k // ROWS, 1), :] = last[:, lanes]
        return carry

    eight[CAP * 8 :, :] = jnp.zeros((eight.shape[0] - CAP * 8, LANES), jnp.float32)
    lax.fori_loop(0, CAP // 8, eight_slots, 0)
    for p in range(8):
        out_ref[pl.ds(p, LANES, stride=8), :] = jnp.transpose(eight[pl.ds(p, LANES, stride=8), :])


def deal_kernel(gauss_ref, pick_ref, in_ref, out_ref, send_sem, done_sem, local_sem, *scratch):
    n_gs, n_img = lax.axis_size("gs"), lax.axis_size("img")
    devices = n_gs * n_img
    me = lax.axis_index("gs") * n_img + lax.axis_index("img")
    place = lambda d: {"gs": lax.div(d, n_img), "img": lax.rem(d, n_img)}
    block = lambda d: pl.ds(pl.multiple_of(d * 8, 8), 8)
    barrier = pltpu.get_barrier_semaphore()

    def greet(d, carry):
        to = lax.rem(me + d, devices)
        pl.semaphore_signal(barrier, inc=1, device_id=place(to), device_id_type=pl.DeviceIdType.MESH)
        return carry

    def send(d, carry):
        to = lax.rem(me + d, devices)
        pltpu.make_async_remote_copy(
            src_ref=out_ref.at[block(to)],
            dst_ref=in_ref.at[block(me)],
            send_sem=send_sem,
            recv_sem=done_sem,
            device_id=place(to),
            device_id_type=pl.DeviceIdType.MESH,
        ).start()
        return carry

    lax.fori_loop(1, devices, greet, 0)
    outgoing_kernel(gauss_ref, pick_ref, out_ref, *scratch)
    own = pltpu.make_async_copy(out_ref.at[block(me)], in_ref.at[block(me)], local_sem)
    own.start()
    own.wait()
    pl.semaphore_wait(barrier, devices - 1)
    lax.fori_loop(1, devices, send, 0)
    others = pl.ds(0, (devices - 1) * 8)
    pltpu.make_async_copy(out_ref.at[others], out_ref.at[others], send_sem).wait()
    pltpu.make_async_copy(in_ref.at[others], in_ref.at[others], done_sem).wait()


def deal(gaussians, picks):
    devices = picks.shape[1]
    rows = gaussians.shape[1] // (2 * LANES)
    vmem = pl.BlockSpec(memory_space=VMEM)
    f32 = jnp.float32
    return pl.pallas_call(
        deal_kernel,
        out_shape=jax.ShapeDtypeStruct((devices * 8, LANES), f32),
        in_specs=[vmem] * 2,
        out_specs=vmem,
        scratch_shapes=[VMEM((devices * 8, LANES), f32)]
        + [pltpu.SemaphoreType.DMA] * 3
        + [
            VMEM((SPLAT * rows, LANES), f32),
            VMEM((SPLAT * rows, LANES), f32),
            VMEM((SPLAT * rows, 512), jnp.bfloat16),
            VMEM((2 * rows, 256), jnp.bfloat16),
            VMEM((8 * LANES, LANES), f32),
        ],
        compiler_params=pltpu.CompilerParams(collective_id=2, has_side_effects=True, vmem_limit_bytes=16 << 20),
        name="deal_splats",
    )(gaussians, picks)


SEG = 32
BLOCK = 8
COEFS = 32
PIXELS = TILE * TILE
CHUNK = 64


def monomials():
    pixel = np.arange(PIXELS)
    x = (pixel % TILE) - 7.5
    y = (pixel // TILE) - 7.5
    cols = np.stack([x * x, y * y, x * y, x, y, np.ones_like(x)], axis=1)
    return np.concatenate([cols, cols, cols, np.zeros((PIXELS, COEFS - 18))], axis=1).astype(np.float32)


def lane_pick(value, index, axis):
    return jnp.take_along_axis(value, index, axis=axis, mode="promise_in_bounds")


def blend_kernel(cols_here, first, base, arrived, lists, ends, mono, out_ref,
                 table_a, table_b, table, third, packed, codes, params, coefs, power_a, power_b, state, total_ref,
                 carry_ref, carry_owner, owner):
    tiles = first.shape[0] - 1
    runs = lists.shape[0] // tiles
    groups = (first[tiles] + LANES - 1) // LANES
    per_group = SEG // BLOCK

    for p in range(8):
        flat = jnp.transpose(arrived[pl.ds(p, LANES, stride=8), :])
        for half, ref in enumerate((table_a, table_b)):
            ref[pl.ds(p, ROWS, stride=8), :] = flat[half * ROWS : (half + 1) * ROWS]
            if p == half:
                ref[8 * ROWS :, :] = flat[CAP : CAP + ROWS]
    fill_table(table, third, (table_a, table_b))

    packed[...] = jnp.full(packed.shape, -1, jnp.int32)
    for t in range(tiles):
        packed[pl.ds(first[t], runs), :] = lists[t * runs : (t + 1) * runs, :]

    def turn(g, carry):
        lanes = jnp.transpose(packed[pl.ds(pl.multiple_of(g * LANES, LANES), LANES), :])
        slot = lanes[0:SEG]
        source = ((slot.astype(jnp.float32) + 0.5) * (1.0 / CAP)).astype(jnp.int32)
        k = slot - source * CAP
        code = source + jnp.where(k < ROWS, k * 256, (k - ROWS) * 256 + LANES)
        codes[pl.ds(pl.multiple_of(g * SEG, SEG), SEG), :] = jnp.where(slot >= 0, code, -1)
        return carry

    lax.fori_loop(0, groups, turn, 0)
    ends_down = jnp.transpose(jnp.broadcast_to(ends[...], (LANES, LANES)))
    along = lax.broadcasted_iota(jnp.int32, (LANES, LANES), 1)

    def own(g, carry):
        past = jnp.where(ends_down <= along + g * LANES, 1, 0)
        owner[pl.ds(g, 1), :] = jnp.sum(past, axis=0, keepdims=True)
        return carry

    lax.fori_loop(0, groups + 1, own, 0)
    total_ref[...] = jnp.zeros_like(total_ref)
    carry_ref[...] = jnp.ones_like(carry_ref)
    carry_owner[...] = jnp.full(carry_owner.shape, -1, jnp.int32)

    def look(block, j):
        where = block * BLOCK + 2 * j
        code = jnp.concatenate([codes[pl.ds(where, 1), :], codes[pl.ds(where + 1, 1), :]], axis=1)
        return ((block % 3) * 72,) + lookup(table, third, code)

    def keep(j, slot, picked, ninth):
        for e in range(2):
            lanes = slice(e * LANES, (e + 1) * LANES)
            params[pl.ds(pl.multiple_of(slot + (2 * j + e) * 8, 8), 8), :] = picked[:, lanes]
            params[pl.ds(slot + 64 + 2 * j + e, 1), :] = ninth[:, lanes]

    def expand(block):
        slot = (block % 3) * 72
        m_x, m_y, a, b, c, o = [params[pl.ds(slot + p, BLOCK, stride=8), :] for p in range(6)]
        live = codes[pl.ds(pl.multiple_of(block * BLOCK, BLOCK), BLOCK), :] >= 0
        tile = owner[pl.ds(block // per_group, 1), :]
        tile_y = lax.shift_right_logical(tile, cols_here.bit_length() - 1)
        tile_x = jnp.bitwise_and(tile, cols_here - 1)
        u = m_x - (tile_x * TILE + base[0]).astype(jnp.float32)
        v = m_y - (tile_y * TILE + base[1]).astype(jnp.float32)
        level = LOG2E * (-0.5 * (a * u * u + c * v * v) - b * u * v)
        values = [
            (-0.5 * LOG2E) * a,
            (-0.5 * LOG2E) * c,
            -LOG2E * b,
            LOG2E * (a * u + b * v),
            LOG2E * (c * v + b * u),
            jnp.where(live, level + jnp.log2(o), -1e30),
        ]
        for i, value in enumerate(values):
            for part, rounded in enumerate(split(value, 3)):
                coefs[pl.ds(part * 6 + i, BLOCK, stride=COEFS), :] = rounded.astype(jnp.float32)

    def exponents(j):
        pair = [
            coefs[pl.ds((2 * j + e) * COEFS, COEFS), :].astype(jnp.bfloat16) for e in range(2)
        ]
        return jnp.dot(mono[...], jnp.concatenate(pair, axis=1), preferred_element_type=jnp.float32)

    def blend(block, j, power):
        slot = (block % 3) * 72
        at = lambda q, i: pl.ds(q * PIXELS + j * CHUNK + i * 8, 8)
        pieces = range(CHUNK // 8)
        left = [state[at(0, i), :] for i in pieces]
        colour = [[state[at(1 + ch, i), :] for i in pieces] for ch in range(3)]
        for k in range(BLOCK):
            rows = (slot + k * 8 + 6, slot + k * 8 + 7, slot + 64 + k)
            tints = [jnp.broadcast_to(params[pl.ds(r, 1), :], (8, LANES)) for r in rows]
            for i in pieces:
                alpha = jnp.exp2(power[k // 2, at(0, i), (k % 2) * LANES : (k % 2 + 1) * LANES])
                weight = left[i] * alpha
                left[i] = left[i] - weight
                for ch in range(3):
                    colour[ch][i] = colour[ch][i] + weight * tints[ch]
        for i in pieces:
            state[at(0, i), :] = left[i]
            for ch in range(3):
                state[at(1 + ch, i), :] = colour[ch][i]

    lane = lax.broadcasted_iota(jnp.int32, (8, LANES), 1)

    def flush(g):
        tile = jnp.broadcast_to(owner[pl.ds(g, 1), :], (8, LANES))
        left = state[0:PIXELS, :]
        same = []
        for d in (1, 2, 4, 8):
            same.append(((pltpu.roll(tile, d, 1) == tile) & (lane >= d))[0:1])
        for d, mask in zip((1, 2, 4, 8), same):
            left = left * jnp.where(mask, pltpu.roll(left, d, 1), 1.0)
        before = jnp.where(same[0], pltpu.roll(left, 1, 1), 1.0)
        goes_on = (tile == carry_owner[...])[0:1]
        behind = jnp.where(goes_on, carry_ref[...], 1.0)
        before = before * behind
        carry_ref[...] = jnp.broadcast_to((left * behind)[:, LANES - 1 :], (PIXELS, LANES))
        carry_owner[...] = jnp.broadcast_to(tile[:, LANES - 1 :], (8, LANES))
        member = lax.broadcasted_iota(jnp.int32, (tiles, LANES), 0) == tile[0:1]
        member = jnp.where(member, 1.0, 0.0).astype(jnp.bfloat16)
        member = jnp.concatenate([member, member], axis=1)
        for ch in range(3):
            part = before * state[(1 + ch) * PIXELS : (2 + ch) * PIXELS, :]
            pair = jnp.concatenate(split(part, 2), axis=1)
            total_ref[ch] += lax.dot_general(
                member, pair, (((1,), (1,)), ((), ())), preferred_element_type=jnp.float32
            )

    coefs[...] = jnp.zeros_like(coefs)
    steps = BLOCK // 2

    def look_ahead(block):
        for j, found in enumerate([look(block, j) for j in range(steps)]):
            keep(j, *found)
        expand(block)

    look_ahead(0)
    for j in range(steps):
        power_a[j] = exponents(j)
    look_ahead(1)

    def one_group(g, carry):
        state[0:PIXELS, :] = jnp.ones((PIXELS, LANES), jnp.float32)
        state[PIXELS:, :] = jnp.zeros((3 * PIXELS, LANES), jnp.float32)

        def two_blocks(i, carry):
            for which in range(2):
                block = g * per_group + 2 * i + which
                now, later = ((power_a, power_b), (power_b, power_a))[which]

                found = [look(block + 2, j) for j in range(steps)]
                for j in range(steps):
                    later[j] = exponents(j)
                for j in range(steps):
                    blend(block, j, now)
                for j in range(steps):
                    keep(j, *found[j])
                expand(block + 2)
            return carry

        lax.fori_loop(0, per_group // 2, two_blocks, 0)
        flush(g)
        return carry

    lax.fori_loop(0, groups, one_group, 0)

    piece = lax.broadcasted_iota(jnp.int32, (8, LANES), 1)
    inner, outer = piece % TILE, piece // TILE
    sub = lax.broadcasted_iota(jnp.int32, (8, LANES), 0)
    skew = (outer + 8 - sub) % 8 * TILE + inner
    down = (outer + 8 - sub) % 8
    back = (outer + sub) % 8 * TILE + inner
    for ch in range(3):
        for r in range(tiles // cols_here):
            for q in range(cols_here // 8):
                for h in range(2):
                    x = total_ref[ch, r * cols_here + q * 8 : r * cols_here + q * 8 + 8, h * LANES : (h + 1) * LANES]
                    x = lane_pick(lane_pick(lane_pick(x, skew, 1), down, 0), back, 1)
                    out_ref[ch, r * TILE + h * 8 : r * TILE + h * 8 + 8, q * LANES : (q + 1) * LANES] = x


def blend_tiles(first, base, arrived, lists, ends, cols_here):
    tiles = first.shape[0] - 1
    most = lists.shape[0] // LANES
    smem = pl.BlockSpec(memory_space=pltpu.SMEM)
    vmem = pl.BlockSpec(memory_space=VMEM)
    f32 = jnp.float32
    return pl.pallas_call(
        functools.partial(blend_kernel, cols_here),
        out_shape=jax.ShapeDtypeStruct((3, tiles // cols_here * TILE, cols_here * TILE), f32),
        in_specs=[smem] * 2 + [vmem] * 4,
        out_specs=vmem,
        scratch_shapes=[
            VMEM((9 * ROWS, LANES), f32),
            VMEM((9 * ROWS, LANES), f32),
            VMEM((9 * ROWS, 512), jnp.bfloat16),
            VMEM((2 * ROWS, 256), jnp.bfloat16),
            VMEM((lists.shape[0] + LANES, LANES), jnp.int32),
            VMEM(((most + 1) * SEG, LANES), jnp.int32),
            VMEM((3 * 72, LANES), f32),
            VMEM((BLOCK * COEFS, LANES), f32),
            VMEM((BLOCK // 2, PIXELS, 256), f32),
            VMEM((BLOCK // 2, PIXELS, 256), f32),
            VMEM((4 * PIXELS, LANES), f32),
            VMEM((3, tiles, PIXELS), f32),
            VMEM((PIXELS, LANES), f32),
            VMEM((8, LANES), jnp.int32),
            VMEM((most + 8, LANES), jnp.int32),
        ],
        compiler_params=pltpu.CompilerParams(vmem_limit_bytes=20 << 20),
        name="blend_tiles",
    )(first, base, arrived, lists, ends, jnp.asarray(monomials()).astype(jnp.bfloat16))


def arrange(tile_lists):
    rows_here, cols_here, list_len = tile_lists.shape
    tiles = rows_here * cols_here
    lists = tile_lists.reshape(tiles, list_len)
    runs = list_len // SEG
    live = (jnp.sum((lists >= 0).astype(jnp.int32), axis=1) + SEG - 1) // SEG
    number = jnp.arange(tiles, dtype=jnp.int32)
    ends = jnp.sum(jnp.where(number[None, :] <= number[:, None], live[None, :], 0), axis=1).astype(jnp.int32)
    first = jnp.concatenate([jnp.zeros((1,), jnp.int32), ends])
    most = tiles * runs
    code = jnp.pad(lists.reshape(most, SEG), ((0, 0), (0, LANES - SEG)), constant_values=-1)
    half = TILE // 2
    base = jnp.stack(
        [lax.axis_index("gs") * (cols_here * TILE) + half, lax.axis_index("img") * (rows_here * TILE) + half]
    ).astype(jnp.int32)
    return first, base, code, ends.reshape(1, tiles)


EDGE = 8
TAPS = 5


def halo_kernel(rendered, truth, row_out, col_out, row_buf, col_buf, row_sem, col_sem, row_done, col_done):
    n_gs, n_img = lax.axis_size("gs"), lax.axis_size("img")
    g, i = lax.axis_index("gs"), lax.axis_index("img")
    place = lambda dg, di: {"gs": lax.rem(g + n_gs + dg, n_gs), "img": lax.rem(i + n_img + di, n_img)}
    around = [(dg, di) for dg in (-1, 0, 1) for di in (-1, 0, 1) if (dg, di) != (0, 0)]
    barrier = pltpu.get_barrier_semaphore()
    for dg, di in around:
        pl.semaphore_signal(barrier, inc=1, device_id=place(dg, di), device_id_type=pl.DeviceIdType.MESH)

    height, width = rendered.shape[1:]
    for c in range(6):
        source = (rendered, truth)[c // 3]
        image = source[c % 3]
        for side in range(2):
            edge = image[0:EDGE] if side == 0 else image[height - EDGE :]
            for half in range(2):
                row_buf[side, c, half] = edge[:, half * LANES : (half + 1) * LANES]
            columns = image[:, 0:LANES] if side == 0 else image[:, width - LANES :]
            turned = jnp.transpose(columns)
            col_buf[side, c] = turned[0:EDGE] if side == 0 else turned[LANES - EDGE :]

    pl.semaphore_wait(barrier, len(around))
    copies = []
    for side in range(2):
        step = -1 if side == 0 else 1
        copies.append(
            pltpu.make_async_remote_copy(
                src_ref=row_buf.at[side],
                dst_ref=row_out.at[side],
                send_sem=row_sem.at[side],
                recv_sem=row_done.at[side],
                device_id=place(0, step),
                device_id_type=pl.DeviceIdType.MESH,
            )
        )
        for di in (-1, 0, 1):
            copies.append(
                pltpu.make_async_remote_copy(
                    src_ref=col_buf.at[side],
                    dst_ref=col_out.at[side * 3 + di + 1],
                    send_sem=col_sem.at[side * 3 + di + 1],
                    recv_sem=col_done.at[side * 3 + di + 1],
                    device_id=place(step, di),
                    device_id_type=pl.DeviceIdType.MESH,
                )
            )
    for copy in copies:
        copy.start()
    for copy in copies:
        copy.wait()


def exchange_halos(rendered, truth):
    vmem = pl.BlockSpec(memory_space=VMEM)
    rows = (2, 6, 2, EDGE, LANES)
    f32 = jnp.float32
    return pl.pallas_call(
        halo_kernel,
        out_shape=(jax.ShapeDtypeStruct(rows, f32), jax.ShapeDtypeStruct((6, 6, EDGE, LANES), f32)),
        in_specs=[vmem] * 2,
        out_specs=(vmem, vmem),
        scratch_shapes=[
            VMEM(rows, f32),
            VMEM((2, 6, EDGE, LANES), f32),
            pltpu.SemaphoreType.DMA((2,)),
            pltpu.SemaphoreType.DMA((6,)),
            pltpu.SemaphoreType.DMA((2,)),
            pltpu.SemaphoreType.DMA((6,)),
        ],
        compiler_params=pltpu.CompilerParams(collective_id=1, has_side_effects=True, vmem_limit_bytes=8 << 20),
        name="exchange_halos",
    )(rendered, truth)


def window():
    offsets = np.arange(11, dtype=np.float32) - 5.0
    weights = np.exp(-offsets * offsets / np.float32(4.5))
    return [float(w) for w in weights / np.sum(weights)]


def loss_kernel(has, rendered, truth, rows, cols, out_ref, maps, summed, turned, likeness):
    height = rendered.shape[1]
    tall = height + 2 * EDGE
    start = lambda q, part: (q * 3 + part) * tall
    left, right, above, below = [has[n] > 0 for n in range(4)]
    keep = lambda flag, value: jnp.where(flag, value, 0.0)
    lane = lax.broadcasted_iota(jnp.int32, (EDGE, LANES), 1)
    gap = jnp.zeros((LANES - 2 * EDGE, LANES), jnp.float32)
    for c in range(6):
        image = (rendered, truth)[c // 3]
        for half in range(2):
            base = start(c, half)
            maps[base : base + EDGE, :] = keep(above, rows[1, c, half])
            maps[base + EDGE : base + EDGE + height, :] = image[c % 3, :, half * LANES : (half + 1) * LANES]
            maps[base + EDGE + height : base + tall, :] = keep(below, rows[0, c, half])
        base = start(c, 2)
        after = keep(right, cols[1, c])
        before = keep(left, cols[4, c])
        maps[base + EDGE : base + EDGE + height, :] = jnp.transpose(jnp.concatenate([after, gap, before], axis=0))
        mixed = []
        for flag, side in ((right, 0), (left, 3)):
            upper = keep(flag & above, cols[side + 2, c])
            lower = keep(flag & below, cols[side + 0, c])
            mixed.append(jnp.where(lane < LANES // 2, lower, upper))
        corners = jnp.transpose(jnp.concatenate([mixed[0], gap, mixed[1]], axis=0))
        maps[base : base + EDGE, :] = corners[LANES - EDGE :]
        maps[base + EDGE + height : base + tall, :] = corners[0:EDGE]

    def products(n, carry):
        for ch in range(3):
            for part in range(3):
                at = lambda q: pl.ds(pl.multiple_of(start(q + ch, part) + n * 8, 8), 8)
                r, t = maps[at(0), :], maps[at(3), :]
                maps[at(6), :] = r * r + t * t
                maps[at(9), :] = r * t
        return carry

    lax.fori_loop(0, tall // 8, products, 0)
    weights = window()

    def window_sum(ref, first):
        row = lambda d: ref[pl.ds(first + d, 8), :]
        total = weights[TAPS] * row(0)
        for d in range(1, TAPS + 1):
            total = total + weights[TAPS + d] * (row(d) + row(-d))
        return total

    def over_rows(n, carry):
        for q in range(12):
            for part in range(3):
                at = pl.ds(pl.multiple_of((q * 3 + part) * height + n * 8, 8), 8)
                summed[at, :] = window_sum(maps, start(q, part) + EDGE + n * 8)
        return carry

    lax.fori_loop(0, height // 8, over_rows, 0)
    wide = 2 * LANES + 2 * EDGE
    for q in range(12):
        blocks = [jnp.transpose(summed[(q * 3 + part) * height : (q * 3 + part + 1) * height, :]) for part in range(3)]
        base = q * wide
        turned[base : base + EDGE, :] = blocks[2][LANES - EDGE :]
        turned[base + EDGE : base + EDGE + LANES, :] = blocks[0]
        turned[base + EDGE + LANES : base + EDGE + 2 * LANES, :] = blocks[1]
        turned[base + EDGE + 2 * LANES : base + wide, :] = blocks[2][:EDGE]

    def over_columns(n, carry):
        alike = 0.0
        for ch in range(3):
            mean_r, mean_t, square, product = [
                window_sum(turned, (q + ch) * wide + EDGE + n * 8) for q in (0, 3, 6, 9)
            ]
            both = mean_r * mean_t
            squared = mean_r * mean_r + mean_t * mean_t
            above_line = (2.0 * both + stable_one) * (2.0 * (product - both) + stable_two)
            below_line = (squared + stable_one) * (square - squared + stable_two)
            alike = alike + above_line / below_line
        likeness[pl.ds(pl.multiple_of(n * 8, 8), 8), :] = alike
        return carry

    lax.fori_loop(0, 2 * LANES // 8, over_columns, 0)
    for half in range(2):
        lanes = slice(half * LANES, (half + 1) * LANES)
        difference = jnp.abs(rendered[0, :, lanes] - truth[0, :, lanes])
        for ch in (1, 2):
            difference = difference + jnp.abs(rendered[ch, :, lanes] - truth[ch, :, lanes])
        alike = jnp.transpose(likeness[lanes, :])
        out_ref[:, lanes] = (1.0 - ssim_share) * (difference * (1.0 / 3.0)) + ssim_share * (1.0 - alike * (1.0 / 3.0))


def pixel_loss(has, rendered, truth, rows, cols):
    vmem = pl.BlockSpec(memory_space=VMEM)
    height, width = rendered.shape[1:]
    return pl.pallas_call(
        loss_kernel,
        out_shape=jax.ShapeDtypeStruct((height, width), jnp.float32),
        in_specs=[pl.BlockSpec(memory_space=pltpu.SMEM)] + [vmem] * 4,
        out_specs=vmem,
        scratch_shapes=[
            VMEM((12 * 3 * (height + 2 * EDGE), LANES), jnp.float32),
            VMEM((12 * 3 * height, LANES), jnp.float32),
            VMEM((12 * (width + 2 * EDGE), LANES), jnp.float32),
            VMEM((width, LANES), jnp.float32),
        ],
        compiler_params=pltpu.CompilerParams(vmem_limit_bytes=16 << 20),
        name="pixel_loss",
    )(has, rendered, truth, rows, cols)


def on_device(gaussians, send_slots, tile_lists, truth):
    rows_here, cols_here, list_len = tile_lists.shape
    devices = send_slots.shape[1] // CAP
    arrived = deal(gaussians, send_slots.reshape(devices, CAP).T)
    first, base, code, ends = arrange(tile_lists)
    rendered = blend_tiles(first, base, arrived, code, ends, cols_here)
    rows, cols = exchange_halos(rendered, truth)
    g, i = lax.axis_index("gs"), lax.axis_index("img")
    has = jnp.stack([g > 0, g < lax.axis_size("gs") - 1, i > 0, i < lax.axis_size("img") - 1]).astype(jnp.int32)
    return (rendered, pixel_loss(has, rendered, truth, rows, cols))


def solution(mesh):
    return jax.shard_map(
        on_device,
        mesh=mesh,
        in_specs=(
            P(None, ("gs", "img")),
            P(("gs", "img"), None),
            P("img", "gs", None),
            P(None, "img", "gs"),
        ),
        out_specs=(P(None, "img", "gs"), P("img", "gs")),
        check_vma=False,
    )
```

```python
import functools
import math

import jax
import jax.numpy as jnp
import numpy as np
from jax import lax
from jax.experimental import pallas as pl
from jax.experimental.pallas import tpu as pltpu
from jax.sharding import PartitionSpec as P

TILE = 16
LANES = 128
CAP = 80
SPLAT = 9
ROWS = CAP // 2
LOG2E = 1.0 / math.log(2.0)
VMEM = pltpu.VMEM


coef_zero = 0.28209479177387814
coef_one = 0.4886025119029199
coef_two = [
    1.0925484305920792,
    -1.0925484305920792,
    0.31539156525252005,
    -1.0925484305920792,
    0.5462742152960396,
]
coef_three = [
    -0.5900435899266435,
    2.890611442640554,
    -0.4570457994644658,
    0.3731763325901154,
    -0.4570457994644658,
    1.445305721320277,
    -0.5900435899266435,
]
camera_z = -3000.0
ssim_share = 0.2
stable_one = 0.0001
stable_two = 0.0009


def project(row):
    mean_x, mean_y, mean_z = (row(0), row(1), row(2))
    sq_0, sq_1, sq_2 = [jnp.exp(2.0 * row(i)) for i in (3, 4, 5)]
    inv = 1.0 / jnp.sqrt(row(6) * row(6) + row(7) * row(7) + row(8) * row(8) + row(9) * row(9))
    quat_w, quat_x, quat_y, quat_z = (row(6) * inv, row(7) * inv, row(8) * inv, row(9) * inv)
    first_a = 1.0 - 2.0 * (quat_y * quat_y + quat_z * quat_z)
    first_b = 2.0 * (quat_x * quat_y - quat_w * quat_z)
    first_c = 2.0 * (quat_x * quat_z + quat_w * quat_y)
    second_a = 2.0 * (quat_x * quat_y + quat_w * quat_z)
    second_b = 1.0 - 2.0 * (quat_x * quat_x + quat_z * quat_z)
    second_c = 2.0 * (quat_y * quat_z - quat_w * quat_x)
    cov_xx = first_a * first_a * sq_0 + first_b * first_b * sq_1 + first_c * first_c * sq_2 + 0.3
    cov_xy = first_a * second_a * sq_0 + first_b * second_b * sq_1 + first_c * second_c * sq_2
    cov_yy = second_a * second_a * sq_0 + second_b * second_b * sq_1 + second_c * second_c * sq_2 + 0.3
    determinant = cov_xx * cov_yy - cov_xy * cov_xy
    opacity = 1.0 / (1.0 + jnp.exp(-row(10)))
    delta_z = mean_z - camera_z
    length = jnp.sqrt(mean_x * mean_x + mean_y * mean_y + delta_z * delta_z)
    dir_x, dir_y, dir_z = (mean_x / length, mean_y / length, delta_z / length)
    sq_x, sq_y, sq_z = (dir_x * dir_x, dir_y * dir_y, dir_z * dir_z)
    prod_xy, prod_yz, prod_xz = (dir_x * dir_y, dir_y * dir_z, dir_x * dir_z)
    basis = [
        coef_zero * jnp.ones_like(dir_x),
        -coef_one * dir_y,
        coef_one * dir_z,
        -coef_one * dir_x,
        coef_two[0] * prod_xy,
        coef_two[1] * prod_yz,
        coef_two[2] * (2.0 * sq_z - sq_x - sq_y),
        coef_two[3] * prod_xz,
        coef_two[4] * (sq_x - sq_y),
        coef_three[0] * dir_y * (3.0 * sq_x - sq_y),
        coef_three[1] * prod_xy * dir_z,
        coef_three[2] * dir_y * (4.0 * sq_z - sq_x - sq_y),
        coef_three[3] * dir_z * (2.0 * sq_z - 3.0 * sq_x - 3.0 * sq_y),
        coef_three[4] * dir_x * (4.0 * sq_z - sq_x - sq_y),
        coef_three[5] * dir_z * (sq_x - sq_y),
        coef_three[6] * dir_x * (sq_x - 3.0 * sq_y),
    ]
    colour = []
    for channel in range(3):
        total = 0.5
        for k, value in enumerate(basis):
            total = total + row(11 + 16 * channel + k) * value
        colour.append(jnp.maximum(total, 0.0))
    return [
        mean_x,
        mean_y,
        cov_yy / determinant,
        -cov_xy / determinant,
        cov_xx / determinant,
        opacity,
    ] + colour


def split(value, parts):
    out = []
    for _ in range(parts):
        rounded = value.astype(jnp.bfloat16)
        out.append(rounded)
        value = value - rounded.astype(jnp.float32)
    return out


def fill_table(table, third, halves):
    rows = third.shape[0] // 2
    for half, ref in enumerate(halves):
        lanes = slice(half * LANES, (half + 1) * LANES)
        for part, value in enumerate(split(ref[...], 2)):
            table[:, part * 256 + half * LANES : part * 256 + (half + 1) * LANES] = value
        for p in range(2):
            third[p * rows : (p + 1) * rows, lanes] = split(ref[pl.ds(p, rows, stride=8), :], 3)[2]


def lookup(table, third, code):
    rows = table.shape[0] // SPLAT
    column = lax.broadcasted_iota(jnp.int32, (256, 256), 0).astype(jnp.float32).astype(jnp.bfloat16)
    col = jnp.bitwise_and(code, 255).astype(jnp.float32).astype(jnp.bfloat16)
    row = lax.shift_right_arithmetic(code, 8)
    hot = jnp.where(column == col, jnp.bfloat16(1), jnp.bfloat16(0))
    found = jnp.dot(table[...], jnp.concatenate([hot, hot], axis=0), preferred_element_type=jnp.float32)
    finer = jnp.dot(third[...], hot, preferred_element_type=jnp.float32)
    picked = jnp.zeros((8, 256), jnp.float32)
    rows8 = jnp.broadcast_to(row, (8, 256))
    for r in range(rows):
        picked = jnp.where(rows8 == r, found[r * 8 : (r + 1) * 8], picked)
    table_row = lax.broadcasted_iota(jnp.int32, (rows, 256), 0)
    choose = lambda lines: jnp.sum(jnp.where(table_row == row, lines, 0.0), axis=0, keepdims=True)
    sub = lax.broadcasted_iota(jnp.int32, (8, 256), 0)
    for p in range(2):
        picked = picked + jnp.where(sub == p, choose(finer[p * rows : (p + 1) * rows]), 0.0)
    return picked, choose(found[8 * rows :])


def outgoing_kernel(gauss_ref, pick_ref, out_ref, table_a, table_b, table, third, eight, chunks, turned):
    blocks = gauss_ref.shape[1] // LANES
    rows = blocks // 2
    height = 64
    for block in range(blocks):
        piece = gauss_ref[:, block * LANES : (block + 1) * LANES]
        chunks[block * height : block * height + gauss_ref.shape[0], :] = piece
    for block in range(0, blocks, 8):
        splat = project(lambda i: chunks[pl.ds(block * height + i, 8, stride=height), :])
        for half, ref in enumerate((table_a, table_b)):
            low, high = max(block, half * rows), min(block + 8, (half + 1) * rows)
            if low < high:
                r, part = low - half * rows, slice(low - block, high - block)
                for p in range(8):
                    ref[pl.ds(r * 8 + p, high - low, stride=8), :] = splat[p][part]
                ref[8 * rows + r : 8 * rows + r + high - low, :] = splat[8][part]
    for d in range(LANES):
        turned[d : d + 1, 0:CAP] = pick_ref[:, d * CAP : (d + 1) * CAP]
    turned[...] = jnp.transpose(turned[...])
    fill_table(table, third, (table_a, table_b))

    def eight_slots(i, carry):
        where = pl.multiple_of(i * 8, 8)
        picks = turned[pl.ds(where, 8), :]
        block = lax.shift_right_logical(picks, 7)
        codes = jnp.bitwise_and(picks, LANES - 1) + jnp.where(block < rows, block * 256, (block - rows) * 256 + LANES)
        found = [
            lookup(table, third, jnp.concatenate([codes[2 * j : 2 * j + 1], codes[2 * j + 1 : 2 * j + 2]], axis=1))
            for j in range(4)
        ]
        for j, (first, last) in enumerate(found):
            for e in range(2):
                lanes = slice(e * LANES, (e + 1) * LANES)
                eight[pl.ds(where * 8 + (2 * j + e) * 8, 8), :] = first[:, lanes]
                k = where + 2 * j + e
                eight[pl.ds((CAP + k % ROWS) * 8 + k // ROWS, 1), :] = last[:, lanes]
        return carry

    eight[CAP * 8 :, :] = jnp.zeros((eight.shape[0] - CAP * 8, LANES), jnp.float32)
    lax.fori_loop(0, CAP // 8, eight_slots, 0)
    for p in range(8):
        out_ref[pl.ds(p, LANES, stride=8), :] = jnp.transpose(eight[pl.ds(p, LANES, stride=8), :])


def deal_kernel(gauss_ref, pick_ref, in_ref, out_ref, send_sem, done_sem, local_sem, *scratch):
    n_gs, n_img = lax.axis_size("gs"), lax.axis_size("img")
    devices = n_gs * n_img
    me = lax.axis_index("gs") * n_img + lax.axis_index("img")
    place = lambda d: {"gs": lax.div(d, n_img), "img": lax.rem(d, n_img)}
    block = lambda d: pl.ds(pl.multiple_of(d * 8, 8), 8)
    barrier = pltpu.get_barrier_semaphore()

    def greet(d, carry):
        to = lax.rem(me + d, devices)
        pl.semaphore_signal(barrier, inc=1, device_id=place(to), device_id_type=pl.DeviceIdType.MESH)
        return carry

    def send(d, carry):
        to = lax.rem(me + d, devices)
        pltpu.make_async_remote_copy(
            src_ref=out_ref.at[block(to)],
            dst_ref=in_ref.at[block(me)],
            send_sem=send_sem,
            recv_sem=done_sem,
            device_id=place(to),
            device_id_type=pl.DeviceIdType.MESH,
        ).start()
        return carry

    lax.fori_loop(1, devices, greet, 0)
    outgoing_kernel(gauss_ref, pick_ref, out_ref, *scratch)
    own = pltpu.make_async_copy(out_ref.at[block(me)], in_ref.at[block(me)], local_sem)
    own.start()
    own.wait()
    pl.semaphore_wait(barrier, devices - 1)
    lax.fori_loop(1, devices, send, 0)
    others = pl.ds(0, (devices - 1) * 8)
    pltpu.make_async_copy(out_ref.at[others], out_ref.at[others], send_sem).wait()
    pltpu.make_async_copy(in_ref.at[others], in_ref.at[others], done_sem).wait()


def deal(gaussians, picks):
    devices = picks.shape[1] // CAP
    rows = gaussians.shape[1] // (2 * LANES)
    vmem = pl.BlockSpec(memory_space=VMEM)
    f32 = jnp.float32
    return pl.pallas_call(
        deal_kernel,
        out_shape=jax.ShapeDtypeStruct((devices * 8, LANES), f32),
        in_specs=[vmem] * 2,
        out_specs=vmem,
        scratch_shapes=[VMEM((devices * 8, LANES), f32)]
        + [pltpu.SemaphoreType.DMA] * 3
        + [
            VMEM((SPLAT * rows, LANES), f32),
            VMEM((SPLAT * rows, LANES), f32),
            VMEM((SPLAT * rows, 512), jnp.bfloat16),
            VMEM((2 * rows, 256), jnp.bfloat16),
            VMEM((8 * LANES, LANES), f32),
            VMEM((gaussians.shape[1] // LANES * 64, LANES), f32),
            VMEM((LANES, LANES), jnp.int32),
        ],
        compiler_params=pltpu.CompilerParams(collective_id=2, has_side_effects=True, vmem_limit_bytes=16 << 20),
        name="deal_splats",
    )(gaussians, picks)


SEG = 32
BLOCK = 8
COEFS = 32
PIXELS = TILE * TILE
CHUNK = 64


def monomials():
    pixel = np.arange(PIXELS)
    x = (pixel % TILE) - 7.5
    y = (pixel // TILE) - 7.5
    cols = np.stack([x * x, y * y, x * y, x, y, np.ones_like(x)], axis=1)
    return np.concatenate([cols, cols, cols, np.zeros((PIXELS, COEFS - 18))], axis=1).astype(np.float32)


def lane_pick(value, index, axis):
    return jnp.take_along_axis(value, index, axis=axis, mode="promise_in_bounds")


def blend_kernel(cols_here, first, base, arrived, lists, ends, mono, out_ref, again_ref,
                 table_a, table_b, table, third, packed, codes, params, coefs, power_a, power_b, state, total_ref,
                 carry_ref, carry_owner, owner, origin):
    tiles = first.shape[0] - 1
    runs = lists.shape[2] // SEG
    share = LANES // SEG
    groups = (first[tiles] + LANES - 1) // LANES
    per_group = SEG // BLOCK

    for p in range(8):
        flat = jnp.transpose(arrived[pl.ds(p, LANES, stride=8), :])
        for half, ref in enumerate((table_a, table_b)):
            ref[pl.ds(p, ROWS, stride=8), :] = flat[half * ROWS : (half + 1) * ROWS]
            if p == half:
                ref[8 * ROWS :, :] = flat[CAP : CAP + ROWS]
    fill_table(table, third, (table_a, table_b))

    upper = lax.broadcasted_iota(jnp.int32, (8, LANES), 0) < share
    packed[...] = jnp.full(packed.shape, -1, jnp.int32)
    for t in range(tiles):
        line = lambda c: jnp.broadcast_to(
            lists[t // cols_here, t % cols_here : t % cols_here + 1, c * LANES : (c + 1) * LANES], (8, LANES)
        )
        for c in range(0, runs // share, 2):
            packed[pl.ds(first[t] + c * share, 8), :] = jnp.where(upper, line(c), line(c + 1))

    ends_down = jnp.transpose(jnp.broadcast_to(ends[...], (LANES, LANES)))
    along = lax.broadcasted_iota(jnp.int32, (LANES, LANES), 1)

    def own(g, carry):
        past = ends_down <= along + g * LANES
        owner[pl.ds(g, 1), :] = jnp.sum(jnp.where(past, 1, 0), axis=0, keepdims=True)
        origin[pl.ds(g, 1), :] = jnp.max(jnp.where(past, ends_down, 0), axis=0, keepdims=True)
        return carry

    lax.fori_loop(0, groups + 1, own, 0)

    def turn(g, carry):
        lanes = jnp.transpose(packed[pl.ds(pl.multiple_of(g * LANES, LANES), LANES), :])
        place = lax.broadcasted_iota(jnp.int32, (1, LANES), 1) + g * LANES - origin[pl.ds(g, 1), :]
        place = jnp.bitwise_and(place, share - 1)
        slot = lanes[0:SEG]
        for c in range(1, share):
            slot = jnp.where(place == c, lanes[c * SEG : (c + 1) * SEG], slot)
        source = ((slot.astype(jnp.float32) + 0.5) * (1.0 / CAP)).astype(jnp.int32)
        k = slot - source * CAP
        code = source + jnp.where(k < ROWS, k * 256, (k - ROWS) * 256 + LANES)
        codes[pl.ds(pl.multiple_of(g * SEG, SEG), SEG), :] = jnp.where(slot >= 0, code, -1)
        return carry

    lax.fori_loop(0, groups, turn, 0)
    total_ref[...] = jnp.zeros_like(total_ref)
    carry_ref[...] = jnp.ones_like(carry_ref)
    carry_owner[...] = jnp.full(carry_owner.shape, -1, jnp.int32)

    def look(block, j):
        where = block * BLOCK + 2 * j
        code = jnp.concatenate([codes[pl.ds(where, 1), :], codes[pl.ds(where + 1, 1), :]], axis=1)
        return ((block % 3) * 72,) + lookup(table, third, code)

    def keep(j, slot, picked, ninth):
        for e in range(2):
            lanes = slice(e * LANES, (e + 1) * LANES)
            params[pl.ds(pl.multiple_of(slot + (2 * j + e) * 8, 8), 8), :] = picked[:, lanes]
            params[pl.ds(slot + 64 + 2 * j + e, 1), :] = ninth[:, lanes]

    def expand(block):
        slot = (block % 3) * 72
        m_x, m_y, a, b, c, o = [params[pl.ds(slot + p, BLOCK, stride=8), :] for p in range(6)]
        live = codes[pl.ds(pl.multiple_of(block * BLOCK, BLOCK), BLOCK), :] >= 0
        tile = owner[pl.ds(block // per_group, 1), :]
        tile_y = lax.shift_right_logical(tile, cols_here.bit_length() - 1)
        tile_x = jnp.bitwise_and(tile, cols_here - 1)
        u = m_x - (tile_x * TILE + base[0]).astype(jnp.float32)
        v = m_y - (tile_y * TILE + base[1]).astype(jnp.float32)
        level = LOG2E * (-0.5 * (a * u * u + c * v * v) - b * u * v)
        values = [
            (-0.5 * LOG2E) * a,
            (-0.5 * LOG2E) * c,
            -LOG2E * b,
            LOG2E * (a * u + b * v),
            LOG2E * (c * v + b * u),
            jnp.where(live, level + jnp.log2(o), -1e30),
        ]
        for i, value in enumerate(values):
            for part, rounded in enumerate(split(value, 3)):
                coefs[pl.ds(part * 6 + i, BLOCK, stride=COEFS), :] = rounded.astype(jnp.float32)

    def exponents(j):
        pair = [
            coefs[pl.ds((2 * j + e) * COEFS, COEFS), :].astype(jnp.bfloat16) for e in range(2)
        ]
        return jnp.dot(mono[...], jnp.concatenate(pair, axis=1), preferred_element_type=jnp.float32)

    def blend(block, j, power):
        slot = (block % 3) * 72
        at = lambda q, i: pl.ds(q * PIXELS + j * CHUNK + i * 8, 8)
        pieces = range(CHUNK // 8)
        left = [state[at(0, i), :] for i in pieces]
        colour = [[state[at(1 + ch, i), :] for i in pieces] for ch in range(3)]
        for k in range(BLOCK):
            rows = (slot + k * 8 + 6, slot + k * 8 + 7, slot + 64 + k)
            tints = [jnp.broadcast_to(params[pl.ds(r, 1), :], (8, LANES)) for r in rows]
            for i in pieces:
                alpha = jnp.exp2(power[k // 2, at(0, i), (k % 2) * LANES : (k % 2 + 1) * LANES])
                weight = left[i] * alpha
                left[i] = left[i] - weight
                for ch in range(3):
                    colour[ch][i] = colour[ch][i] + weight * tints[ch]
        for i in pieces:
            state[at(0, i), :] = left[i]
            for ch in range(3):
                state[at(1 + ch, i), :] = colour[ch][i]

    lane = lax.broadcasted_iota(jnp.int32, (8, LANES), 1)

    def flush(g):
        tile = jnp.broadcast_to(owner[pl.ds(g, 1), :], (8, LANES))
        left = state[0:PIXELS, :]
        same = []
        for d in (1, 2, 4, 8):
            same.append(((pltpu.roll(tile, d, 1) == tile) & (lane >= d))[0:1])
        for d, mask in zip((1, 2, 4, 8), same):
            left = left * jnp.where(mask, pltpu.roll(left, d, 1), 1.0)
        before = jnp.where(same[0], pltpu.roll(left, 1, 1), 1.0)
        goes_on = (tile == carry_owner[...])[0:1]
        behind = jnp.where(goes_on, carry_ref[...], 1.0)
        before = before * behind
        carry_ref[...] = jnp.broadcast_to((left * behind)[:, LANES - 1 :], (PIXELS, LANES))
        carry_owner[...] = jnp.broadcast_to(tile[:, LANES - 1 :], (8, LANES))
        member = lax.broadcasted_iota(jnp.int32, (tiles, LANES), 0) == tile[0:1]
        member = jnp.where(member, 1.0, 0.0).astype(jnp.bfloat16)
        member = jnp.concatenate([member, member], axis=1)
        for ch in range(3):
            part = before * state[(1 + ch) * PIXELS : (2 + ch) * PIXELS, :]
            pair = jnp.concatenate(split(part, 2), axis=1)
            total_ref[ch] += lax.dot_general(
                member, pair, (((1,), (1,)), ((), ())), preferred_element_type=jnp.float32
            )

    coefs[...] = jnp.zeros_like(coefs)
    steps = BLOCK // 2

    def look_ahead(block):
        for j, found in enumerate([look(block, j) for j in range(steps)]):
            keep(j, *found)
        expand(block)

    look_ahead(0)
    for j in range(steps):
        power_a[j] = exponents(j)
    look_ahead(1)

    def one_group(g, carry):
        state[0:PIXELS, :] = jnp.ones((PIXELS, LANES), jnp.float32)
        state[PIXELS:, :] = jnp.zeros((3 * PIXELS, LANES), jnp.float32)

        def two_blocks(i, carry):
            for which in range(2):
                block = g * per_group + 2 * i + which
                now, later = ((power_a, power_b), (power_b, power_a))[which]

                found = [look(block + 2, j) for j in range(steps)]
                for j in range(steps):
                    later[j] = exponents(j)
                for j in range(steps):
                    blend(block, j, now)
                for j in range(steps):
                    keep(j, *found[j])
                expand(block + 2)
            return carry

        lax.fori_loop(0, per_group // 2, two_blocks, 0)
        flush(g)
        return carry

    lax.fori_loop(0, groups, one_group, 0)

    piece = lax.broadcasted_iota(jnp.int32, (8, LANES), 1)
    inner, outer = piece % TILE, piece // TILE
    sub = lax.broadcasted_iota(jnp.int32, (8, LANES), 0)
    skew = (outer + 8 - sub) % 8 * TILE + inner
    down = (outer + 8 - sub) % 8
    back = (outer + sub) % 8 * TILE + inner
    for ch in range(3):
        for r in range(tiles // cols_here):
            for q in range(cols_here // 8):
                for h in range(2):
                    x = total_ref[ch, r * cols_here + q * 8 : r * cols_here + q * 8 + 8, h * LANES : (h + 1) * LANES]
                    x = lane_pick(lane_pick(lane_pick(x, skew, 1), down, 0), back, 1)
                    for ref in (out_ref, again_ref):
                        ref[ch, r * TILE + h * 8 : r * TILE + h * 8 + 8, q * LANES : (q + 1) * LANES] = x


def blend_tiles(first, base, arrived, lists, ends, cols_here):
    tiles = first.shape[0] - 1
    most = tiles * (lists.shape[2] // SEG) // LANES
    smem = pl.BlockSpec(memory_space=pltpu.SMEM)
    vmem = pl.BlockSpec(memory_space=VMEM)
    f32 = jnp.float32
    return pl.pallas_call(
        functools.partial(blend_kernel, cols_here),
        out_shape=(jax.ShapeDtypeStruct((3, tiles // cols_here * TILE, cols_here * TILE), f32),) * 2,
        in_specs=[smem] * 2 + [vmem] * 4,
        out_specs=(vmem, vmem),
        scratch_shapes=[
            VMEM((9 * ROWS, LANES), f32),
            VMEM((9 * ROWS, LANES), f32),
            VMEM((9 * ROWS, 512), jnp.bfloat16),
            VMEM((2 * ROWS, 256), jnp.bfloat16),
            VMEM(((most + 1) * LANES, LANES), jnp.int32),
            VMEM(((most + 1) * SEG, LANES), jnp.int32),
            VMEM((3 * 72, LANES), f32),
            VMEM((BLOCK * COEFS, LANES), f32),
            VMEM((BLOCK // 2, PIXELS, 256), f32),
            VMEM((BLOCK // 2, PIXELS, 256), f32),
            VMEM((4 * PIXELS, LANES), f32),
            VMEM((3, tiles, PIXELS), f32),
            VMEM((PIXELS, LANES), f32),
            VMEM((8, LANES), jnp.int32),
            VMEM((most + 8, LANES), jnp.int32),
            VMEM((most + 8, LANES), jnp.int32),
        ],
        compiler_params=pltpu.CompilerParams(vmem_limit_bytes=20 << 20),
        name="blend_tiles",
    )(first, base, arrived, lists, ends, jnp.asarray(monomials()).astype(jnp.bfloat16))


def arrange(tile_lists):
    rows_here, cols_here, list_len = tile_lists.shape
    tiles = rows_here * cols_here
    lists = tile_lists.reshape(tiles, list_len)
    live = (jnp.sum((lists >= 0).astype(jnp.int32), axis=1) + SEG - 1) // SEG
    number = jnp.arange(tiles, dtype=jnp.int32)
    ends = jnp.sum(jnp.where(number[None, :] <= number[:, None], live[None, :], 0), axis=1).astype(jnp.int32)
    first = jnp.concatenate([jnp.zeros((1,), jnp.int32), ends])
    half = TILE // 2
    base = jnp.stack(
        [lax.axis_index("gs") * (cols_here * TILE) + half, lax.axis_index("img") * (rows_here * TILE) + half]
    ).astype(jnp.int32)
    return first, base, ends.reshape(1, tiles)


EDGE = 8
TAPS = 5


def halo_kernel(rendered, truth, row_out, col_out, row_buf, col_buf, row_sem, col_sem, row_done, col_done):
    n_gs, n_img = lax.axis_size("gs"), lax.axis_size("img")
    g, i = lax.axis_index("gs"), lax.axis_index("img")
    place = lambda dg, di: {"gs": lax.rem(g + n_gs + dg, n_gs), "img": lax.rem(i + n_img + di, n_img)}
    around = [(dg, di) for dg in (-1, 0, 1) for di in (-1, 0, 1) if (dg, di) != (0, 0)]
    barrier = pltpu.get_barrier_semaphore()
    for dg, di in around:
        pl.semaphore_signal(barrier, inc=1, device_id=place(dg, di), device_id_type=pl.DeviceIdType.MESH)

    height, width = rendered.shape[1:]
    for c in range(6):
        source = (rendered, truth)[c // 3]
        image = source[c % 3]
        for side in range(2):
            edge = image[0:EDGE] if side == 0 else image[height - EDGE :]
            for half in range(2):
                row_buf[side, c, half] = edge[:, half * LANES : (half + 1) * LANES]
            columns = image[:, 0:LANES] if side == 0 else image[:, width - LANES :]
            turned = jnp.transpose(columns)
            col_buf[side, c] = turned[0:EDGE] if side == 0 else turned[LANES - EDGE :]

    pl.semaphore_wait(barrier, len(around))
    copies = []
    for side in range(2):
        step = -1 if side == 0 else 1
        copies.append(
            pltpu.make_async_remote_copy(
                src_ref=row_buf.at[side],
                dst_ref=row_out.at[side],
                send_sem=row_sem.at[side],
                recv_sem=row_done.at[side],
                device_id=place(0, step),
                device_id_type=pl.DeviceIdType.MESH,
            )
        )
        for di in (-1, 0, 1):
            copies.append(
                pltpu.make_async_remote_copy(
                    src_ref=col_buf.at[side],
                    dst_ref=col_out.at[side * 3 + di + 1],
                    send_sem=col_sem.at[side * 3 + di + 1],
                    recv_sem=col_done.at[side * 3 + di + 1],
                    device_id=place(step, di),
                    device_id_type=pl.DeviceIdType.MESH,
                )
            )
    for copy in copies:
        copy.start()
    for copy in copies:
        copy.wait()


def exchange_halos(rendered, truth):
    vmem = pl.BlockSpec(memory_space=VMEM)
    rows = (2, 6, 2, EDGE, LANES)
    f32 = jnp.float32
    return pl.pallas_call(
        halo_kernel,
        out_shape=(jax.ShapeDtypeStruct(rows, f32), jax.ShapeDtypeStruct((6, 6, EDGE, LANES), f32)),
        in_specs=[vmem] * 2,
        out_specs=(vmem, vmem),
        scratch_shapes=[
            VMEM(rows, f32),
            VMEM((2, 6, EDGE, LANES), f32),
            pltpu.SemaphoreType.DMA((2,)),
            pltpu.SemaphoreType.DMA((6,)),
            pltpu.SemaphoreType.DMA((2,)),
            pltpu.SemaphoreType.DMA((6,)),
        ],
        compiler_params=pltpu.CompilerParams(collective_id=1, has_side_effects=True, vmem_limit_bytes=8 << 20),
        name="exchange_halos",
    )(rendered, truth)


def window():
    offsets = np.arange(11, dtype=np.float32) - 5.0
    weights = np.exp(-offsets * offsets / np.float32(4.5))
    return [float(w) for w in weights / np.sum(weights)]


def loss_kernel(has, rendered, truth, rows, cols, out_ref, maps, summed, turned, likeness):
    height = rendered.shape[1]
    tall = height + 2 * EDGE
    start = lambda q, part: (q * 3 + part) * tall
    left, right, above, below = [has[n] > 0 for n in range(4)]
    keep = lambda flag, value: jnp.where(flag, value, 0.0)
    lane = lax.broadcasted_iota(jnp.int32, (EDGE, LANES), 1)
    gap = jnp.zeros((LANES - 2 * EDGE, LANES), jnp.float32)
    for c in range(6):
        image = (rendered, truth)[c // 3]
        for half in range(2):
            base = start(c, half)
            maps[base : base + EDGE, :] = keep(above, rows[1, c, half])
            maps[base + EDGE : base + EDGE + height, :] = image[c % 3, :, half * LANES : (half + 1) * LANES]
            maps[base + EDGE + height : base + tall, :] = keep(below, rows[0, c, half])
        base = start(c, 2)
        after = keep(right, cols[1, c])
        before = keep(left, cols[4, c])
        maps[base + EDGE : base + EDGE + height, :] = jnp.transpose(jnp.concatenate([after, gap, before], axis=0))
        mixed = []
        for flag, side in ((right, 0), (left, 3)):
            upper = keep(flag & above, cols[side + 2, c])
            lower = keep(flag & below, cols[side + 0, c])
            mixed.append(jnp.where(lane < LANES // 2, lower, upper))
        corners = jnp.transpose(jnp.concatenate([mixed[0], gap, mixed[1]], axis=0))
        maps[base : base + EDGE, :] = corners[LANES - EDGE :]
        maps[base + EDGE + height : base + tall, :] = corners[0:EDGE]

    def products(n, carry):
        for ch in range(3):
            for part in range(3):
                at = lambda q: pl.ds(pl.multiple_of(start(q + ch, part) + n * 8, 8), 8)
                r, t = maps[at(0), :], maps[at(3), :]
                maps[at(6), :] = r * r + t * t
                maps[at(9), :] = r * t
        return carry

    lax.fori_loop(0, tall // 8, products, 0)
    weights = window()

    def window_sum(ref, first):
        row = lambda d: ref[pl.ds(first + d, 8), :]
        total = weights[TAPS] * row(0)
        for d in range(1, TAPS + 1):
            total = total + weights[TAPS + d] * (row(d) + row(-d))
        return total

    def over_rows(n, carry):
        for q in range(12):
            for part in range(3):
                at = pl.ds(pl.multiple_of((q * 3 + part) * height + n * 8, 8), 8)
                summed[at, :] = window_sum(maps, start(q, part) + EDGE + n * 8)
        return carry

    lax.fori_loop(0, height // 8, over_rows, 0)
    wide = 2 * LANES + 2 * EDGE
    for q in range(12):
        blocks = [jnp.transpose(summed[(q * 3 + part) * height : (q * 3 + part + 1) * height, :]) for part in range(3)]
        base = q * wide
        turned[base : base + EDGE, :] = blocks[2][LANES - EDGE :]
        turned[base + EDGE : base + EDGE + LANES, :] = blocks[0]
        turned[base + EDGE + LANES : base + EDGE + 2 * LANES, :] = blocks[1]
        turned[base + EDGE + 2 * LANES : base + wide, :] = blocks[2][:EDGE]

    def over_columns(n, carry):
        alike = 0.0
        for ch in range(3):
            mean_r, mean_t, square, product = [
                window_sum(turned, (q + ch) * wide + EDGE + n * 8) for q in (0, 3, 6, 9)
            ]
            both = mean_r * mean_t
            squared = mean_r * mean_r + mean_t * mean_t
            above_line = (2.0 * both + stable_one) * (2.0 * (product - both) + stable_two)
            below_line = (squared + stable_one) * (square - squared + stable_two)
            alike = alike + above_line / below_line
        likeness[pl.ds(pl.multiple_of(n * 8, 8), 8), :] = alike
        return carry

    lax.fori_loop(0, 2 * LANES // 8, over_columns, 0)
    for half in range(2):
        lanes = slice(half * LANES, (half + 1) * LANES)
        difference = jnp.abs(rendered[0, :, lanes] - truth[0, :, lanes])
        for ch in (1, 2):
            difference = difference + jnp.abs(rendered[ch, :, lanes] - truth[ch, :, lanes])
        alike = jnp.transpose(likeness[lanes, :])
        out_ref[:, lanes] = (1.0 - ssim_share) * (difference * (1.0 / 3.0)) + ssim_share * (1.0 - alike * (1.0 / 3.0))


def pixel_loss(has, rendered, truth, rows, cols):
    vmem = pl.BlockSpec(memory_space=VMEM)
    height, width = rendered.shape[1:]
    return pl.pallas_call(
        loss_kernel,
        out_shape=jax.ShapeDtypeStruct((height, width), jnp.float32),
        in_specs=[pl.BlockSpec(memory_space=pltpu.SMEM)] + [vmem] * 4,
        out_specs=vmem,
        scratch_shapes=[
            VMEM((12 * 3 * (height + 2 * EDGE), LANES), jnp.float32),
            VMEM((12 * 3 * height, LANES), jnp.float32),
            VMEM((12 * (width + 2 * EDGE), LANES), jnp.float32),
            VMEM((width, LANES), jnp.float32),
        ],
        compiler_params=pltpu.CompilerParams(vmem_limit_bytes=16 << 20),
        name="pixel_loss",
    )(has, rendered, truth, rows, cols)


def on_device(gaussians, send_slots, tile_lists, truth):
    rows_here, cols_here, list_len = tile_lists.shape
    arrived = deal(gaussians, send_slots)
    first, base, ends = arrange(tile_lists)
    rendered, again = blend_tiles(first, base, arrived, tile_lists, ends, cols_here)
    rows, cols = exchange_halos(again, truth)
    g, i = lax.axis_index("gs"), lax.axis_index("img")
    has = jnp.stack([g > 0, g < lax.axis_size("gs") - 1, i > 0, i < lax.axis_size("img") - 1]).astype(jnp.int32)
    return (rendered, pixel_loss(has, again, truth, rows, cols))


def solution(mesh):
    return jax.shard_map(
        on_device,
        mesh=mesh,
        in_specs=(
            P(None, ("gs", "img")),
            P(("gs", "img"), None),
            P("img", "gs", None),
            P(None, "img", "gs"),
        ),
        out_specs=(P(None, "img", "gs"), P("img", "gs")),
        check_vma=False,
    )
```

```python
import functools
import math

import jax
import jax.numpy as jnp
import numpy as np
from jax import lax
from jax.experimental import pallas as pl
from jax.experimental.pallas import tpu as pltpu
from jax.sharding import PartitionSpec as P

TILE = 16
LANES = 128
CAP = 80
SPLAT = 9
ROWS = CAP // 2
LOG2E = 1.0 / math.log(2.0)
VMEM = pltpu.VMEM


coef_zero = 0.28209479177387814
coef_one = 0.4886025119029199
coef_two = [
    1.0925484305920792,
    -1.0925484305920792,
    0.31539156525252005,
    -1.0925484305920792,
    0.5462742152960396,
]
coef_three = [
    -0.5900435899266435,
    2.890611442640554,
    -0.4570457994644658,
    0.3731763325901154,
    -0.4570457994644658,
    1.445305721320277,
    -0.5900435899266435,
]
camera_z = -3000.0
ssim_share = 0.2
stable_one = 0.0001
stable_two = 0.0009


def project(row):
    mean_x, mean_y, mean_z = (row(0), row(1), row(2))
    sq_0, sq_1, sq_2 = [jnp.exp(2.0 * row(i)) for i in (3, 4, 5)]
    inv = 1.0 / jnp.sqrt(row(6) * row(6) + row(7) * row(7) + row(8) * row(8) + row(9) * row(9))
    quat_w, quat_x, quat_y, quat_z = (row(6) * inv, row(7) * inv, row(8) * inv, row(9) * inv)
    first_a = 1.0 - 2.0 * (quat_y * quat_y + quat_z * quat_z)
    first_b = 2.0 * (quat_x * quat_y - quat_w * quat_z)
    first_c = 2.0 * (quat_x * quat_z + quat_w * quat_y)
    second_a = 2.0 * (quat_x * quat_y + quat_w * quat_z)
    second_b = 1.0 - 2.0 * (quat_x * quat_x + quat_z * quat_z)
    second_c = 2.0 * (quat_y * quat_z - quat_w * quat_x)
    cov_xx = first_a * first_a * sq_0 + first_b * first_b * sq_1 + first_c * first_c * sq_2 + 0.3
    cov_xy = first_a * second_a * sq_0 + first_b * second_b * sq_1 + first_c * second_c * sq_2
    cov_yy = second_a * second_a * sq_0 + second_b * second_b * sq_1 + second_c * second_c * sq_2 + 0.3
    determinant = cov_xx * cov_yy - cov_xy * cov_xy
    opacity = 1.0 / (1.0 + jnp.exp(-row(10)))
    delta_z = mean_z - camera_z
    length = jnp.sqrt(mean_x * mean_x + mean_y * mean_y + delta_z * delta_z)
    dir_x, dir_y, dir_z = (mean_x / length, mean_y / length, delta_z / length)
    sq_x, sq_y, sq_z = (dir_x * dir_x, dir_y * dir_y, dir_z * dir_z)
    prod_xy, prod_yz, prod_xz = (dir_x * dir_y, dir_y * dir_z, dir_x * dir_z)
    basis = [
        coef_zero * jnp.ones_like(dir_x),
        -coef_one * dir_y,
        coef_one * dir_z,
        -coef_one * dir_x,
        coef_two[0] * prod_xy,
        coef_two[1] * prod_yz,
        coef_two[2] * (2.0 * sq_z - sq_x - sq_y),
        coef_two[3] * prod_xz,
        coef_two[4] * (sq_x - sq_y),
        coef_three[0] * dir_y * (3.0 * sq_x - sq_y),
        coef_three[1] * prod_xy * dir_z,
        coef_three[2] * dir_y * (4.0 * sq_z - sq_x - sq_y),
        coef_three[3] * dir_z * (2.0 * sq_z - 3.0 * sq_x - 3.0 * sq_y),
        coef_three[4] * dir_x * (4.0 * sq_z - sq_x - sq_y),
        coef_three[5] * dir_z * (sq_x - sq_y),
        coef_three[6] * dir_x * (sq_x - 3.0 * sq_y),
    ]
    colour = []
    for channel in range(3):
        total = 0.5
        for k, value in enumerate(basis):
            total = total + row(11 + 16 * channel + k) * value
        colour.append(jnp.maximum(total, 0.0))
    return [
        mean_x,
        mean_y,
        cov_yy / determinant,
        -cov_xy / determinant,
        cov_xx / determinant,
        opacity,
    ] + colour


def split(value, parts):
    out = []
    for _ in range(parts):
        rounded = value.astype(jnp.bfloat16)
        out.append(rounded)
        value = value - rounded.astype(jnp.float32)
    return out


def fill_table(table, third, halves):
    rows = third.shape[0] // 2
    for half, ref in enumerate(halves):
        lanes = slice(half * LANES, (half + 1) * LANES)
        for part, value in enumerate(split(ref[...], 2)):
            table[:, part * 256 + half * LANES : part * 256 + (half + 1) * LANES] = value
        for p in range(2):
            third[p * rows : (p + 1) * rows, lanes] = split(ref[pl.ds(p, rows, stride=8), :], 3)[2]


def lookup(table, third, code):
    rows = table.shape[0] // SPLAT
    column = lax.broadcasted_iota(jnp.int32, (256, 256), 0).astype(jnp.float32).astype(jnp.bfloat16)
    col = jnp.bitwise_and(code, 255).astype(jnp.float32).astype(jnp.bfloat16)
    row = lax.shift_right_arithmetic(code, 8)
    hot = jnp.where(column == col, jnp.bfloat16(1), jnp.bfloat16(0))
    found = jnp.dot(table[...], jnp.concatenate([hot, hot], axis=0), preferred_element_type=jnp.float32)
    finer = jnp.dot(third[...], hot, preferred_element_type=jnp.float32)
    picked = jnp.zeros((8, 256), jnp.float32)
    rows8 = jnp.broadcast_to(row, (8, 256))
    for r in range(rows):
        picked = jnp.where(rows8 == r, found[r * 8 : (r + 1) * 8], picked)
    table_row = lax.broadcasted_iota(jnp.int32, (rows, 256), 0)
    choose = lambda lines: jnp.sum(jnp.where(table_row == row, lines, 0.0), axis=0, keepdims=True)
    sub = lax.broadcasted_iota(jnp.int32, (8, 256), 0)
    for p in range(2):
        picked = picked + jnp.where(sub == p, choose(finer[p * rows : (p + 1) * rows]), 0.0)
    return picked, choose(found[8 * rows :])


def outgoing_kernel(gauss_ref, pick_ref, out_ref, table_a, table_b, table, third, eight, chunks, turned):
    blocks = gauss_ref.shape[1] // LANES
    rows = blocks // 2
    height = 64
    for block in range(blocks):
        piece = gauss_ref[:, block * LANES : (block + 1) * LANES]
        chunks[block * height : block * height + gauss_ref.shape[0], :] = piece
    for block in range(0, blocks, 8):
        splat = project(lambda i: chunks[pl.ds(block * height + i, 8, stride=height), :])
        for half, ref in enumerate((table_a, table_b)):
            low, high = max(block, half * rows), min(block + 8, (half + 1) * rows)
            if low < high:
                r, part = low - half * rows, slice(low - block, high - block)
                for p in range(8):
                    ref[pl.ds(r * 8 + p, high - low, stride=8), :] = splat[p][part]
                ref[8 * rows + r : 8 * rows + r + high - low, :] = splat[8][part]
    for d in range(LANES):
        turned[d : d + 1, 0:CAP] = pick_ref[:, d * CAP : (d + 1) * CAP]
    turned[...] = jnp.transpose(turned[...])
    fill_table(table, third, (table_a, table_b))

    def eight_slots(i, carry):
        where = pl.multiple_of(i * 8, 8)
        picks = turned[pl.ds(where, 8), :]
        block = lax.shift_right_logical(picks, 7)
        codes = jnp.bitwise_and(picks, LANES - 1) + jnp.where(block < rows, block * 256, (block - rows) * 256 + LANES)
        found = [
            lookup(table, third, jnp.concatenate([codes[2 * j : 2 * j + 1], codes[2 * j + 1 : 2 * j + 2]], axis=1))
            for j in range(4)
        ]
        for j, (first, last) in enumerate(found):
            for e in range(2):
                lanes = slice(e * LANES, (e + 1) * LANES)
                eight[pl.ds(where * 8 + (2 * j + e) * 8, 8), :] = first[:, lanes]
                k = where + 2 * j + e
                eight[pl.ds((CAP + k % ROWS) * 8 + k // ROWS, 1), :] = last[:, lanes]
        return carry

    eight[CAP * 8 :, :] = jnp.zeros((eight.shape[0] - CAP * 8, LANES), jnp.float32)
    lax.fori_loop(0, CAP // 8, eight_slots, 0)
    for p in range(8):
        out_ref[pl.ds(p, LANES, stride=8), :] = jnp.transpose(eight[pl.ds(p, LANES, stride=8), :])


def deal_kernel(gauss_hbm, pick_hbm, in_ref, gauss_ref, pick_ref, out_ref, send_sem, done_sem, local_sem, load_sem, *scratch):
    n_gs, n_img = lax.axis_size("gs"), lax.axis_size("img")
    devices = n_gs * n_img
    me = lax.axis_index("gs") * n_img + lax.axis_index("img")
    place = lambda d: {"gs": lax.div(d, n_img), "img": lax.rem(d, n_img)}
    block = lambda d: pl.ds(pl.multiple_of(d * 8, 8), 8)
    barrier = pltpu.get_barrier_semaphore()

    def greet(d, carry):
        to = lax.rem(me + d, devices)
        pl.semaphore_signal(barrier, inc=1, device_id=place(to), device_id_type=pl.DeviceIdType.MESH)
        return carry

    def send(d, carry):
        to = lax.rem(me + d, devices)
        pltpu.make_async_remote_copy(
            src_ref=out_ref.at[block(to)],
            dst_ref=in_ref.at[block(me)],
            send_sem=send_sem,
            recv_sem=done_sem,
            device_id=place(to),
            device_id_type=pl.DeviceIdType.MESH,
        ).start()
        return carry

    loads = [
        pltpu.make_async_copy(gauss_hbm, gauss_ref, load_sem.at[0]),
        pltpu.make_async_copy(pick_hbm, pick_ref, load_sem.at[1]),
    ]
    for load in loads:
        load.start()
    lax.fori_loop(1, devices, greet, 0)
    for load in loads:
        load.wait()
    outgoing_kernel(gauss_ref, pick_ref, out_ref, *scratch)
    own = pltpu.make_async_copy(out_ref.at[block(me)], in_ref.at[block(me)], local_sem)
    own.start()
    own.wait()
    pl.semaphore_wait(barrier, devices - 1)
    lax.fori_loop(1, devices, send, 0)
    others = pl.ds(0, (devices - 1) * 8)
    pltpu.make_async_copy(out_ref.at[others], out_ref.at[others], send_sem).wait()
    pltpu.make_async_copy(in_ref.at[others], in_ref.at[others], done_sem).wait()


def deal(gaussians, picks):
    devices = picks.shape[1] // CAP
    rows = gaussians.shape[1] // (2 * LANES)
    vmem = pl.BlockSpec(memory_space=VMEM)
    f32 = jnp.float32
    return pl.pallas_call(
        deal_kernel,
        out_shape=jax.ShapeDtypeStruct((devices * 8, LANES), f32),
        in_specs=[pl.BlockSpec(memory_space=pltpu.HBM)] * 2,
        out_specs=vmem,
        scratch_shapes=[VMEM(gaussians.shape, f32), VMEM(picks.shape, jnp.int32), VMEM((devices * 8, LANES), f32)]
        + [pltpu.SemaphoreType.DMA] * 3
        + [pltpu.SemaphoreType.DMA((2,))]
        + [
            VMEM((SPLAT * rows, LANES), f32),
            VMEM((SPLAT * rows, LANES), f32),
            VMEM((SPLAT * rows, 512), jnp.bfloat16),
            VMEM((2 * rows, 256), jnp.bfloat16),
            VMEM((8 * LANES, LANES), f32),
            VMEM((gaussians.shape[1] // LANES * 64, LANES), f32),
            VMEM((LANES, LANES), jnp.int32),
        ],
        compiler_params=pltpu.CompilerParams(collective_id=2, has_side_effects=True, vmem_limit_bytes=211 << 18),
        name="deal_splats",
    )(gaussians, picks)


SEG = 32
BLOCK = 8
COEFS = 32
PIXELS = TILE * TILE
CHUNK = 64


def monomials():
    pixel = np.arange(PIXELS)
    x = (pixel % TILE) - 7.5
    y = (pixel // TILE) - 7.5
    cols = np.stack([x * x, y * y, x * y, x, y, np.ones_like(x)], axis=1)
    return np.concatenate([cols, cols, cols, np.zeros((PIXELS, COEFS - 18))], axis=1).astype(np.float32)


def lane_pick(value, index, axis):
    return jnp.take_along_axis(value, index, axis=axis, mode="promise_in_bounds")


def blend_kernel(cols_here, first, base, arrived, lists, ends, mono, out_ref, again_ref,
                 table_a, table_b, table, third, packed, codes, params, coefs, power_a, power_b, state, total_ref,
                 carry_ref, carry_owner, owner, origin):
    tiles = first.shape[0] - 1
    runs = lists.shape[2] // SEG
    share = LANES // SEG
    groups = (first[tiles] + LANES - 1) // LANES
    per_group = SEG // BLOCK

    for p in range(8):
        flat = jnp.transpose(arrived[pl.ds(p, LANES, stride=8), :])
        for half, ref in enumerate((table_a, table_b)):
            ref[pl.ds(p, ROWS, stride=8), :] = flat[half * ROWS : (half + 1) * ROWS]
            if p == half:
                ref[8 * ROWS :, :] = flat[CAP : CAP + ROWS]
    fill_table(table, third, (table_a, table_b))

    upper = lax.broadcasted_iota(jnp.int32, (8, LANES), 0) < share
    packed[...] = jnp.full(packed.shape, -1, jnp.int32)
    for t in range(tiles):
        line = lambda c: jnp.broadcast_to(
            lists[t // cols_here, t % cols_here : t % cols_here + 1, c * LANES : (c + 1) * LANES], (8, LANES)
        )
        for c in range(0, runs // share, 2):
            packed[pl.ds(first[t] + c * share, 8), :] = jnp.where(upper, line(c), line(c + 1))

    ends_down = jnp.transpose(jnp.broadcast_to(ends[...], (LANES, LANES)))
    along = lax.broadcasted_iota(jnp.int32, (LANES, LANES), 1)

    def own(g, carry):
        past = ends_down <= along + g * LANES
        owner[pl.ds(g, 1), :] = jnp.sum(jnp.where(past, 1, 0), axis=0, keepdims=True)
        origin[pl.ds(g, 1), :] = jnp.max(jnp.where(past, ends_down, 0), axis=0, keepdims=True)
        return carry

    lax.fori_loop(0, groups + 1, own, 0)

    def turn(g, carry):
        lanes = jnp.transpose(packed[pl.ds(pl.multiple_of(g * LANES, LANES), LANES), :])
        place = lax.broadcasted_iota(jnp.int32, (1, LANES), 1) + g * LANES - origin[pl.ds(g, 1), :]
        place = jnp.bitwise_and(place, share - 1)
        slot = lanes[0:SEG]
        for c in range(1, share):
            slot = jnp.where(place == c, lanes[c * SEG : (c + 1) * SEG], slot)
        source = ((slot.astype(jnp.float32) + 0.5) * (1.0 / CAP)).astype(jnp.int32)
        k = slot - source * CAP
        code = source + jnp.where(k < ROWS, k * 256, (k - ROWS) * 256 + LANES)
        codes[pl.ds(pl.multiple_of(g * SEG, SEG), SEG), :] = jnp.where(slot >= 0, code, -1)
        return carry

    lax.fori_loop(0, groups, turn, 0)
    total_ref[...] = jnp.zeros_like(total_ref)
    carry_ref[...] = jnp.ones_like(carry_ref)
    carry_owner[...] = jnp.full(carry_owner.shape, -1, jnp.int32)

    def look(block, j):
        where = block * BLOCK + 2 * j
        code = jnp.concatenate([codes[pl.ds(where, 1), :], codes[pl.ds(where + 1, 1), :]], axis=1)
        return ((block % 3) * 72,) + lookup(table, third, code)

    def keep(j, slot, picked, ninth):
        for e in range(2):
            lanes = slice(e * LANES, (e + 1) * LANES)
            params[pl.ds(pl.multiple_of(slot + (2 * j + e) * 8, 8), 8), :] = picked[:, lanes]
            params[pl.ds(slot + 64 + 2 * j + e, 1), :] = ninth[:, lanes]

    def expand(block):
        slot = (block % 3) * 72
        m_x, m_y, a, b, c, o = [params[pl.ds(slot + p, BLOCK, stride=8), :] for p in range(6)]
        live = codes[pl.ds(pl.multiple_of(block * BLOCK, BLOCK), BLOCK), :] >= 0
        tile = owner[pl.ds(block // per_group, 1), :]
        tile_y = lax.shift_right_logical(tile, cols_here.bit_length() - 1)
        tile_x = jnp.bitwise_and(tile, cols_here - 1)
        u = m_x - (tile_x * TILE + base[0]).astype(jnp.float32)
        v = m_y - (tile_y * TILE + base[1]).astype(jnp.float32)
        level = LOG2E * (-0.5 * (a * u * u + c * v * v) - b * u * v)
        values = [
            (-0.5 * LOG2E) * a,
            (-0.5 * LOG2E) * c,
            -LOG2E * b,
            LOG2E * (a * u + b * v),
            LOG2E * (c * v + b * u),
            jnp.where(live, level + jnp.log2(o), -1e30),
        ]
        for i, value in enumerate(values):
            for part, rounded in enumerate(split(value, 3)):
                coefs[pl.ds(part * 6 + i, BLOCK, stride=COEFS), :] = rounded.astype(jnp.float32)

    def exponents(j):
        pair = [
            coefs[pl.ds((2 * j + e) * COEFS, COEFS), :].astype(jnp.bfloat16) for e in range(2)
        ]
        return jnp.dot(mono[...], jnp.concatenate(pair, axis=1), preferred_element_type=jnp.float32)

    def blend(block, j, power):
        slot = (block % 3) * 72
        at = lambda q, i: pl.ds(q * PIXELS + j * CHUNK + i * 8, 8)
        pieces = range(CHUNK // 8)
        left = [state[at(0, i), :] for i in pieces]
        colour = [[state[at(1 + ch, i), :] for i in pieces] for ch in range(3)]
        for k in range(BLOCK):
            rows = (slot + k * 8 + 6, slot + k * 8 + 7, slot + 64 + k)
            tints = [jnp.broadcast_to(params[pl.ds(r, 1), :], (8, LANES)) for r in rows]
            for i in pieces:
                alpha = jnp.exp2(power[k // 2, at(0, i), (k % 2) * LANES : (k % 2 + 1) * LANES])
                weight = left[i] * alpha
                left[i] = left[i] - weight
                for ch in range(3):
                    colour[ch][i] = colour[ch][i] + weight * tints[ch]
        for i in pieces:
            state[at(0, i), :] = left[i]
            for ch in range(3):
                state[at(1 + ch, i), :] = colour[ch][i]

    lane = lax.broadcasted_iota(jnp.int32, (8, LANES), 1)

    def flush(g):
        tile = jnp.broadcast_to(owner[pl.ds(g, 1), :], (8, LANES))
        left = state[0:PIXELS, :]
        same = []
        for d in (1, 2, 4, 8):
            same.append(((pltpu.roll(tile, d, 1) == tile) & (lane >= d))[0:1])
        for d, mask in zip((1, 2, 4, 8), same):
            left = left * jnp.where(mask, pltpu.roll(left, d, 1), 1.0)
        before = jnp.where(same[0], pltpu.roll(left, 1, 1), 1.0)
        goes_on = (tile == carry_owner[...])[0:1]
        behind = jnp.where(goes_on, carry_ref[...], 1.0)
        before = before * behind
        carry_ref[...] = jnp.broadcast_to((left * behind)[:, LANES - 1 :], (PIXELS, LANES))
        carry_owner[...] = jnp.broadcast_to(tile[:, LANES - 1 :], (8, LANES))
        member = lax.broadcasted_iota(jnp.int32, (tiles, LANES), 0) == tile[0:1]
        member = jnp.where(member, 1.0, 0.0).astype(jnp.bfloat16)
        member = jnp.concatenate([member, member], axis=1)
        for ch in range(3):
            part = before * state[(1 + ch) * PIXELS : (2 + ch) * PIXELS, :]
            pair = jnp.concatenate(split(part, 2), axis=1)
            total_ref[ch] += lax.dot_general(
                member, pair, (((1,), (1,)), ((), ())), preferred_element_type=jnp.float32
            )

    coefs[...] = jnp.zeros_like(coefs)
    steps = BLOCK // 2

    def look_ahead(block):
        for j, found in enumerate([look(block, j) for j in range(steps)]):
            keep(j, *found)
        expand(block)

    look_ahead(0)
    for j in range(steps):
        power_a[j] = exponents(j)
    look_ahead(1)

    def one_group(g, carry):
        state[0:PIXELS, :] = jnp.ones((PIXELS, LANES), jnp.float32)
        state[PIXELS:, :] = jnp.zeros((3 * PIXELS, LANES), jnp.float32)

        def two_blocks(i, carry):
            for which in range(2):
                block = g * per_group + 2 * i + which
                now, later = ((power_a, power_b), (power_b, power_a))[which]

                found = [look(block + 2, j) for j in range(steps)]
                for j in range(steps):
                    later[j] = exponents(j)
                for j in range(steps):
                    blend(block, j, now)
                for j in range(steps):
                    keep(j, *found[j])
                expand(block + 2)
            return carry

        lax.fori_loop(0, per_group // 2, two_blocks, 0)
        flush(g)
        return carry

    lax.fori_loop(0, groups, one_group, 0)

    piece = lax.broadcasted_iota(jnp.int32, (8, LANES), 1)
    inner, outer = piece % TILE, piece // TILE
    sub = lax.broadcasted_iota(jnp.int32, (8, LANES), 0)
    skew = (outer + 8 - sub) % 8 * TILE + inner
    down = (outer + 8 - sub) % 8
    back = (outer + sub) % 8 * TILE + inner
    for ch in range(3):
        for r in range(tiles // cols_here):
            for q in range(cols_here // 8):
                for h in range(2):
                    x = total_ref[ch, r * cols_here + q * 8 : r * cols_here + q * 8 + 8, h * LANES : (h + 1) * LANES]
                    x = lane_pick(lane_pick(lane_pick(x, skew, 1), down, 0), back, 1)
                    for ref in (out_ref, again_ref):
                        ref[ch, r * TILE + h * 8 : r * TILE + h * 8 + 8, q * LANES : (q + 1) * LANES] = x


def blend_tiles(first, base, arrived, lists, ends, cols_here):
    tiles = first.shape[0] - 1
    most = tiles * (lists.shape[2] // SEG) // LANES
    smem = pl.BlockSpec(memory_space=pltpu.SMEM)
    vmem = pl.BlockSpec(memory_space=VMEM)
    f32 = jnp.float32
    return pl.pallas_call(
        functools.partial(blend_kernel, cols_here),
        out_shape=(jax.ShapeDtypeStruct((3, tiles // cols_here * TILE, cols_here * TILE), f32),) * 2,
        in_specs=[smem] * 2 + [vmem] * 4,
        out_specs=(vmem, vmem),
        scratch_shapes=[
            VMEM((9 * ROWS, LANES), f32),
            VMEM((9 * ROWS, LANES), f32),
            VMEM((9 * ROWS, 512), jnp.bfloat16),
            VMEM((2 * ROWS, 256), jnp.bfloat16),
            VMEM(((most + 1) * LANES, LANES), jnp.int32),
            VMEM(((most + 1) * SEG, LANES), jnp.int32),
            VMEM((3 * 72, LANES), f32),
            VMEM((BLOCK * COEFS, LANES), f32),
            VMEM((BLOCK // 2, PIXELS, 256), f32),
            VMEM((BLOCK // 2, PIXELS, 256), f32),
            VMEM((4 * PIXELS, LANES), f32),
            VMEM((3, tiles, PIXELS), f32),
            VMEM((PIXELS, LANES), f32),
            VMEM((8, LANES), jnp.int32),
            VMEM((most + 8, LANES), jnp.int32),
            VMEM((most + 8, LANES), jnp.int32),
        ],
        compiler_params=pltpu.CompilerParams(vmem_limit_bytes=20 << 20),
        name="blend_tiles",
    )(first, base, arrived, lists, ends, jnp.asarray(monomials()).astype(jnp.bfloat16))


def arrange(tile_lists):
    rows_here, cols_here, list_len = tile_lists.shape
    tiles = rows_here * cols_here
    lists = tile_lists.reshape(tiles, list_len)
    live = (jnp.sum((lists >= 0).astype(jnp.int32), axis=1) + SEG - 1) // SEG
    number = jnp.arange(tiles, dtype=jnp.int32)
    ends = jnp.sum(jnp.where(number[None, :] <= number[:, None], live[None, :], 0), axis=1).astype(jnp.int32)
    first = jnp.concatenate([jnp.zeros((1,), jnp.int32), ends])
    half = TILE // 2
    base = jnp.stack(
        [lax.axis_index("gs") * (cols_here * TILE) + half, lax.axis_index("img") * (rows_here * TILE) + half]
    ).astype(jnp.int32)
    return first, base, ends.reshape(1, tiles)


EDGE = 8
TAPS = 5


def halo_kernel(rendered, truth, row_out, col_out, row_buf, col_buf, row_sem, col_sem, row_done, col_done):
    n_gs, n_img = lax.axis_size("gs"), lax.axis_size("img")
    g, i = lax.axis_index("gs"), lax.axis_index("img")
    place = lambda dg, di: {"gs": lax.rem(g + n_gs + dg, n_gs), "img": lax.rem(i + n_img + di, n_img)}
    around = [(dg, di) for dg in (-1, 0, 1) for di in (-1, 0, 1) if (dg, di) != (0, 0)]
    barrier = pltpu.get_barrier_semaphore()
    for dg, di in around:
        pl.semaphore_signal(barrier, inc=1, device_id=place(dg, di), device_id_type=pl.DeviceIdType.MESH)

    height, width = rendered.shape[1:]
    for c in range(6):
        source = (rendered, truth)[c // 3]
        image = source[c % 3]
        for side in range(2):
            edge = image[0:EDGE] if side == 0 else image[height - EDGE :]
            for half in range(2):
                row_buf[side, c, half] = edge[:, half * LANES : (half + 1) * LANES]
            columns = image[:, 0:LANES] if side == 0 else image[:, width - LANES :]
            turned = jnp.transpose(columns)
            col_buf[side, c] = turned[0:EDGE] if side == 0 else turned[LANES - EDGE :]

    pl.semaphore_wait(barrier, len(around))
    copies = []
    for side in range(2):
        step = -1 if side == 0 else 1
        copies.append(
            pltpu.make_async_remote_copy(
                src_ref=row_buf.at[side],
                dst_ref=row_out.at[side],
                send_sem=row_sem.at[side],
                recv_sem=row_done.at[side],
                device_id=place(0, step),
                device_id_type=pl.DeviceIdType.MESH,
            )
        )
        for di in (-1, 0, 1):
            copies.append(
                pltpu.make_async_remote_copy(
                    src_ref=col_buf.at[side],
                    dst_ref=col_out.at[side * 3 + di + 1],
                    send_sem=col_sem.at[side * 3 + di + 1],
                    recv_sem=col_done.at[side * 3 + di + 1],
                    device_id=place(step, di),
                    device_id_type=pl.DeviceIdType.MESH,
                )
            )
    for copy in copies:
        copy.start()
    for copy in copies:
        copy.wait()


def exchange_halos(rendered, truth):
    vmem = pl.BlockSpec(memory_space=VMEM)
    rows = (2, 6, 2, EDGE, LANES)
    f32 = jnp.float32
    return pl.pallas_call(
        halo_kernel,
        out_shape=(jax.ShapeDtypeStruct(rows, f32), jax.ShapeDtypeStruct((6, 6, EDGE, LANES), f32)),
        in_specs=[vmem] * 2,
        out_specs=(vmem, vmem),
        scratch_shapes=[
            VMEM(rows, f32),
            VMEM((2, 6, EDGE, LANES), f32),
            pltpu.SemaphoreType.DMA((2,)),
            pltpu.SemaphoreType.DMA((6,)),
            pltpu.SemaphoreType.DMA((2,)),
            pltpu.SemaphoreType.DMA((6,)),
        ],
        compiler_params=pltpu.CompilerParams(collective_id=1, has_side_effects=True, vmem_limit_bytes=8 << 20),
        name="exchange_halos",
    )(rendered, truth)


def window():
    offsets = np.arange(11, dtype=np.float32) - 5.0
    weights = np.exp(-offsets * offsets / np.float32(4.5))
    return [float(w) for w in weights / np.sum(weights)]


def loss_kernel(has, rendered, truth, rows, cols, out_ref, maps, summed, turned, likeness):
    height = rendered.shape[1]
    tall = height + 2 * EDGE
    start = lambda q, part: (q * 3 + part) * tall
    left, right, above, below = [has[n] > 0 for n in range(4)]
    keep = lambda flag, value: jnp.where(flag, value, 0.0)
    lane = lax.broadcasted_iota(jnp.int32, (EDGE, LANES), 1)
    gap = jnp.zeros((LANES - 2 * EDGE, LANES), jnp.float32)
    for c in range(6):
        image = (rendered, truth)[c // 3]
        for half in range(2):
            base = start(c, half)
            maps[base : base + EDGE, :] = keep(above, rows[1, c, half])
            maps[base + EDGE : base + EDGE + height, :] = image[c % 3, :, half * LANES : (half + 1) * LANES]
            maps[base + EDGE + height : base + tall, :] = keep(below, rows[0, c, half])
        base = start(c, 2)
        after = keep(right, cols[1, c])
        before = keep(left, cols[4, c])
        maps[base + EDGE : base + EDGE + height, :] = jnp.transpose(jnp.concatenate([after, gap, before], axis=0))
        mixed = []
        for flag, side in ((right, 0), (left, 3)):
            upper = keep(flag & above, cols[side + 2, c])
            lower = keep(flag & below, cols[side + 0, c])
            mixed.append(jnp.where(lane < LANES // 2, lower, upper))
        corners = jnp.transpose(jnp.concatenate([mixed[0], gap, mixed[1]], axis=0))
        maps[base : base + EDGE, :] = corners[LANES - EDGE :]
        maps[base + EDGE + height : base + tall, :] = corners[0:EDGE]

    def products(n, carry):
        for ch in range(3):
            for part in range(3):
                at = lambda q: pl.ds(pl.multiple_of(start(q + ch, part) + n * 8, 8), 8)
                r, t = maps[at(0), :], maps[at(3), :]
                maps[at(6), :] = r * r + t * t
                maps[at(9), :] = r * t
        return carry

    lax.fori_loop(0, tall // 8, products, 0)
    weights = window()

    def window_sum(ref, first):
        row = lambda d: ref[pl.ds(first + d, 8), :]
        total = weights[TAPS] * row(0)
        for d in range(1, TAPS + 1):
            total = total + weights[TAPS + d] * (row(d) + row(-d))
        return total

    def over_rows(n, carry):
        for q in range(12):
            for part in range(3):
                at = pl.ds(pl.multiple_of((q * 3 + part) * height + n * 8, 8), 8)
                summed[at, :] = window_sum(maps, start(q, part) + EDGE + n * 8)
        return carry

    lax.fori_loop(0, height // 8, over_rows, 0)
    wide = 2 * LANES + 2 * EDGE
    for q in range(12):
        blocks = [jnp.transpose(summed[(q * 3 + part) * height : (q * 3 + part + 1) * height, :]) for part in range(3)]
        base = q * wide
        turned[base : base + EDGE, :] = blocks[2][LANES - EDGE :]
        turned[base + EDGE : base + EDGE + LANES, :] = blocks[0]
        turned[base + EDGE + LANES : base + EDGE + 2 * LANES, :] = blocks[1]
        turned[base + EDGE + 2 * LANES : base + wide, :] = blocks[2][:EDGE]

    def over_columns(n, carry):
        alike = 0.0
        for ch in range(3):
            mean_r, mean_t, square, product = [
                window_sum(turned, (q + ch) * wide + EDGE + n * 8) for q in (0, 3, 6, 9)
            ]
            both = mean_r * mean_t
            squared = mean_r * mean_r + mean_t * mean_t
            above_line = (2.0 * both + stable_one) * (2.0 * (product - both) + stable_two)
            below_line = (squared + stable_one) * (square - squared + stable_two)
            alike = alike + above_line / below_line
        likeness[pl.ds(pl.multiple_of(n * 8, 8), 8), :] = alike
        return carry

    lax.fori_loop(0, 2 * LANES // 8, over_columns, 0)
    for half in range(2):
        lanes = slice(half * LANES, (half + 1) * LANES)
        difference = jnp.abs(rendered[0, :, lanes] - truth[0, :, lanes])
        for ch in (1, 2):
            difference = difference + jnp.abs(rendered[ch, :, lanes] - truth[ch, :, lanes])
        alike = jnp.transpose(likeness[lanes, :])
        out_ref[:, lanes] = (1.0 - ssim_share) * (difference * (1.0 / 3.0)) + ssim_share * (1.0 - alike * (1.0 / 3.0))


def pixel_loss(has, rendered, truth, rows, cols):
    vmem = pl.BlockSpec(memory_space=VMEM)
    height, width = rendered.shape[1:]
    return pl.pallas_call(
        loss_kernel,
        out_shape=jax.ShapeDtypeStruct((height, width), jnp.float32),
        in_specs=[pl.BlockSpec(memory_space=pltpu.SMEM)] + [vmem] * 4,
        out_specs=vmem,
        scratch_shapes=[
            VMEM((12 * 3 * (height + 2 * EDGE), LANES), jnp.float32),
            VMEM((12 * 3 * height, LANES), jnp.float32),
            VMEM((12 * (width + 2 * EDGE), LANES), jnp.float32),
            VMEM((width, LANES), jnp.float32),
        ],
        compiler_params=pltpu.CompilerParams(vmem_limit_bytes=16 << 20),
        name="pixel_loss",
    )(has, rendered, truth, rows, cols)


def on_device(gaussians, send_slots, tile_lists, truth):
    rows_here, cols_here, list_len = tile_lists.shape
    arrived = deal(gaussians, send_slots)
    first, base, ends = arrange(tile_lists)
    rendered, again = blend_tiles(first, base, arrived, tile_lists, ends, cols_here)
    rows, cols = exchange_halos(again, truth)
    g, i = lax.axis_index("gs"), lax.axis_index("img")
    has = jnp.stack([g > 0, g < lax.axis_size("gs") - 1, i > 0, i < lax.axis_size("img") - 1]).astype(jnp.int32)
    return (rendered, pixel_loss(has, again, truth, rows, cols))


def solution(mesh):
    return jax.shard_map(
        on_device,
        mesh=mesh,
        in_specs=(
            P(None, ("gs", "img")),
            P(("gs", "img"), None),
            P("img", "gs", None),
            P(None, "img", "gs"),
        ),
        out_specs=(P(None, "img", "gs"), P("img", "gs")),
        check_vma=False,
    )
```

```python
import functools
import math

import jax
import jax.numpy as jnp
import numpy as np
from jax import lax
from jax.experimental import pallas as pl
from jax.experimental.pallas import tpu as pltpu
from jax.sharding import PartitionSpec as P

TILE = 16
LANES = 128
CAP = 80
SPLAT = 9
ROWS = CAP // 2
LOG2E = 1.0 / math.log(2.0)
VMEM = pltpu.VMEM


coef_zero = 0.28209479177387814
coef_one = 0.4886025119029199
coef_two = [
    1.0925484305920792,
    -1.0925484305920792,
    0.31539156525252005,
    -1.0925484305920792,
    0.5462742152960396,
]
coef_three = [
    -0.5900435899266435,
    2.890611442640554,
    -0.4570457994644658,
    0.3731763325901154,
    -0.4570457994644658,
    1.445305721320277,
    -0.5900435899266435,
]
camera_z = -3000.0
ssim_share = 0.2
stable_one = 0.0001
stable_two = 0.0009


def project(row):
    mean_x, mean_y, mean_z = (row(0), row(1), row(2))
    sq_0, sq_1, sq_2 = [jnp.exp(2.0 * row(i)) for i in (3, 4, 5)]
    inv = 1.0 / jnp.sqrt(row(6) * row(6) + row(7) * row(7) + row(8) * row(8) + row(9) * row(9))
    quat_w, quat_x, quat_y, quat_z = (row(6) * inv, row(7) * inv, row(8) * inv, row(9) * inv)
    first_a = 1.0 - 2.0 * (quat_y * quat_y + quat_z * quat_z)
    first_b = 2.0 * (quat_x * quat_y - quat_w * quat_z)
    first_c = 2.0 * (quat_x * quat_z + quat_w * quat_y)
    second_a = 2.0 * (quat_x * quat_y + quat_w * quat_z)
    second_b = 1.0 - 2.0 * (quat_x * quat_x + quat_z * quat_z)
    second_c = 2.0 * (quat_y * quat_z - quat_w * quat_x)
    cov_xx = first_a * first_a * sq_0 + first_b * first_b * sq_1 + first_c * first_c * sq_2 + 0.3
    cov_xy = first_a * second_a * sq_0 + first_b * second_b * sq_1 + first_c * second_c * sq_2
    cov_yy = second_a * second_a * sq_0 + second_b * second_b * sq_1 + second_c * second_c * sq_2 + 0.3
    determinant = cov_xx * cov_yy - cov_xy * cov_xy
    opacity = 1.0 / (1.0 + jnp.exp(-row(10)))
    delta_z = mean_z - camera_z
    length = jnp.sqrt(mean_x * mean_x + mean_y * mean_y + delta_z * delta_z)
    dir_x, dir_y, dir_z = (mean_x / length, mean_y / length, delta_z / length)
    sq_x, sq_y, sq_z = (dir_x * dir_x, dir_y * dir_y, dir_z * dir_z)
    prod_xy, prod_yz, prod_xz = (dir_x * dir_y, dir_y * dir_z, dir_x * dir_z)
    basis = [
        coef_zero * jnp.ones_like(dir_x),
        -coef_one * dir_y,
        coef_one * dir_z,
        -coef_one * dir_x,
        coef_two[0] * prod_xy,
        coef_two[1] * prod_yz,
        coef_two[2] * (2.0 * sq_z - sq_x - sq_y),
        coef_two[3] * prod_xz,
        coef_two[4] * (sq_x - sq_y),
        coef_three[0] * dir_y * (3.0 * sq_x - sq_y),
        coef_three[1] * prod_xy * dir_z,
        coef_three[2] * dir_y * (4.0 * sq_z - sq_x - sq_y),
        coef_three[3] * dir_z * (2.0 * sq_z - 3.0 * sq_x - 3.0 * sq_y),
        coef_three[4] * dir_x * (4.0 * sq_z - sq_x - sq_y),
        coef_three[5] * dir_z * (sq_x - sq_y),
        coef_three[6] * dir_x * (sq_x - 3.0 * sq_y),
    ]
    colour = []
    for channel in range(3):
        total = 0.5
        for k, value in enumerate(basis):
            total = total + row(11 + 16 * channel + k) * value
        colour.append(jnp.maximum(total, 0.0))
    return [
        mean_x,
        mean_y,
        cov_yy / determinant,
        -cov_xy / determinant,
        cov_xx / determinant,
        opacity,
    ] + colour


def split(value, parts):
    out = []
    for _ in range(parts):
        rounded = value.astype(jnp.bfloat16)
        out.append(rounded)
        value = value - rounded.astype(jnp.float32)
    return out


def fill_table(table, third, halves):
    rows = third.shape[0] // 2
    for half, ref in enumerate(halves):
        lanes = slice(half * LANES, (half + 1) * LANES)
        for part, value in enumerate(split(ref[...], 2)):
            table[:, part * 256 + half * LANES : part * 256 + (half + 1) * LANES] = value
        for p in range(2):
            third[p * rows : (p + 1) * rows, lanes] = split(ref[pl.ds(p, rows, stride=8), :], 3)[2]


def lookup(table, third, code):
    rows = table.shape[0] // SPLAT
    column = lax.broadcasted_iota(jnp.int32, (256, 256), 0).astype(jnp.float32).astype(jnp.bfloat16)
    col = jnp.bitwise_and(code, 255).astype(jnp.float32).astype(jnp.bfloat16)
    row = lax.shift_right_arithmetic(code, 8)
    hot = jnp.where(column == col, jnp.bfloat16(1), jnp.bfloat16(0))
    found = jnp.dot(table[...], jnp.concatenate([hot, hot], axis=0), preferred_element_type=jnp.float32)
    finer = jnp.dot(third[...], hot, preferred_element_type=jnp.float32)
    picked = jnp.zeros((8, 256), jnp.float32)
    rows8 = jnp.broadcast_to(row, (8, 256))
    for r in range(rows):
        picked = jnp.where(rows8 == r, found[r * 8 : (r + 1) * 8], picked)
    table_row = lax.broadcasted_iota(jnp.int32, (rows, 256), 0)
    choose = lambda lines: jnp.sum(jnp.where(table_row == row, lines, 0.0), axis=0, keepdims=True)
    sub = lax.broadcasted_iota(jnp.int32, (8, 256), 0)
    for p in range(2):
        picked = picked + jnp.where(sub == p, choose(finer[p * rows : (p + 1) * rows]), 0.0)
    return picked, choose(found[8 * rows :])


def outgoing_kernel(gauss_ref, pick_ref, out_ref, table_a, table_b, table, third, eight, chunks, turned):
    blocks = gauss_ref.shape[1] // LANES
    rows = blocks // 2
    height = 64
    for block in range(blocks):
        piece = gauss_ref[:, block * LANES : (block + 1) * LANES]
        chunks[block * height : block * height + gauss_ref.shape[0], :] = piece
    for block in range(0, blocks, 8):
        splat = project(lambda i: chunks[pl.ds(block * height + i, 8, stride=height), :])
        for half, ref in enumerate((table_a, table_b)):
            low, high = max(block, half * rows), min(block + 8, (half + 1) * rows)
            if low < high:
                r, part = low - half * rows, slice(low - block, high - block)
                for p in range(8):
                    ref[pl.ds(r * 8 + p, high - low, stride=8), :] = splat[p][part]
                ref[8 * rows + r : 8 * rows + r + high - low, :] = splat[8][part]
    for d in range(LANES):
        turned[d : d + 1, 0:CAP] = pick_ref[:, d * CAP : (d + 1) * CAP]
    turned[...] = jnp.transpose(turned[...])
    fill_table(table, third, (table_a, table_b))

    def eight_slots(i, carry):
        where = pl.multiple_of(i * 8, 8)
        picks = turned[pl.ds(where, 8), :]
        block = lax.shift_right_logical(picks, 7)
        codes = jnp.bitwise_and(picks, LANES - 1) + jnp.where(block < rows, block * 256, (block - rows) * 256 + LANES)
        found = [
            lookup(table, third, jnp.concatenate([codes[2 * j : 2 * j + 1], codes[2 * j + 1 : 2 * j + 2]], axis=1))
            for j in range(4)
        ]
        for j, (first, last) in enumerate(found):
            for e in range(2):
                lanes = slice(e * LANES, (e + 1) * LANES)
                eight[pl.ds(where * 8 + (2 * j + e) * 8, 8), :] = first[:, lanes]
                k = where + 2 * j + e
                eight[pl.ds((CAP + k % ROWS) * 8 + k // ROWS, 1), :] = last[:, lanes]
        return carry

    eight[CAP * 8 :, :] = jnp.zeros((eight.shape[0] - CAP * 8, LANES), jnp.float32)
    lax.fori_loop(0, CAP // 8, eight_slots, 0)
    for p in range(8):
        out_ref[pl.ds(p, LANES, stride=8), :] = jnp.transpose(eight[pl.ds(p, LANES, stride=8), :])


def deal_kernel(gauss_hbm, pick_hbm, in_ref, gauss_ref, pick_ref, out_ref, send_sem, done_sem, local_sem, load_sem, *scratch):
    n_gs, n_img = lax.axis_size("gs"), lax.axis_size("img")
    devices = n_gs * n_img
    me = lax.axis_index("gs") * n_img + lax.axis_index("img")
    place = lambda d: {"gs": lax.div(d, n_img), "img": lax.rem(d, n_img)}
    block = lambda d: pl.ds(pl.multiple_of(d * 8, 8), 8)
    barrier = pltpu.get_barrier_semaphore()

    def greet(d, carry):
        to = lax.rem(me + d, devices)
        pl.semaphore_signal(barrier, inc=1, device_id=place(to), device_id_type=pl.DeviceIdType.MESH)
        return carry

    def send(d, carry):
        to = lax.rem(me + d, devices)
        pltpu.make_async_remote_copy(
            src_ref=out_ref.at[block(to)],
            dst_ref=in_ref.at[block(me)],
            send_sem=send_sem,
            recv_sem=done_sem,
            device_id=place(to),
            device_id_type=pl.DeviceIdType.MESH,
        ).start()
        return carry

    loads = [
        pltpu.make_async_copy(gauss_hbm, gauss_ref, load_sem.at[0]),
        pltpu.make_async_copy(pick_hbm, pick_ref, load_sem.at[1]),
    ]
    for load in loads:
        load.start()
    lax.fori_loop(1, devices, greet, 0)
    for load in loads:
        load.wait()
    outgoing_kernel(gauss_ref, pick_ref, out_ref, *scratch)
    own = pltpu.make_async_copy(out_ref.at[block(me)], in_ref.at[block(me)], local_sem)
    own.start()
    own.wait()
    pl.semaphore_wait(barrier, devices - 1)
    lax.fori_loop(1, devices, send, 0)
    others = pl.ds(0, (devices - 1) * 8)
    pltpu.make_async_copy(out_ref.at[others], out_ref.at[others], send_sem).wait()
    pltpu.make_async_copy(in_ref.at[others], in_ref.at[others], done_sem).wait()


def deal(gaussians, picks):
    devices = picks.shape[1] // CAP
    rows = gaussians.shape[1] // (2 * LANES)
    vmem = pl.BlockSpec(memory_space=VMEM)
    f32 = jnp.float32
    return pl.pallas_call(
        deal_kernel,
        out_shape=jax.ShapeDtypeStruct((devices * 8, LANES), f32),
        in_specs=[pl.BlockSpec(memory_space=pltpu.HBM)] * 2,
        out_specs=vmem,
        scratch_shapes=[VMEM(gaussians.shape, f32), VMEM(picks.shape, jnp.int32), VMEM((devices * 8, LANES), f32)]
        + [pltpu.SemaphoreType.DMA] * 3
        + [pltpu.SemaphoreType.DMA((2,))]
        + [
            VMEM((SPLAT * rows, LANES), f32),
            VMEM((SPLAT * rows, LANES), f32),
            VMEM((SPLAT * rows, 512), jnp.bfloat16),
            VMEM((2 * rows, 256), jnp.bfloat16),
            VMEM((8 * LANES, LANES), f32),
            VMEM((gaussians.shape[1] // LANES * 64, LANES), f32),
            VMEM((LANES, LANES), jnp.int32),
        ],
        compiler_params=pltpu.CompilerParams(collective_id=2, has_side_effects=True, vmem_limit_bytes=211 << 18),
        name="deal_splats",
    )(gaussians, picks)


SEG = 32
BLOCK = 8
COEFS = 32
PIXELS = TILE * TILE
CHUNK = 64


def monomials():
    pixel = np.arange(PIXELS)
    x = (pixel % TILE) - 7.5
    y = (pixel // TILE) - 7.5
    cols = np.stack([x * x, y * y, x * y, x, y, np.ones_like(x)], axis=1)
    return np.concatenate([cols, cols, cols, np.zeros((PIXELS, COEFS - 18))], axis=1).astype(np.float32)


def lane_pick(value, index, axis):
    return jnp.take_along_axis(value, index, axis=axis, mode="promise_in_bounds")


def blend_kernel(cols_here, first, base, arrived, lists, ends, mono, out_ref, again_ref,
                 table_a, table_b, table, third, packed, codes, params, coefs, power_a, power_b, state, total_ref,
                 carry_ref, carry_owner, owner, origin):
    tiles = first.shape[0] - 1
    runs = lists.shape[2] // SEG
    share = LANES // SEG
    groups = (first[tiles] + LANES - 1) // LANES
    per_group = SEG // BLOCK

    for p in range(8):
        flat = jnp.transpose(arrived[pl.ds(p, LANES, stride=8), :])
        for half, ref in enumerate((table_a, table_b)):
            ref[pl.ds(p, ROWS, stride=8), :] = flat[half * ROWS : (half + 1) * ROWS]
            if p == half:
                ref[8 * ROWS :, :] = flat[CAP : CAP + ROWS]
    fill_table(table, third, (table_a, table_b))

    upper = lax.broadcasted_iota(jnp.int32, (8, LANES), 0) < share
    packed[...] = jnp.full(packed.shape, -1, jnp.int32)
    for t in range(tiles):
        line = lambda c: jnp.broadcast_to(
            lists[t // cols_here, t % cols_here : t % cols_here + 1, c * LANES : (c + 1) * LANES], (8, LANES)
        )
        for c in range(0, runs // share, 2):
            packed[pl.ds(first[t] + c * share, 8), :] = jnp.where(upper, line(c), line(c + 1))

    ends_down = jnp.transpose(jnp.broadcast_to(ends[...], (LANES, LANES)))
    along = lax.broadcasted_iota(jnp.int32, (LANES, LANES), 1)

    def own(g, carry):
        past = ends_down <= along + g * LANES
        owner[pl.ds(g, 1), :] = jnp.sum(jnp.where(past, 1, 0), axis=0, keepdims=True)
        origin[pl.ds(g, 1), :] = jnp.max(jnp.where(past, ends_down, 0), axis=0, keepdims=True)
        return carry

    lax.fori_loop(0, groups + 1, own, 0)

    def turn(g, carry):
        lanes = jnp.transpose(packed[pl.ds(pl.multiple_of(g * LANES, LANES), LANES), :])
        place = lax.broadcasted_iota(jnp.int32, (1, LANES), 1) + g * LANES - origin[pl.ds(g, 1), :]
        place = jnp.bitwise_and(place, share - 1)
        slot = lanes[0:SEG]
        for c in range(1, share):
            slot = jnp.where(place == c, lanes[c * SEG : (c + 1) * SEG], slot)
        source = ((slot.astype(jnp.float32) + 0.5) * (1.0 / CAP)).astype(jnp.int32)
        k = slot - source * CAP
        code = source + jnp.where(k < ROWS, k * 256, (k - ROWS) * 256 + LANES)
        codes[pl.ds(pl.multiple_of(g * SEG, SEG), SEG), :] = jnp.where(slot >= 0, code, -1)
        return carry

    lax.fori_loop(0, groups, turn, 0)
    total_ref[...] = jnp.zeros_like(total_ref)
    carry_ref[...] = jnp.ones_like(carry_ref)
    carry_owner[...] = jnp.full(carry_owner.shape, -1, jnp.int32)

    def look(block, j):
        where = block * BLOCK + 2 * j
        code = jnp.concatenate([codes[pl.ds(where, 1), :], codes[pl.ds(where + 1, 1), :]], axis=1)
        return ((block % 3) * 72,) + lookup(table, third, code)

    def keep(j, slot, picked, ninth):
        for e in range(2):
            lanes = slice(e * LANES, (e + 1) * LANES)
            params[pl.ds(pl.multiple_of(slot + (2 * j + e) * 8, 8), 8), :] = picked[:, lanes]
            params[pl.ds(slot + 64 + 2 * j + e, 1), :] = ninth[:, lanes]

    def expand(block):
        slot = (block % 3) * 72
        m_x, m_y, a, b, c, o = [params[pl.ds(slot + p, BLOCK, stride=8), :] for p in range(6)]
        live = codes[pl.ds(pl.multiple_of(block * BLOCK, BLOCK), BLOCK), :] >= 0
        tile = owner[pl.ds(block // per_group, 1), :]
        tile_y = lax.shift_right_logical(tile, cols_here.bit_length() - 1)
        tile_x = jnp.bitwise_and(tile, cols_here - 1)
        u = m_x - (tile_x * TILE + base[0]).astype(jnp.float32)
        v = m_y - (tile_y * TILE + base[1]).astype(jnp.float32)
        level = LOG2E * (-0.5 * (a * u * u + c * v * v) - b * u * v)
        values = [
            (-0.5 * LOG2E) * a,
            (-0.5 * LOG2E) * c,
            -LOG2E * b,
            LOG2E * (a * u + b * v),
            LOG2E * (c * v + b * u),
            jnp.where(live, level + jnp.log2(o), -1e30),
        ]
        for i, value in enumerate(values):
            for part, rounded in enumerate(split(value, 3)):
                coefs[pl.ds(part * 6 + i, BLOCK, stride=COEFS), :] = rounded.astype(jnp.float32)

    def exponents(j):
        pair = [
            coefs[pl.ds((2 * j + e) * COEFS, COEFS), :].astype(jnp.bfloat16) for e in range(2)
        ]
        return jnp.dot(mono[...], jnp.concatenate(pair, axis=1), preferred_element_type=jnp.float32)

    def blend(block, j, power):
        slot = (block % 3) * 72
        at = lambda q, i: pl.ds(q * PIXELS + j * CHUNK + i * 8, 8)
        pieces = range(CHUNK // 8)
        left = [state[at(0, i), :] for i in pieces]
        colour = [[state[at(1 + ch, i), :] for i in pieces] for ch in range(3)]
        for k in range(BLOCK):
            rows = (slot + k * 8 + 6, slot + k * 8 + 7, slot + 64 + k)
            tints = [jnp.broadcast_to(params[pl.ds(r, 1), :], (8, LANES)) for r in rows]
            for i in pieces:
                alpha = jnp.exp2(power[k // 2, at(0, i), (k % 2) * LANES : (k % 2 + 1) * LANES])
                weight = left[i] * alpha
                left[i] = left[i] - weight
                for ch in range(3):
                    colour[ch][i] = colour[ch][i] + weight * tints[ch]
        for i in pieces:
            state[at(0, i), :] = left[i]
            for ch in range(3):
                state[at(1 + ch, i), :] = colour[ch][i]

    lane = lax.broadcasted_iota(jnp.int32, (8, LANES), 1)

    def flush(g):
        tile = jnp.broadcast_to(owner[pl.ds(g, 1), :], (8, LANES))
        left = state[0:PIXELS, :]
        same = []
        for d in (1, 2, 4, 8):
            same.append(((pltpu.roll(tile, d, 1) == tile) & (lane >= d))[0:1])
        for d, mask in zip((1, 2, 4, 8), same):
            left = left * jnp.where(mask, pltpu.roll(left, d, 1), 1.0)
        before = jnp.where(same[0], pltpu.roll(left, 1, 1), 1.0)
        goes_on = (tile == carry_owner[...])[0:1]
        behind = jnp.where(goes_on, carry_ref[...], 1.0)
        before = before * behind
        carry_ref[...] = jnp.broadcast_to((left * behind)[:, LANES - 1 :], (PIXELS, LANES))
        carry_owner[...] = jnp.broadcast_to(tile[:, LANES - 1 :], (8, LANES))
        member = lax.broadcasted_iota(jnp.int32, (tiles, LANES), 0) == tile[0:1]
        member = jnp.where(member, 1.0, 0.0).astype(jnp.bfloat16)
        member = jnp.concatenate([member, member], axis=1)
        for ch in range(3):
            part = before * state[(1 + ch) * PIXELS : (2 + ch) * PIXELS, :]
            pair = jnp.concatenate(split(part, 2), axis=1)
            total_ref[ch] += lax.dot_general(
                member, pair, (((1,), (1,)), ((), ())), preferred_element_type=jnp.float32
            )

    coefs[...] = jnp.zeros_like(coefs)
    steps = BLOCK // 2

    def look_ahead(block):
        for j, found in enumerate([look(block, j) for j in range(steps)]):
            keep(j, *found)
        expand(block)

    look_ahead(0)
    for j in range(steps):
        power_a[j] = exponents(j)
    look_ahead(1)

    def one_group(g, carry):
        state[0:PIXELS, :] = jnp.ones((PIXELS, LANES), jnp.float32)
        state[PIXELS:, :] = jnp.zeros((3 * PIXELS, LANES), jnp.float32)

        def two_blocks(i, carry):
            for which in range(2):
                block = g * per_group + 2 * i + which
                now, later = ((power_a, power_b), (power_b, power_a))[which]

                found = [look(block + 2, j) for j in range(steps)]
                for j in range(steps):
                    later[j] = exponents(j)
                for j in range(steps):
                    blend(block, j, now)
                for j in range(steps):
                    keep(j, *found[j])
                expand(block + 2)
            return carry

        lax.fori_loop(0, per_group // 2, two_blocks, 0)
        flush(g)
        return carry

    lax.fori_loop(0, groups, one_group, 0)

    piece = lax.broadcasted_iota(jnp.int32, (8, LANES), 1)
    inner, outer = piece % TILE, piece // TILE
    sub = lax.broadcasted_iota(jnp.int32, (8, LANES), 0)
    skew = (outer + 8 - sub) % 8 * TILE + inner
    down = (outer + 8 - sub) % 8
    back = (outer + sub) % 8 * TILE + inner
    for ch in range(3):
        for r in range(tiles // cols_here):
            for q in range(cols_here // 8):
                for h in range(2):
                    x = total_ref[ch, r * cols_here + q * 8 : r * cols_here + q * 8 + 8, h * LANES : (h + 1) * LANES]
                    x = lane_pick(lane_pick(lane_pick(x, skew, 1), down, 0), back, 1)
                    for ref in (out_ref, again_ref):
                        ref[ch, r * TILE + h * 8 : r * TILE + h * 8 + 8, q * LANES : (q + 1) * LANES] = x


def blend_tiles(first, base, arrived, lists, ends, cols_here):
    tiles = first.shape[0] - 1
    most = tiles * (lists.shape[2] // SEG) // LANES
    smem = pl.BlockSpec(memory_space=pltpu.SMEM)
    vmem = pl.BlockSpec(memory_space=VMEM)
    f32 = jnp.float32
    return pl.pallas_call(
        functools.partial(blend_kernel, cols_here),
        out_shape=(jax.ShapeDtypeStruct((3, tiles // cols_here * TILE, cols_here * TILE), f32),) * 2,
        in_specs=[smem] * 2 + [vmem] * 4,
        out_specs=(vmem, vmem),
        scratch_shapes=[
            VMEM((9 * ROWS, LANES), f32),
            VMEM((9 * ROWS, LANES), f32),
            VMEM((9 * ROWS, 512), jnp.bfloat16),
            VMEM((2 * ROWS, 256), jnp.bfloat16),
            VMEM(((most + 1) * LANES, LANES), jnp.int32),
            VMEM(((most + 1) * SEG, LANES), jnp.int32),
            VMEM((3 * 72, LANES), f32),
            VMEM((BLOCK * COEFS, LANES), f32),
            VMEM((BLOCK // 2, PIXELS, 256), f32),
            VMEM((BLOCK // 2, PIXELS, 256), f32),
            VMEM((4 * PIXELS, LANES), f32),
            VMEM((3, tiles, PIXELS), f32),
            VMEM((PIXELS, LANES), f32),
            VMEM((8, LANES), jnp.int32),
            VMEM((most + 8, LANES), jnp.int32),
            VMEM((most + 8, LANES), jnp.int32),
        ],
        compiler_params=pltpu.CompilerParams(vmem_limit_bytes=20 << 20),
        name="blend_tiles",
    )(first, base, arrived, lists, ends, jnp.asarray(monomials()).astype(jnp.bfloat16))


def arrange(tile_lists):
    rows_here, cols_here, list_len = tile_lists.shape
    tiles = rows_here * cols_here
    lists = tile_lists.reshape(tiles, list_len)
    live = (jnp.sum((lists >= 0).astype(jnp.int32), axis=1) + SEG - 1) // SEG
    number = jnp.arange(tiles, dtype=jnp.int32)
    ends = jnp.sum(jnp.where(number[None, :] <= number[:, None], live[None, :], 0), axis=1).astype(jnp.int32)
    first = jnp.concatenate([jnp.zeros((1,), jnp.int32), ends])
    half = TILE // 2
    base = jnp.stack(
        [lax.axis_index("gs") * (cols_here * TILE) + half, lax.axis_index("img") * (rows_here * TILE) + half]
    ).astype(jnp.int32)
    return first, base, ends.reshape(1, tiles)


EDGE = 8
TAPS = 5


def halo_kernel(rendered, truth, row_out, col_out, row_buf, col_buf, row_sem, col_sem, row_done, col_done):
    n_gs, n_img = lax.axis_size("gs"), lax.axis_size("img")
    g, i = lax.axis_index("gs"), lax.axis_index("img")
    place = lambda dg, di: {"gs": lax.rem(g + n_gs + dg, n_gs), "img": lax.rem(i + n_img + di, n_img)}
    around = [(dg, di) for dg in (-1, 0, 1) for di in (-1, 0, 1) if (dg, di) != (0, 0)]
    barrier = pltpu.get_barrier_semaphore()
    for dg, di in around:
        pl.semaphore_signal(barrier, inc=1, device_id=place(dg, di), device_id_type=pl.DeviceIdType.MESH)

    height, width = rendered.shape[1:]
    for c in range(6):
        source = (rendered, truth)[c // 3]
        image = source[c % 3]
        for side in range(2):
            edge = image[0:EDGE] if side == 0 else image[height - EDGE :]
            for half in range(2):
                row_buf[side, c, half] = edge[:, half * LANES : (half + 1) * LANES]
            columns = image[:, 0:LANES] if side == 0 else image[:, width - LANES :]
            turned = jnp.transpose(columns)
            col_buf[side, c] = turned[0:EDGE] if side == 0 else turned[LANES - EDGE :]

    pl.semaphore_wait(barrier, len(around))
    copies = []
    for side in range(2):
        step = -1 if side == 0 else 1
        copies.append(
            pltpu.make_async_remote_copy(
                src_ref=row_buf.at[side],
                dst_ref=row_out.at[side],
                send_sem=row_sem.at[side],
                recv_sem=row_done.at[side],
                device_id=place(0, step),
                device_id_type=pl.DeviceIdType.MESH,
            )
        )
        for di in (-1, 0, 1):
            copies.append(
                pltpu.make_async_remote_copy(
                    src_ref=col_buf.at[side],
                    dst_ref=col_out.at[side * 3 + di + 1],
                    send_sem=col_sem.at[side * 3 + di + 1],
                    recv_sem=col_done.at[side * 3 + di + 1],
                    device_id=place(step, di),
                    device_id_type=pl.DeviceIdType.MESH,
                )
            )
    for copy in copies:
        copy.start()
    for copy in copies:
        copy.wait()


def exchange_halos(rendered, truth):
    vmem = pl.BlockSpec(memory_space=VMEM)
    rows = (2, 6, 2, EDGE, LANES)
    f32 = jnp.float32
    return pl.pallas_call(
        halo_kernel,
        out_shape=(jax.ShapeDtypeStruct(rows, f32), jax.ShapeDtypeStruct((6, 6, EDGE, LANES), f32)),
        in_specs=[vmem] * 2,
        out_specs=(vmem, vmem),
        scratch_shapes=[
            VMEM(rows, f32),
            VMEM((2, 6, EDGE, LANES), f32),
            pltpu.SemaphoreType.DMA((2,)),
            pltpu.SemaphoreType.DMA((6,)),
            pltpu.SemaphoreType.DMA((2,)),
            pltpu.SemaphoreType.DMA((6,)),
        ],
        compiler_params=pltpu.CompilerParams(collective_id=1, has_side_effects=True, vmem_limit_bytes=8 << 20),
        name="exchange_halos",
    )(rendered, truth)


def window():
    offsets = np.arange(11, dtype=np.float32) - 5.0
    weights = np.exp(-offsets * offsets / np.float32(4.5))
    return [float(w) for w in weights / np.sum(weights)]


def loss_kernel(has, rendered, truth, rows, cols, out_ref, maps, summed, turned, likeness):
    height = rendered.shape[1]
    tall = height + 2 * EDGE
    start = lambda q, part: (q * 3 + part) * tall
    left, right, above, below = [has[n] > 0 for n in range(4)]
    keep = lambda flag, value: jnp.where(flag, value, 0.0)
    lane = lax.broadcasted_iota(jnp.int32, (EDGE, LANES), 1)
    gap = jnp.zeros((LANES - 2 * EDGE, LANES), jnp.float32)
    for c in range(6):
        image = (rendered, truth)[c // 3]
        for half in range(2):
            base = start(c, half)
            maps[base : base + EDGE, :] = keep(above, rows[1, c, half])
            maps[base + EDGE : base + EDGE + height, :] = image[c % 3, :, half * LANES : (half + 1) * LANES]
            maps[base + EDGE + height : base + tall, :] = keep(below, rows[0, c, half])
        base = start(c, 2)
        after = keep(right, cols[1, c])
        before = keep(left, cols[4, c])
        maps[base + EDGE : base + EDGE + height, :] = jnp.transpose(jnp.concatenate([after, gap, before], axis=0))
        mixed = []
        for flag, side in ((right, 0), (left, 3)):
            upper = keep(flag & above, cols[side + 2, c])
            lower = keep(flag & below, cols[side + 0, c])
            mixed.append(jnp.where(lane < LANES // 2, lower, upper))
        corners = jnp.transpose(jnp.concatenate([mixed[0], gap, mixed[1]], axis=0))
        maps[base : base + EDGE, :] = corners[LANES - EDGE :]
        maps[base + EDGE + height : base + tall, :] = corners[0:EDGE]

    def products(n, carry):
        for ch in range(3):
            for part in range(3):
                at = lambda q: pl.ds(pl.multiple_of(start(q + ch, part) + n * 8, 8), 8)
                r, t = maps[at(0), :], maps[at(3), :]
                maps[at(6), :] = r * r + t * t
                maps[at(9), :] = r * t
        return carry

    lax.fori_loop(0, tall // 8, products, 0, unroll=3)
    weights = window()

    def window_sum(ref, first):
        row = lambda d: ref[pl.ds(first + d, 8), :]
        total = weights[TAPS] * row(0)
        for d in range(1, TAPS + 1):
            total = total + weights[TAPS + d] * (row(d) + row(-d))
        return total

    def over_rows(n, carry):
        for q in range(12):
            for part in range(3):
                at = pl.ds(pl.multiple_of((q * 3 + part) * height + n * 8, 8), 8)
                summed[at, :] = window_sum(maps, start(q, part) + EDGE + n * 8)
        return carry

    lax.fori_loop(0, height // 8, over_rows, 0, unroll=2)
    wide = 2 * LANES + 2 * EDGE
    for q in range(12):
        blocks = [jnp.transpose(summed[(q * 3 + part) * height : (q * 3 + part + 1) * height, :]) for part in range(3)]
        base = q * wide
        turned[base : base + EDGE, :] = blocks[2][LANES - EDGE :]
        turned[base + EDGE : base + EDGE + LANES, :] = blocks[0]
        turned[base + EDGE + LANES : base + EDGE + 2 * LANES, :] = blocks[1]
        turned[base + EDGE + 2 * LANES : base + wide, :] = blocks[2][:EDGE]

    def over_columns(n, carry):
        alike = 0.0
        for ch in range(3):
            mean_r, mean_t, square, product = [
                window_sum(turned, (q + ch) * wide + EDGE + n * 8) for q in (0, 3, 6, 9)
            ]
            both = mean_r * mean_t
            squared = mean_r * mean_r + mean_t * mean_t
            above_line = (2.0 * both + stable_one) * (2.0 * (product - both) + stable_two)
            below_line = (squared + stable_one) * (square - squared + stable_two)
            alike = alike + above_line / below_line
        likeness[pl.ds(pl.multiple_of(n * 8, 8), 8), :] = alike
        return carry

    lax.fori_loop(0, 2 * LANES // 8, over_columns, 0, unroll=4)
    for half in range(2):
        lanes = slice(half * LANES, (half + 1) * LANES)
        difference = jnp.abs(rendered[0, :, lanes] - truth[0, :, lanes])
        for ch in (1, 2):
            difference = difference + jnp.abs(rendered[ch, :, lanes] - truth[ch, :, lanes])
        alike = jnp.transpose(likeness[lanes, :])
        out_ref[:, lanes] = (1.0 - ssim_share) * (difference * (1.0 / 3.0)) + ssim_share * (1.0 - alike * (1.0 / 3.0))


def pixel_loss(has, rendered, truth, rows, cols):
    vmem = pl.BlockSpec(memory_space=VMEM)
    height, width = rendered.shape[1:]
    return pl.pallas_call(
        loss_kernel,
        out_shape=jax.ShapeDtypeStruct((height, width), jnp.float32),
        in_specs=[pl.BlockSpec(memory_space=pltpu.SMEM)] + [vmem] * 4,
        out_specs=vmem,
        scratch_shapes=[
            VMEM((12 * 3 * (height + 2 * EDGE), LANES), jnp.float32),
            VMEM((12 * 3 * height, LANES), jnp.float32),
            VMEM((12 * (width + 2 * EDGE), LANES), jnp.float32),
            VMEM((width, LANES), jnp.float32),
        ],
        compiler_params=pltpu.CompilerParams(vmem_limit_bytes=16 << 20),
        name="pixel_loss",
    )(has, rendered, truth, rows, cols)


def on_device(gaussians, send_slots, tile_lists, truth):
    rows_here, cols_here, list_len = tile_lists.shape
    arrived = deal(gaussians, send_slots)
    first, base, ends = arrange(tile_lists)
    rendered, again = blend_tiles(first, base, arrived, tile_lists, ends, cols_here)
    rows, cols = exchange_halos(again, truth)
    g, i = lax.axis_index("gs"), lax.axis_index("img")
    has = jnp.stack([g > 0, g < lax.axis_size("gs") - 1, i > 0, i < lax.axis_size("img") - 1]).astype(jnp.int32)
    return (rendered, pixel_loss(has, again, truth, rows, cols))


def solution(mesh):
    return jax.shard_map(
        on_device,
        mesh=mesh,
        in_specs=(
            P(None, ("gs", "img")),
            P(("gs", "img"), None),
            P("img", "gs", None),
            P(None, "img", "gs"),
        ),
        out_specs=(P(None, "img", "gs"), P("img", "gs")),
        check_vma=False,
    )
```
